32 devices in a mesh: ens: 2 (over y), lat: 4 (over z), lon: 2 (over x), lev: 2 (over core).
Axes of the slice: x: 2, y: 2, z: 4, core: 2. Of those that a mesh axis runs over, the one named last changes fastest.
Arguments:
- tracers: float32 [4, 64, 16, 256], P('lev', 'ens', 'lat', 'lon'), parts along dimension 1, may hold values from -6 to 6
- face_winds: float32 [2, 64, 16, 256], P(None, 'ens', 'lat', 'lon'), parts along dimension 1, may hold values from -0.25 to 0.25
- inverse_mass: float32 [64, 16, 256], P('ens', 'lat', 'lon'), parts along dimension 0, may hold values from 0.5 to 1
- span_owner: int32 [16, 256], P('lat', 'lon'), may hold values from 0 to 7, as said below
- span_slot: int32 [16, 256], P('lat', 'lon'), may hold values from 0 to 639, as said below
- span_column_count: int32 [40], P(('lat', 'lon')), may hold values from 1 to 128, as said below
- diffusivity: float32 [62, 5120], P('ens', ('lat', 'lon')), parts along dimension 0, may hold values from 0.2 to 2
Outputs:
- tracers_out: float32 [4, 64, 16, 256], P('lev', 'ens', 'lat', 'lon'), parts along dimension 1
- diffusivity_out: float32 [62, 5120], P('ens', ('lat', 'lon')), parts along dimension 0
The draws below stay inside these ranges and needn't reach their ends.
There are 2 independent parts, one for each index of `ens`. The reference program is written for one: setup_inputs(seed, part) draws one part's arguments, and reference() takes and returns one part's arrays. A program takes and returns all parts, laid end to end along the dimension named above; an argument that names none is the same for every part. Nothing has to cross between parts.
Inputs may be any that keep to these rules, and one draw needn't show every extreme that they name: `span_owner`: owners are numbered over lat+lon with lat slowest. Each device's block sends columns to exactly 4 distinct owners, exactly 128 columns to each, and every owner takes 4 * 128 columns in all. `span_slot`: slot s of an owner lies in its span s // 128 at position s % 128, below that span's count; no two columns share an owner and slot, and every slot below its span's count holds a column. `span_column_count`: span c belongs to owner c // 5; every owner's counts sum to 512, and every owner's last span holds exactly 128 columns.
All inputs are finite; a program needn't handle non-finite values.
Results may differ from the reference program's by a relative error of at most 0.00002.
Values sent between devices are 32-bit elements; how exact they have to be, the bound alone decides.
No kernel may reach another device: no remote copies, remote signals or barrier semaphores. Data moves between devices by JAX's collectives and lax.ppermute only.
A program may use at most 64 MiB of HBM per device.

```python
import math
import jax
import jax.numpy as jnp

VERTICAL_LEVELS = 32
NTRC = 4
LAT_DEV = 4
LON_DEV = 128
NSUB = 2
SPAN_COLUMNS = 128
SPANS_DEV = 5
GROUP = 128
NLAT = 16
NLON = 256
TOTAL_SLOTS = 5120
N_LAT = 4
N_LON = 2


def span_plan(key):
    devices = N_LAT * N_LON
    per_device = LAT_DEV * LON_DEV
    key_cols, key_dest, key_offset, key_weight, key_order, key_assign = jax.random.split(key, 6)
    column_rank = jax.vmap(lambda subkey: jax.random.permutation(subkey, per_device))(jax.random.split(key_cols, devices)).astype(jnp.int32)
    dest_perm = jax.random.permutation(key_dest, devices).astype(jnp.int32)
    offsets = jax.random.permutation(key_offset, devices).astype(jnp.int32)
    group_id = column_rank // GROUP
    owner_dev = dest_perm[(offsets[:, None] + group_id) % devices]
    weights = jax.random.randint(key_weight, (devices, SPANS_DEV - 1), 4, 6).astype(jnp.int32)
    running = jnp.cumsum(weights, axis=1)
    spare_cols = per_device - SPAN_COLUMNS
    bounds = spare_cols * running // running[:, -1:]
    bound_starts = jnp.concatenate([jnp.zeros((devices, 1), jnp.int32), bounds[:, :-1].astype(jnp.int32)], axis=1)
    rest_counts = bounds.astype(jnp.int32) - bound_starts
    shuffle = jax.vmap(lambda subkey: jax.random.permutation(subkey, SPANS_DEV - 1))(jax.random.split(key_order, devices)).astype(jnp.int32)
    mixed_counts = jnp.take_along_axis(rest_counts, shuffle, axis=1)
    counts = jnp.concatenate([mixed_counts, jnp.full((devices, 1), SPAN_COLUMNS, jnp.int32)], axis=1)
    position = jnp.arange(SPANS_DEV * SPAN_COLUMNS, dtype=jnp.int32)
    slot_used = position[None, :] % SPAN_COLUMNS < jnp.repeat(counts, SPAN_COLUMNS, axis=1)
    used_first = jnp.argsort(1 - slot_used.astype(jnp.int32), axis=1, stable=True)[:, :per_device].astype(jnp.int32)
    assign = jax.vmap(lambda subkey: jax.random.permutation(subkey, per_device))(jax.random.split(key_assign, devices)).astype(jnp.int32)
    slot_table = jnp.take_along_axis(used_first, assign, axis=1)
    slot_dev = slot_table[owner_dev, column_rank]

    def to_grid(values):
        return values.reshape(N_LAT, N_LON, LAT_DEV, LON_DEV).transpose(0, 2, 1, 3).reshape(NLAT, NLON).astype(jnp.int32)
    return (to_grid(owner_dev), to_grid(slot_dev), counts.reshape(-1).astype(jnp.int32))


def draw_span_owner(key, part):
    owner_grid, slot_grid, counts = span_plan(key)
    return owner_grid


def draw_span_slot(key, part):
    owner_grid, slot_grid, counts = span_plan(key)
    return slot_grid


def draw_span_column_count(key, part):
    owner_grid, slot_grid, counts = span_plan(key)
    return counts


def steps_of(stream_key, dims, cuts, least, top_value):
    def one(dim, parts):
        draws = jax.random.uniform(jax.random.fold_in(jax.random.fold_in(stream_key, 6), dim), (parts,), jnp.float32, least / len(cuts), top_value / len(cuts))
        return jnp.repeat(jnp.exp(draws), dims[dim] // parts).reshape((-1,) + (1,) * (len(dims) - dim - 1))

    level = one(*cuts[0])
    for cut in cuts[1:]:
        level = level * one(*cut)
    return level


def noise(rng, shape, spread, limit, cuts=(), kind=jnp.bfloat16):
    array = spread * jax.random.normal(rng, shape, jnp.float32)
    if cuts:
        array = array * steps_of(rng, shape, cuts, -0.22, 0.18)
    return jnp.clip(array, -limit, limit).astype(kind)


def setup_inputs(seed: int = 0, part: int = 0) -> dict:
    seeds = jax.random.split(jax.random.key(seed), 8)
    own_keys = jax.random.split(jax.random.fold_in(seeds[7], part), 8)
    tracers = noise(own_keys[0], (NTRC, VERTICAL_LEVELS, NLAT, NLON), 1.0, 6.0, ((0, 2), (2, 4), (3, 2)), jnp.float32)
    face_winds = jnp.clip(jax.random.uniform(own_keys[1], (2, VERTICAL_LEVELS, NLAT, NLON), jnp.float32, -0.25, 0.25) * steps_of(own_keys[1], (2, VERTICAL_LEVELS, NLAT, NLON), ((2, 4), (3, 2)), -0.4, 0.0), -0.25, 0.25)
    inverse_mass = jnp.clip(jnp.exp(math.log(1.0) - 0.6931472 * jax.random.uniform(own_keys[2], (VERTICAL_LEVELS, NLAT, NLON), jnp.float32) ** steps_of(own_keys[2], (VERTICAL_LEVELS, NLAT, NLON), ((1, 4), (2, 2)), -0.2, 0.2)), 0.5, 1.0)
    span_owner = draw_span_owner(jax.random.fold_in(seeds[7], 71), part)
    span_slot = draw_span_slot(jax.random.fold_in(seeds[7], 71), part)
    span_column_count = draw_span_column_count(jax.random.fold_in(seeds[7], 71), part)
    diffusivity = jnp.clip(jnp.exp(math.log(2.0) - 2.3025851 * jax.random.uniform(own_keys[6], (VERTICAL_LEVELS - 1, TOTAL_SLOTS), jnp.float32) ** steps_of(own_keys[6], (VERTICAL_LEVELS - 1, TOTAL_SLOTS), ((1, 8),), -0.2, 0.2)), 0.2, 2.0)
    return {"tracers": tracers, "face_winds": face_winds, "inverse_mass": inverse_mass, "span_owner": span_owner, "span_slot": span_slot, "span_column_count": span_column_count, "diffusivity": diffusivity}


def advect(tracer_field, east_wind, north_wind, inverse_mass, open_rows):
    east_flux = jnp.maximum(east_wind[..., :-1], 0.0) * tracer_field[..., :-1] + jnp.minimum(east_wind[..., :-1], 0.0) * tracer_field[..., 1:]
    north_flux = (jnp.maximum(north_wind[..., :-1, :], 0.0) * tracer_field[..., :-1, :] + jnp.minimum(north_wind[..., :-1, :], 0.0) * tracer_field[..., 1:, :]) * open_rows[:-1, None]
    zonal_div = east_flux[..., 1:-1, 1:] - east_flux[..., 1:-1, :-1]
    merid_div = north_flux[..., 1:, 1:-1] - north_flux[..., :-1, 1:-1]
    return tracer_field[..., 1:-1, 1:-1] - inverse_mass[..., 1:-1, 1:-1] * (zonal_div + merid_div)


def new_diffusivity(previous, wind_shear, active):
    return jnp.where(active, 0.5 * previous + 2.0 * wind_shear / (0.05 + wind_shear), previous)


def implicit_diffusion(tracer_field, diffus, active):
    layers = tracer_field.shape[-2]
    ratios = []
    sweeps = []
    lower_kv = jnp.zeros_like(diffus[0])
    for layer_idx in range(layers):
        upper_kv = diffus[layer_idx] if layer_idx < layers - 1 else jnp.zeros_like(diffus[0])
        pivot_sum = 1.0 + lower_kv + upper_kv
        rhs_value = tracer_field[..., layer_idx, :]
        if layer_idx > 0:
            pivot_sum = pivot_sum - lower_kv * ratios[-1]
            rhs_value = rhs_value + lower_kv * sweeps[-1]
        ratios.append(upper_kv / pivot_sum)
        sweeps.append(rhs_value / pivot_sum)
        lower_kv = upper_kv
    result = [sweeps[-1]]
    for layer_idx in range(layers - 2, -1, -1):
        result.append(sweeps[layer_idx] + ratios[layer_idx] * result[-1])
    solved = jnp.stack(result[::-1], axis=-2)
    return jnp.where(active, solved, tracer_field)


def pad_cells(values):
    values = jnp.concatenate([values[..., -1:], values, values[..., :1]], axis=-1)
    border = jnp.zeros(values.shape[:-2] + (1, values.shape[-1]), jnp.float32)
    return jnp.concatenate([border, values, border], axis=-2)


def reference(tracers, face_winds, inverse_mass, span_owner, span_slot, span_column_count, diffusivity):
    glob_rows = jnp.arange(NLAT + 2, dtype=jnp.int32) - 1
    open_rows = ((glob_rows >= 0) & (glob_rows < NLAT - 1)).astype(jnp.float32)
    east_wind = pad_cells(face_winds[0])
    north_wind = pad_cells(face_winds[1])
    mass_pad = pad_cells(inverse_mass)
    advected = tracers
    for substep in range(NSUB):
        advected = advect(pad_cells(advected), east_wind, north_wind, mass_pad, open_rows)
    east_step = face_winds[0, 1:] - face_winds[0, :-1]
    north_step = face_winds[1, 1:] - face_winds[1, :-1]
    wind_shear = (east_step * east_step + north_step * north_step).reshape(VERTICAL_LEVELS - 1, NLAT * NLON)
    global_slot = (span_owner * (SPANS_DEV * SPAN_COLUMNS) + span_slot).reshape(-1).astype(jnp.int32)
    slot_position_index = jnp.arange(TOTAL_SLOTS, dtype=jnp.int32)
    slot_is_active = (slot_position_index % SPAN_COLUMNS) < jnp.repeat(span_column_count, SPAN_COLUMNS, total_repeat_length=TOTAL_SLOTS)
    column_active = slot_is_active[global_slot]
    column_kv = new_diffusivity(diffusivity[:, global_slot], wind_shear, column_active)
    diffused = implicit_diffusion(advected.reshape(NTRC, VERTICAL_LEVELS, NLAT * NLON), column_kv, column_active)
    retained = jnp.where(slot_is_active, 0.5 * diffusivity, diffusivity)
    diffusivity_out = retained.at[:, global_slot].set(column_kv)
    return diffused.reshape(NTRC, VERTICAL_LEVELS, NLAT, NLON), diffusivity_out
```

```python
import functools

import jax
import jax.numpy as jnp
from jax import lax
from jax.experimental import pallas as pl
from jax.experimental.pallas import tpu as pltpu
from jax.sharding import PartitionSpec as P

LANES = 128
EDGE = 16
VMEM_LIMIT = 48 * 1024 * 1024
NT = (((1,), (1,)), ((), ()))


def lane_iota(shape):
    return lax.broadcasted_iota(jnp.int32, shape, len(shape) - 1)


def split3(values):
    top = values.astype(jnp.bfloat16)
    rest = values - top.astype(jnp.float32)
    mid = rest.astype(jnp.bfloat16)
    low = (rest - mid.astype(jnp.float32)).astype(jnp.bfloat16)
    return jnp.concatenate([top, mid, low], axis=0)


def pick_columns(values, hot):
    rows = values.shape[0]
    out = lax.dot_general(split3(values), hot, NT, preferred_element_type=jnp.float32)
    return out[:rows] + out[rows : 2 * rows] + out[2 * rows :]


def hot_matrix(row_of, size, base=0):
    cols = row_of.shape[-1]
    index = lax.broadcasted_iota(jnp.int32, (size, cols), 0) + base
    return jnp.where(index == row_of, 1.0, 0.0).astype(jnp.bfloat16)


def loop_over(count, body):
    if count <= 8:
        for index in range(count):
            body(index)
    else:
        pl.loop(0, count)(body)


def half_levels(first, second):
    return jnp.where(lax.axis_index("lev") == 0, first, second)


def pack_kernel(
    levels, rows, devices, tr_ref, wind_ref, mass_ref, owner_ref, slot_ref, diff_ref,
    send_ref, north_ref, south_ref, shear_ref, rank_ref,
):
    faces = levels - 1
    half = levels // 2
    spans = diff_ref.shape[1] // LANES

    def tracer_row(j):
        return tr_ref[pl.ds(j, 2 * levels, stride=rows), :]

    def east_row(j):
        return wind_ref[pl.ds(j, levels, stride=rows), :]

    def north_row(j):
        return wind_ref[pl.ds(levels * rows + j, levels, stride=rows), :]

    def mass_row(j):
        return mass_ref[pl.ds(j, levels, stride=rows), :]

    two, lev = 2 * levels, levels
    last = rows - 1
    north_ref[0:two] = tracer_row(last - 1)
    north_ref[two : 2 * two] = tracer_row(last)
    north_ref[2 * two : 2 * two + lev] = east_row(last)
    north_ref[2 * two + lev : 2 * two + 2 * lev] = north_row(last - 1)
    north_ref[2 * two + 2 * lev : 2 * two + 3 * lev] = north_row(last)
    north_ref[2 * two + 3 * lev : 2 * two + 4 * lev] = mass_row(last)
    south_ref[0:two] = tracer_row(0)
    south_ref[two : 2 * two] = tracer_row(1)
    south_ref[2 * two : 2 * two + lev] = east_row(0)
    south_ref[2 * two + lev : 2 * two + 2 * lev] = north_row(0)
    south_ref[2 * two + 2 * lev : 2 * two + 3 * lev] = mass_row(0)

    shears = []
    for j in range(rows):
        east, north = east_row(j), north_row(j)
        east_step = east[1:] - east[:-1]
        north_step = north[1:] - north[:-1]
        shear = east_step * east_step + north_step * north_step
        shears.append(half_levels(shear[:half], shear[faces - half :]))
    shear = jnp.concatenate(shears, axis=1)
    shear_ref[...] = shear

    owner_index = lax.broadcasted_iota(jnp.int32, (devices, LANES), 0)
    owned = [owner_index == owner_ref[j : j + 1, :] for j in range(rows)]
    upto = lax.broadcasted_iota(jnp.int32, (LANES, LANES), 0) <= lane_iota((LANES, LANES))
    counted = lax.dot_general(
        jnp.concatenate([jnp.where(hit, 1.0, 0.0) for hit in owned], axis=0).astype(jnp.bfloat16),
        jnp.where(upto, 1.0, 0.0).astype(jnp.bfloat16),
        (((1,), (0,)), ((), ())),
        preferred_element_type=jnp.float32,
    )
    before = jnp.full((devices, 1), -1.0, jnp.float32)
    for j in range(rows):
        count = counted[j * devices : (j + 1) * devices]
        rank_ref[:, j * LANES : (j + 1) * LANES] = jnp.where(owned[j], count + before, -1.0).astype(
            jnp.int32
        )
        before = before + count[:, LANES - 1 :]

    lane_row = lane_iota((1, LANES))
    masses = jnp.transpose(jnp.concatenate([mass_row(j) for j in range(rows)], axis=0))
    edge_rows = [[], [], [], []]
    for j in range(rows):
        turned = jnp.transpose(jnp.concatenate([tracer_row(j), east_row(j), north_row(j)], axis=0))
        west_mass = pltpu.roll(masses[0:1], (2 * levels - j * levels) % LANES, 1)
        east_mass = pltpu.roll(masses[LANES - 1 :], (3 * levels - j * levels) % LANES, 1)
        edge_rows[0].append(
            jnp.where(lane_row >= 3 * levels, east_mass, turned[LANES - 2 : LANES - 1])
        )
        edge_rows[1].append(turned[LANES - 1 :])
        edge_rows[2].append(turned[0:1])
        edge_rows[3].append(jnp.where(lane_row >= 2 * levels, west_mass, turned[1:2]))
    edges = jnp.concatenate([row for group in edge_rows for row in group], axis=0)

    diffs = half_levels(diff_ref[0:half], diff_ref[faces - half :])
    slots = jnp.concatenate([slot_ref[j : j + 1, :] for j in range(rows)], axis=1)
    extra = jnp.concatenate(
        [slots.astype(jnp.float32) + 1.0, jnp.zeros((7, rows * LANES), jnp.float32)], axis=0
    )
    payload = jnp.concatenate([shear, extra], axis=0)

    def fill(dest):
        hot = hot_matrix(rank_ref[pl.ds(dest, 1), :], LANES)
        grouped = pick_columns(payload, hot)
        slot_row = grouped[half : half + 1] - 1.0
        tail = jnp.concatenate(
            [pltpu.roll(slot_row, (3 * levels - j * levels) % LANES, 1) for j in range(rows)], axis=0
        )
        send_ref[dest, 0 : EDGE - rows] = edges[: EDGE - rows]
        send_ref[dest, EDGE - rows : EDGE] = jnp.where(
            lane_row >= 3 * levels, tail, edges[EDGE - rows :]
        )
        send_ref[dest, EDGE : EDGE + half] = grouped[:half]
        for span in range(spans):
            send_ref[dest, EDGE + half * (span + 1) : EDGE + half * (span + 2)] = diffs[
                :, span * LANES : (span + 1) * LANES
            ]

    loop_over(devices, fill)


def source_term(shear):
    return 2.0 * shear / (0.05 + shear)


def select_kernel(
    levels, rows, devices, recv_ref, owner_ref, slot_ref, diff_ref, count_ref, shear_ref,
    mine_ref, place_ref, arrived_ref,
):
    faces = levels - 1
    half = levels // 2
    slot_total = diff_ref.shape[1]
    spans = slot_total // LANES
    cols = rows * LANES
    lane_row = lane_iota((1, LANES))

    for j in range(rows):
        mine_ref[:, j * LANES : (j + 1) * LANES] = jnp.zeros((half, LANES), jnp.float32)
    span_of = []
    position = []
    for j in range(rows):
        slot = slot_ref[j : j + 1, :]
        span = slot // LANES
        span_of.append(owner_ref[j : j + 1, :] * spans + span)
        position.append(jnp.broadcast_to(slot - span * LANES, (half, LANES)))

    def gather(source):
        for j in range(rows):
            found = mine_ref[:, j * LANES : (j + 1) * LANES]
            for span in range(spans):
                held = recv_ref[source, EDGE + half * (span + 1) : EDGE + half * (span + 2), :]
                taken = jnp.take_along_axis(held, position[j], axis=1)
                found = jnp.where(span_of[j] == source * spans + span, taken, found)
            mine_ref[:, j * LANES : (j + 1) * LANES] = found

    loop_over(devices, gather)
    mine_ref[:, 0:cols] = 0.5 * mine_ref[:, 0:cols] + source_term(shear_ref[...])

    def unpack(source):
        tail = recv_ref[source, EDGE - rows : EDGE, :]
        slot_row = jnp.zeros((1, LANES), jnp.float32)
        for j in range(rows):
            back = pltpu.roll(tail[j : j + 1], (levels + j * levels) % LANES, 1)
            slot_row = jnp.where(lane_row // levels == j, back, slot_row)
        place_ref[source] = slot_row.astype(jnp.int32)

    loop_over(devices, unpack)
    if devices <= 8:
        slot_row = jnp.concatenate([place_ref[source] for source in range(devices)], axis=1)
        arrived = jnp.concatenate(
            [recv_ref[source, EDGE : EDGE + half, :] for source in range(devices)], axis=1
        )
        arrived_ref[...] = pick_columns(arrived, hot_matrix(slot_row, slot_total))
    else:
        arrived_ref[...] = jnp.zeros((half, slot_total), jnp.float32)

        def place(source):
            arrived_ref[...] += pick_columns(
                recv_ref[source, EDGE : EDGE + half, :], hot_matrix(place_ref[source], slot_total)
            )

        loop_over(devices, place)
    for span in range(spans):
        here = slice(span * LANES, (span + 1) * LANES)
        old = half_levels(diff_ref[0:half, here], diff_ref[faces - half :, here])
        new = 0.5 * old + source_term(arrived_ref[:, here])
        active = lane_row < count_ref[span]
        mine_ref[:, cols + span * LANES : cols + (span + 1) * LANES] = jnp.where(active, new, old)


def advect_kernel(
    levels, rows, lat_count, lon_count, tr_ref, wind_ref, mass_ref, low_ref, high_ref, edge_ref,
    out_ref,
):
    lev, two = levels, 2 * levels
    lat, lon = lax.axis_index("lat"), lax.axis_index("lon")
    first, final = lat == 0, lat == lat_count - 1
    lane_row = lane_iota((1, LANES))

    def block(lat_index, lon_index):
        return lat_index * lon_count + lon_index

    west_lon = lax.rem(lon + lon_count - 1, lon_count)
    east_lon = lax.rem(lon + 1, lon_count)
    south_lat = jnp.maximum(lat - 1, 0)
    north_lat = jnp.minimum(lat + 1, lat_count - 1)

    def edge(lat_index, lon_index, group):
        return edge_ref[block(lat_index, lon_index), group * rows : (group + 1) * rows, :]

    def east_of(row):
        return jnp.where(lane_row < lev, pltpu.roll(row, 2 * lev, 1), pltpu.roll(row, 3 * lev, 1))

    def north_of(row):
        return jnp.where(lane_row < lev, pltpu.roll(row, lev, 1), pltpu.roll(row, 2 * lev, 1))

    def upwind(wind, here, ahead):
        return jnp.maximum(wind, 0.0) * here + jnp.minimum(wind, 0.0) * ahead

    def beside(column, west_east, west_value, here_east, east_value, mass):
        fluxes = upwind(north_of(column[: rows + 1]), column[: rows + 1], column[1:])
        index = lax.broadcasted_iota(jnp.int32, (rows + 1, LANES), 0)
        closed = ((index == 0) & first) | ((index == rows) & final)
        fluxes = jnp.where(closed, 0.0, fluxes)
        here = column[1 : rows + 1]
        zonal = upwind(here_east, here, east_value) - upwind(west_east, west_value, here)
        return here - mass * (zonal + fluxes[1:] - fluxes[:-1])

    far_west = edge(lat, west_lon, 0)
    west = jnp.concatenate(
        [
            edge(south_lat, west_lon, 1)[rows - 1 :],
            edge(lat, west_lon, 1),
            edge(north_lat, west_lon, 1)[0:1],
        ],
        axis=0,
    )
    east = jnp.concatenate(
        [
            edge(south_lat, east_lon, 2)[rows - 1 :],
            edge(lat, east_lon, 2),
            edge(north_lat, east_lon, 2)[0:1],
        ],
        axis=0,
    )
    far_east = edge(lat, east_lon, 3)
    own_first, own_last = edge(lat, lon, 2), edge(lat, lon, 1)
    west_mid, east_mid = west[1 : rows + 1], east[1 : rows + 1]
    west_new = beside(
        west, east_of(far_west), far_west, east_of(west_mid), own_first, north_of(far_west)
    )
    east_new = beside(
        east, east_of(own_last), own_last, east_of(east_mid), far_east, east_of(far_east)
    )
    filler = jnp.zeros((LANES - 2 * (rows + 2) - 2 * rows, LANES), jnp.float32)
    turned = jnp.transpose(jnp.concatenate([west, east, west_new, east_new, filler], axis=0))

    def column(index, start, size):
        return jnp.broadcast_to(turned[start : start + size, index : index + 1], (size, LANES))

    def place(value, lane, index, start, size):
        return jnp.where(lane_row == lane, column(index, start, size), value)

    tracer = {-2: low_ref[0:two], -1: low_ref[two : 2 * two]}
    east_wind = {-1: low_ref[2 * two : 2 * two + lev]}
    north_wind = {
        -2: low_ref[2 * two + lev : 2 * two + 2 * lev],
        -1: low_ref[2 * two + 2 * lev : 2 * two + 3 * lev],
    }
    mass = {-1: low_ref[2 * two + 3 * lev : 2 * two + 4 * lev]}
    for j in range(rows):
        tracer[j] = tr_ref[pl.ds(j, two, stride=rows), :]
        east_wind[j] = wind_ref[pl.ds(j, lev, stride=rows), :]
        north_wind[j] = wind_ref[pl.ds(levels * rows + j, lev, stride=rows), :]
        mass[j] = mass_ref[pl.ds(j, lev, stride=rows), :]
    tracer[rows] = high_ref[0:two]
    tracer[rows + 1] = high_ref[two : 2 * two]
    east_wind[rows] = high_ref[2 * two : 2 * two + lev]
    north_wind[rows] = high_ref[2 * two + lev : 2 * two + 2 * lev]
    mass[rows] = high_ref[2 * two + 2 * lev : 2 * two + 3 * lev]

    west_wind = {
        j: place(pltpu.roll(east_wind[j], 1, 1), 0, j + 1, two, lev) for j in range(-1, rows + 1)
    }

    def substep(field, row_range, west_index, east_index, start):
        fluxes = {}
        for j in range(row_range[0] - 1, row_range[-1] + 1):
            flux = upwind(north_wind[j], field[j], field[j + 1])
            if j == -1:
                flux = jnp.where(first, 0.0, flux)
            if j == rows - 1:
                flux = jnp.where(final, 0.0, flux)
            fluxes[j] = flux
        result = {}
        for j in row_range:
            here = field[j]
            ahead = place(pltpu.roll(here, LANES - 1, 1), LANES - 1, east_index(j), start, lev)
            behind = place(pltpu.roll(here, 1, 1), 0, west_index(j), start, lev)
            zonal = upwind(east_wind[j], here, ahead) - upwind(west_wind[j], behind, here)
            result[j] = here - mass[j] * (zonal + fluxes[j] - fluxes[j - 1])
        return result

    for t in range(2):
        start = t * lev
        field = {j: value[start : start + lev] for j, value in tracer.items()}
        once = substep(
            field, range(-1, rows + 1), lambda j: j + 1, lambda j: rows + 2 + j + 1, start
        )
        base = 2 * (rows + 2)
        twice = substep(once, range(rows), lambda j: base + j, lambda j: base + rows + j, start)
        for j in range(rows):
            out_ref[pl.ds(t * rows + j, lev, stride=2 * rows), :] = twice[j]


def solve_kernel(levels, rows, adv_ref, mine_ref, other_ref, out_ref, diff_ref, kv_ref):
    faces = levels - 1
    half = levels // 2
    slot_total = diff_ref.shape[1]
    cols = rows * LANES
    width = 2 * rows
    low = half_levels(mine_ref[...], other_ref[...])
    high = half_levels(other_ref[...], mine_ref[...])
    diff_ref[0:half] = low[:, cols:]
    diff_ref[half:] = high[1:, cols:]
    for j in range(rows):
        here = slice(j * LANES, (j + 1) * LANES)
        for t in range(2):
            kv_ref[pl.ds(t * rows + j, half, stride=width), :] = low[:, here]
            kv_ref[pl.ds((faces - half) * width + t * rows + j, half, stride=width), :] = high[:, here]

    ratios, sweeps = [], []
    lower = None
    for level in range(levels):
        rhs = adv_ref[level * width : (level + 1) * width]
        pivot = 1.0
        upper = None
        if level < levels - 1:
            upper = kv_ref[level * width : (level + 1) * width]
            pivot = pivot + upper
        if level > 0:
            pivot = pivot + lower - lower * ratios[-1]
            rhs = rhs + lower * sweeps[-1]
        inverse = 1.0 / pivot
        if upper is not None:
            ratios.append(upper * inverse)
        sweeps.append(rhs * inverse)
        lower = upper
    value = sweeps[-1]
    for level in range(levels - 1, -1, -1):
        if level < levels - 1:
            value = sweeps[level] + ratios[level] * value
        for t in range(2):
            out_ref[(t * levels + level) * rows : (t * levels + level + 1) * rows] = value[
                t * rows : (t + 1) * rows
            ]


def call(kernel, outs, in_specs, scratch=()):
    vmem = pl.BlockSpec(memory_space=pltpu.VMEM)
    return pl.pallas_call(
        kernel,
        out_shape=[jax.ShapeDtypeStruct(shape, jnp.float32) for shape in outs],
        in_specs=in_specs,
        out_specs=[vmem] * len(outs),
        scratch_shapes=list(scratch),
        compiler_params=pltpu.CompilerParams(vmem_limit_bytes=VMEM_LIMIT),
    )


def on_device(
    tracers, face_winds, inverse_mass, span_owner, span_slot, span_column_count, diffusivity
):
    own_count, levels, rows, cols = tracers.shape
    lat_count, lon_count = lax.axis_size("lat"), lax.axis_size("lon")
    devices = lat_count * lon_count
    half = levels // 2
    slot_total = diffusivity.shape[1]
    spans = span_column_count.shape[0]
    block_rows = EDGE + half * (1 + spans)
    vmem = pl.BlockSpec(memory_space=pltpu.VMEM)
    smem = pl.BlockSpec(memory_space=pltpu.SMEM)

    tr = tracers.reshape(own_count * levels * rows, cols)
    winds = face_winds.reshape(2 * levels * rows, cols)
    mass = inverse_mass.reshape(levels * rows, cols)

    send, north, south, shear = call(
        functools.partial(pack_kernel, levels, rows, devices),
        [
            (devices, block_rows, LANES),
            (8 * levels, LANES),
            (7 * levels, LANES),
            (half, rows * LANES),
        ],
        [vmem] * 6,
        [pltpu.VMEM((devices, rows * LANES), jnp.int32)],
    )(tr, winds, mass, span_owner, span_slot, diffusivity)
    recv = lax.all_to_all(send, ("lat", "lon"), split_axis=0, concat_axis=0, tiled=True)
    up = [(i, (i + 1) % lat_count) for i in range(lat_count)]
    down = [(target, source) for source, target in up]
    low = lax.ppermute(north, "lat", up)
    high = lax.ppermute(south, "lat", down)
    (mine,) = call(
        functools.partial(select_kernel, levels, rows, devices),
        [(half, rows * LANES + slot_total)],
        [vmem, vmem, vmem, vmem, smem, vmem],
        [
            pltpu.VMEM((devices, 1, LANES), jnp.int32),
            pltpu.VMEM((half, slot_total), jnp.float32),
        ],
    )(recv, span_owner, span_slot, diffusivity, span_column_count, shear)
    other = lax.ppermute(mine, "lev", [(0, 1), (1, 0)])
    (advected,) = call(
        functools.partial(advect_kernel, levels, rows, lat_count, lon_count),
        [(levels * own_count * rows, LANES)],
        [vmem] * 6,
    )(tr, winds, mass, low, high, recv)
    out, diff_out = call(
        functools.partial(solve_kernel, levels, rows),
        [(own_count * levels * rows, cols), (levels - 1, slot_total)],
        [vmem] * 3,
        [pltpu.VMEM((levels * 2 * rows, LANES), jnp.float32)],
    )(advected, mine, other)
    return out.reshape(own_count, levels, rows, cols), diff_out


def solution(mesh):
    placed = (
        P("lev", "ens", "lat", "lon"),
        P(None, "ens", "lat", "lon"),
        P("ens", "lat", "lon"),
        P("lat", "lon"),
        P("lat", "lon"),
        P(("lat", "lon")),
        P("ens", ("lat", "lon")),
    )
    return jax.shard_map(
        on_device,
        mesh=mesh,
        in_specs=placed,
        out_specs=(P("lev", "ens", "lat", "lon"), P("ens", ("lat", "lon"))),
        check_vma=False,
    )
```

```python
import functools

import jax
import jax.numpy as jnp
from jax import lax
from jax.experimental import pallas as pl
from jax.experimental.pallas import tpu as pltpu
from jax.sharding import PartitionSpec as P

LANES = 128
MISC = 8
VMEM_LIMIT = 48 * 1024 * 1024
NT = (((1,), (1,)), ((), ()))


def lane_iota(shape):
    return lax.broadcasted_iota(jnp.int32, shape, len(shape) - 1)


def split3(values):
    top = values.astype(jnp.bfloat16)
    rest = values - top.astype(jnp.float32)
    mid = rest.astype(jnp.bfloat16)
    low = (rest - mid.astype(jnp.float32)).astype(jnp.bfloat16)
    return jnp.concatenate([top, mid, low], axis=0)


def pick_columns(values, hot):
    rows = values.shape[0]
    out = lax.dot_general(split3(values), hot, NT, preferred_element_type=jnp.float32)
    return out[:rows] + out[rows : 2 * rows] + out[2 * rows :]


def hot_matrix(row_of, size, base=0):
    cols = row_of.shape[-1]
    index = lax.broadcasted_iota(jnp.int32, (size, cols), 0) + base
    return jnp.where(index == row_of, 1.0, 0.0).astype(jnp.bfloat16)


def loop_over(count, body):
    if count <= 8:
        for index in range(count):
            body(index)
    else:
        pl.loop(0, count)(body)


def half_levels(first, second):
    return jnp.where(lax.axis_index("lev") == 0, first, second)


def pack_kernel(
    levels, rows, devices, tr_hbm, wind_hbm, mass_hbm, owner_hbm, slot_hbm, diff_hbm, count_hbm,
    send_ref, north_ref, south_ref, shear_ref, edge_ref,
    tr_ref, wind_ref, mass_ref, owner_ref, slot_ref, diff_ref, count_ref, rank_ref, sems,
):
    faces = levels - 1
    half = levels // 2
    spans = diff_ref.shape[1] // LANES
    pairs = [
        (owner_hbm, owner_ref), (slot_hbm, slot_ref), (wind_hbm, wind_ref), (count_hbm, count_ref),
        (diff_hbm, diff_ref), (mass_hbm, mass_ref), (tr_hbm, tr_ref),
    ]
    copies = [
        pltpu.make_async_copy(source, target, sems.at[index])
        for index, (source, target) in enumerate(pairs)
    ]
    for copy in copies:
        copy.start()

    def tracer_row(j):
        return tr_ref[pl.ds(j, 2 * levels, stride=rows), :]

    def east_row(j):
        return wind_ref[pl.ds(j, levels, stride=rows), :]

    def north_row(j):
        return wind_ref[pl.ds(levels * rows + j, levels, stride=rows), :]

    def mass_row(j):
        return mass_ref[pl.ds(j, levels, stride=rows), :]

    copies[0].wait()
    owner_index = lax.broadcasted_iota(jnp.int32, (devices, LANES), 0)
    owned = [owner_index == owner_ref[j : j + 1, :] for j in range(rows)]
    upto = lax.broadcasted_iota(jnp.int32, (LANES, LANES), 0) <= lane_iota((LANES, LANES))
    counted = lax.dot_general(
        jnp.concatenate([jnp.where(hit, 1.0, 0.0) for hit in owned], axis=0).astype(jnp.bfloat16),
        jnp.where(upto, 1.0, 0.0).astype(jnp.bfloat16),
        (((1,), (0,)), ((), ())),
        preferred_element_type=jnp.float32,
    )
    before = jnp.full((devices, 1), -1.0, jnp.float32)
    for j in range(rows):
        count = counted[j * devices : (j + 1) * devices]
        rank_ref[:, j * LANES : (j + 1) * LANES] = jnp.where(owned[j], count + before, -1.0).astype(
            jnp.int32
        )
        before = before + count[:, LANES - 1 :]

    copies[1].wait()
    copies[2].wait()
    shears = []
    for j in range(rows):
        east, north = east_row(j), north_row(j)
        east_step = east[1:] - east[:-1]
        north_step = north[1:] - north[:-1]
        shear = east_step * east_step + north_step * north_step
        shears.append(half_levels(shear[:half], shear[faces - half :]))
    shear = jnp.concatenate(shears, axis=1)
    shear_ref[...] = shear

    copies[3].wait()
    copies[4].wait()
    diffs = half_levels(diff_ref[0:half], diff_ref[faces - half :])
    lane_half = lane_iota((half, LANES))
    lane_row = lane_iota((1, LANES))
    starts, start = [], 0
    for span in range(spans):
        starts.append(start)
        start = start + count_ref[span]
    packed = []
    for group in range(rows - 1):
        value = jnp.zeros((half, LANES), jnp.float32)
        for span in range(spans - 1):
            spot = lane_half + (group * LANES - starts[span])
            taken = jnp.take_along_axis(
                diffs[:, span * LANES : (span + 1) * LANES], spot & (LANES - 1), axis=1
            )
            value = jnp.where((spot >= 0) & (spot < count_ref[span]), taken, value)
        packed.append(value)
    packed.append(diffs[:, (spans - 1) * LANES :])
    start_row = jnp.zeros((1, LANES), jnp.float32)
    for span in range(spans):
        start_row = jnp.where(
            lane_row == span, lax.convert_element_type(starts[span], jnp.float32), start_row
        )

    copies[5].wait()
    copies[6].wait()
    two, lev = 2 * levels, levels
    last = rows - 1
    north_ref[0:two] = tracer_row(last - 1)
    north_ref[two : 2 * two] = tracer_row(last)
    north_ref[2 * two : 2 * two + lev] = east_row(last)
    north_ref[2 * two + lev : 2 * two + 2 * lev] = north_row(last - 1)
    north_ref[2 * two + 2 * lev : 2 * two + 3 * lev] = north_row(last)
    north_ref[2 * two + 3 * lev : 2 * two + 4 * lev] = mass_row(last)
    south_ref[0:two] = tracer_row(0)
    south_ref[two : 2 * two] = tracer_row(1)
    south_ref[2 * two : 2 * two + lev] = east_row(0)
    south_ref[2 * two + lev : 2 * two + 2 * lev] = north_row(0)
    south_ref[2 * two + 2 * lev : 2 * two + 3 * lev] = mass_row(0)

    masses = jnp.transpose(jnp.concatenate([mass_row(j) for j in range(rows)], axis=0))
    edge_rows = [[], [], [], []]
    for j in range(rows):
        turned = jnp.transpose(jnp.concatenate([tracer_row(j), east_row(j), north_row(j)], axis=0))
        west_mass = pltpu.roll(masses[0:1], (2 * levels - j * levels) % LANES, 1)
        east_mass = pltpu.roll(masses[LANES - 1 :], (3 * levels - j * levels) % LANES, 1)
        edge_rows[0].append(
            jnp.where(lane_row >= 3 * levels, east_mass, turned[LANES - 2 : LANES - 1])
        )
        edge_rows[1].append(turned[LANES - 1 :])
        edge_rows[2].append(turned[0:1])
        edge_rows[3].append(jnp.where(lane_row >= 2 * levels, west_mass, turned[1:2]))
    edge_ref[...] = jnp.concatenate([row for group in edge_rows for row in group], axis=0)

    slots = jnp.concatenate([slot_ref[j : j + 1, :] for j in range(rows)], axis=1)
    extra = jnp.concatenate(
        [slots.astype(jnp.float32) + 1.0, jnp.zeros((7, rows * LANES), jnp.float32)], axis=0
    )
    payload = jnp.concatenate([shear, extra], axis=0)
    misc = jnp.concatenate(
        [
            jnp.zeros((1, LANES), jnp.float32),
            start_row,
            edge_rows[1][last],
            edge_rows[2][last],
            edge_rows[1][0],
            edge_rows[2][0],
            jnp.zeros((2, LANES), jnp.float32),
        ],
        axis=0,
    )

    def fill(dest):
        hot = hot_matrix(rank_ref[pl.ds(dest, 1), :], LANES)
        grouped = pick_columns(payload, hot)
        send_ref[dest, 0:MISC] = misc
        send_ref[dest, 0:1] = grouped[half : half + 1] - 1.0
        send_ref[dest, MISC : MISC + half] = grouped[:half]
        for group in range(rows):
            send_ref[dest, MISC + half * (group + 1) : MISC + half * (group + 2)] = packed[group]

    loop_over(devices, fill)


def source_term(shear):
    return 2.0 * shear / (0.05 + shear)


def select_kernel(
    levels, rows, devices, recv_ref, owner_ref, slot_ref, diff_ref, count_ref, shear_ref,
    after_ref, mine_ref, start_ref, arrived_ref,
):
    faces = levels - 1
    half = levels // 2
    slot_total = diff_ref.shape[1]
    spans = slot_total // LANES
    cols = rows * LANES
    lane_row = lane_iota((1, LANES))

    owner = owner_ref[...]
    slot = slot_ref[...]
    span = slot // LANES
    start_ref[...] = jnp.zeros((rows, LANES), jnp.float32)

    def look_up(source):
        table = jnp.broadcast_to(recv_ref[source, 1:2, :], (rows, LANES))
        start_ref[...] = jnp.where(
            owner == source, jnp.take_along_axis(table, span, axis=1), start_ref[...]
        )

    loop_over(devices, look_up)
    place = start_ref[...].astype(jnp.int32) + (slot - span * LANES)
    group_of = owner * rows + place // LANES
    position = place & (LANES - 1)

    mine_ref[:, 0:cols] = jnp.zeros((half, cols), jnp.float32)

    def gather(source):
        for j in range(rows):
            spot = jnp.broadcast_to(position[j : j + 1], (half, LANES))
            found = mine_ref[:, j * LANES : (j + 1) * LANES]
            for group in range(rows):
                held = recv_ref[source, MISC + half * (group + 1) : MISC + half * (group + 2), :]
                taken = jnp.take_along_axis(held, spot, axis=1)
                found = jnp.where(group_of[j : j + 1] == source * rows + group, taken, found)
            mine_ref[:, j * LANES : (j + 1) * LANES] = found

    loop_over(devices, gather)
    mine_ref[:, 0:cols] = 0.5 * mine_ref[:, 0:cols] + source_term(shear_ref[...])

    def slots_of(source):
        return recv_ref[source, 0:1, :].astype(jnp.int32)

    if devices <= 8:
        slot_row = jnp.concatenate([slots_of(source) for source in range(devices)], axis=1)
        arrived = jnp.concatenate(
            [recv_ref[source, MISC : MISC + half, :] for source in range(devices)], axis=1
        )
        arrived_ref[...] = pick_columns(arrived, hot_matrix(slot_row, slot_total))
    else:
        arrived_ref[...] = jnp.zeros((half, slot_total), jnp.float32)

        def add(source):
            arrived_ref[...] += pick_columns(
                recv_ref[source, MISC : MISC + half, :], hot_matrix(slots_of(source), slot_total)
            )

        loop_over(devices, add)
    for index in range(spans):
        here = slice(index * LANES, (index + 1) * LANES)
        old = half_levels(diff_ref[0:half, here], diff_ref[faces - half :, here])
        new = 0.5 * old + source_term(arrived_ref[:, here])
        active = lane_row < count_ref[index]
        mine_ref[:, cols + index * LANES : cols + (index + 1) * LANES] = jnp.where(active, new, old)


def advect_kernel(
    levels, rows, lat_count, lon_count, tr_ref, wind_ref, mass_ref, low_ref, high_ref, recv_ref,
    own_ref, west_ref, east_ref, out_ref,
):
    lev, two = levels, 2 * levels
    lat, lon = lax.axis_index("lat"), lax.axis_index("lon")
    first, final = lat == 0, lat == lat_count - 1
    lane_row = lane_iota((1, LANES))

    def block(lat_index, lon_index):
        return lat_index * lon_count + lon_index

    west_lon = lax.rem(lon + lon_count - 1, lon_count)
    east_lon = lax.rem(lon + 1, lon_count)
    south_lat = jnp.maximum(lat - 1, 0)
    north_lat = jnp.minimum(lat + 1, lat_count - 1)

    def edge(ref, group):
        return ref[group * rows : (group + 1) * rows, :]

    def corner(lat_index, lon_index, row):
        return recv_ref[block(lat_index, lon_index), row : row + 1, :]

    def east_of(row):
        return jnp.where(lane_row < lev, pltpu.roll(row, 2 * lev, 1), pltpu.roll(row, 3 * lev, 1))

    def north_of(row):
        return jnp.where(lane_row < lev, pltpu.roll(row, lev, 1), pltpu.roll(row, 2 * lev, 1))

    def upwind(wind, here, ahead):
        return jnp.maximum(wind, 0.0) * here + jnp.minimum(wind, 0.0) * ahead

    def beside(column, west_east, west_value, here_east, east_value, mass):
        fluxes = upwind(north_of(column[: rows + 1]), column[: rows + 1], column[1:])
        index = lax.broadcasted_iota(jnp.int32, (rows + 1, LANES), 0)
        closed = ((index == 0) & first) | ((index == rows) & final)
        fluxes = jnp.where(closed, 0.0, fluxes)
        here = column[1 : rows + 1]
        zonal = upwind(here_east, here, east_value) - upwind(west_east, west_value, here)
        return here - mass * (zonal + fluxes[1:] - fluxes[:-1])

    far_west, far_east = edge(west_ref, 0), edge(east_ref, 3)
    own_first, own_last = edge(own_ref, 2), edge(own_ref, 1)
    west = jnp.concatenate(
        [corner(south_lat, west_lon, 2), edge(west_ref, 1), corner(north_lat, west_lon, 4)], axis=0
    )
    east = jnp.concatenate(
        [corner(south_lat, east_lon, 3), edge(east_ref, 2), corner(north_lat, east_lon, 5)], axis=0
    )
    west_mid, east_mid = west[1 : rows + 1], east[1 : rows + 1]
    west_new = beside(
        west, east_of(far_west), far_west, east_of(west_mid), own_first, north_of(far_west)
    )
    east_new = beside(
        east, east_of(own_last), own_last, east_of(east_mid), far_east, east_of(far_east)
    )
    filler = jnp.zeros((LANES - 2 * (rows + 2) - 2 * rows, LANES), jnp.float32)
    turned = jnp.transpose(jnp.concatenate([west, east, west_new, east_new, filler], axis=0))

    def column(index, start, size):
        return jnp.broadcast_to(turned[start : start + size, index : index + 1], (size, LANES))

    def place(value, lane, index, start, size):
        return jnp.where(lane_row == lane, column(index, start, size), value)

    tracer = {-2: low_ref[0:two], -1: low_ref[two : 2 * two]}
    east_wind = {-1: low_ref[2 * two : 2 * two + lev]}
    north_wind = {
        -2: low_ref[2 * two + lev : 2 * two + 2 * lev],
        -1: low_ref[2 * two + 2 * lev : 2 * two + 3 * lev],
    }
    mass = {-1: low_ref[2 * two + 3 * lev : 2 * two + 4 * lev]}
    for j in range(rows):
        tracer[j] = tr_ref[pl.ds(j, two, stride=rows), :]
        east_wind[j] = wind_ref[pl.ds(j, lev, stride=rows), :]
        north_wind[j] = wind_ref[pl.ds(levels * rows + j, lev, stride=rows), :]
        mass[j] = mass_ref[pl.ds(j, lev, stride=rows), :]
    tracer[rows] = high_ref[0:two]
    tracer[rows + 1] = high_ref[two : 2 * two]
    east_wind[rows] = high_ref[2 * two : 2 * two + lev]
    north_wind[rows] = high_ref[2 * two + lev : 2 * two + 2 * lev]
    mass[rows] = high_ref[2 * two + 2 * lev : 2 * two + 3 * lev]

    west_wind = {
        j: place(pltpu.roll(east_wind[j], 1, 1), 0, j + 1, two, lev) for j in range(-1, rows + 1)
    }

    def substep(field, row_range, west_index, east_index, start):
        fluxes = {}
        for j in range(row_range[0] - 1, row_range[-1] + 1):
            flux = upwind(north_wind[j], field[j], field[j + 1])
            if j == -1:
                flux = jnp.where(first, 0.0, flux)
            if j == rows - 1:
                flux = jnp.where(final, 0.0, flux)
            fluxes[j] = flux
        result = {}
        for j in row_range:
            here = field[j]
            ahead = place(pltpu.roll(here, LANES - 1, 1), LANES - 1, east_index(j), start, lev)
            behind = place(pltpu.roll(here, 1, 1), 0, west_index(j), start, lev)
            zonal = upwind(east_wind[j], here, ahead) - upwind(west_wind[j], behind, here)
            result[j] = here - mass[j] * (zonal + fluxes[j] - fluxes[j - 1])
        return result

    for t in range(2):
        start = t * lev
        field = {j: value[start : start + lev] for j, value in tracer.items()}
        once = substep(
            field, range(-1, rows + 1), lambda j: j + 1, lambda j: rows + 2 + j + 1, start
        )
        base = 2 * (rows + 2)
        twice = substep(once, range(rows), lambda j: base + j, lambda j: base + rows + j, start)
        for j in range(rows):
            out_ref[pl.ds(t * rows + j, lev, stride=2 * rows), :] = twice[j]


def solve_kernel(levels, rows, adv_ref, mine_ref, other_ref, out_ref, diff_ref, kv_ref):
    faces = levels - 1
    half = levels // 2
    slot_total = diff_ref.shape[1]
    cols = rows * LANES
    width = 2 * rows
    low = half_levels(mine_ref[...], other_ref[...])
    high = half_levels(other_ref[...], mine_ref[...])
    diff_ref[0:half] = low[:, cols:]
    diff_ref[half:] = high[1:, cols:]
    for j in range(rows):
        here = slice(j * LANES, (j + 1) * LANES)
        for t in range(2):
            kv_ref[pl.ds(t * rows + j, half, stride=width), :] = low[:, here]
            kv_ref[pl.ds((faces - half) * width + t * rows + j, half, stride=width), :] = high[:, here]

    ratios, sweeps = [], []
    lower = None
    for level in range(levels):
        rhs = adv_ref[level * width : (level + 1) * width]
        pivot = 1.0
        upper = None
        if level < levels - 1:
            upper = kv_ref[level * width : (level + 1) * width]
            pivot = pivot + upper
        if level > 0:
            pivot = pivot + lower - lower * ratios[-1]
            rhs = rhs + lower * sweeps[-1]
        inverse = 1.0 / pivot
        if upper is not None:
            ratios.append(upper * inverse)
        sweeps.append(rhs * inverse)
        lower = upper
    value = sweeps[-1]
    for level in range(levels - 1, -1, -1):
        if level < levels - 1:
            value = sweeps[level] + ratios[level] * value
        for t in range(2):
            out_ref[(t * levels + level) * rows : (t * levels + level + 1) * rows] = value[
                t * rows : (t + 1) * rows
            ]


def call(kernel, outs, in_specs, scratch=()):
    vmem = pl.BlockSpec(memory_space=pltpu.VMEM)
    return pl.pallas_call(
        kernel,
        out_shape=[jax.ShapeDtypeStruct(shape, jnp.float32) for shape in outs],
        in_specs=in_specs,
        out_specs=[vmem] * len(outs),
        scratch_shapes=list(scratch),
        compiler_params=pltpu.CompilerParams(vmem_limit_bytes=VMEM_LIMIT),
    )


def on_device(
    tracers, face_winds, inverse_mass, span_owner, span_slot, span_column_count, diffusivity
):
    own_count, levels, rows, cols = tracers.shape
    lat_count, lon_count = lax.axis_size("lat"), lax.axis_size("lon")
    devices = lat_count * lon_count
    half = levels // 2
    slot_total = diffusivity.shape[1]
    block_rows = MISC + half * (1 + rows)
    vmem = pl.BlockSpec(memory_space=pltpu.VMEM)
    smem = pl.BlockSpec(memory_space=pltpu.SMEM)
    hbm = pl.BlockSpec(memory_space=pltpu.HBM)

    tr = tracers.reshape(own_count * levels * rows, cols)
    winds = face_winds.reshape(2 * levels * rows, cols)
    mass = inverse_mass.reshape(levels * rows, cols)

    send, north, south, shear, edges = call(
        functools.partial(pack_kernel, levels, rows, devices),
        [
            (devices, block_rows, LANES),
            (8 * levels, LANES),
            (7 * levels, LANES),
            (half, rows * LANES),
            (4 * rows, LANES),
        ],
        [hbm] * 7,
        [
            pltpu.VMEM(tr.shape, jnp.float32),
            pltpu.VMEM(winds.shape, jnp.float32),
            pltpu.VMEM(mass.shape, jnp.float32),
            pltpu.VMEM(span_owner.shape, jnp.int32),
            pltpu.VMEM(span_slot.shape, jnp.int32),
            pltpu.VMEM(diffusivity.shape, jnp.float32),
            pltpu.SMEM(span_column_count.shape, jnp.int32),
            pltpu.VMEM((devices, rows * LANES), jnp.int32),
            pltpu.SemaphoreType.DMA((7,)),
        ],
    )(
        *(
            pltpu.with_memory_space_constraint(value, pltpu.HBM)
            for value in (tr, winds, mass, span_owner, span_slot, diffusivity, span_column_count)
        )
    )
    recv = lax.all_to_all(send, ("lat", "lon"), split_axis=0, concat_axis=0, tiled=True)
    up = [(i, i + 1) for i in range(lat_count - 1)]
    down = [(target, source) for source, target in up]
    low = lax.ppermute(north, "lat", up)
    high = lax.ppermute(south, "lat", down)
    to_east = [(i, (i + 1) % lon_count) for i in range(lon_count)]
    to_west = [(target, source) for source, target in to_east]
    west_edges = lax.ppermute(edges, "lon", to_east)
    east_edges = west_edges if lon_count == 2 else lax.ppermute(edges, "lon", to_west)
    (mine,) = call(
        functools.partial(select_kernel, levels, rows, devices),
        [(half, rows * LANES + slot_total)],
        [vmem, vmem, vmem, vmem, smem, vmem, pl.BlockSpec(memory_space=pl.ANY)],
        [
            pltpu.VMEM((rows, LANES), jnp.float32),
            pltpu.VMEM((half, slot_total), jnp.float32),
        ],
    )(recv, span_owner, span_slot, diffusivity, span_column_count, shear, west_edges)
    other = lax.ppermute(mine, "lev", [(0, 1), (1, 0)])
    (advected,) = call(
        functools.partial(advect_kernel, levels, rows, lat_count, lon_count),
        [(levels * own_count * rows, LANES)],
        [vmem] * 9,
    )(tr, winds, mass, low, high, recv, edges, west_edges, east_edges)
    out, diff_out = call(
        functools.partial(solve_kernel, levels, rows),
        [(own_count * levels * rows, cols), (levels - 1, slot_total)],
        [vmem] * 3,
        [pltpu.VMEM((levels * 2 * rows, LANES), jnp.float32)],
    )(advected, mine, other)
    return out.reshape(own_count, levels, rows, cols), diff_out


def solution(mesh):
    placed = (
        P("lev", "ens", "lat", "lon"),
        P(None, "ens", "lat", "lon"),
        P("ens", "lat", "lon"),
        P("lat", "lon"),
        P("lat", "lon"),
        P(("lat", "lon")),
        P("ens", ("lat", "lon")),
    )
    return jax.shard_map(
        on_device,
        mesh=mesh,
        in_specs=placed,
        out_specs=(P("lev", "ens", "lat", "lon"), P("ens", ("lat", "lon"))),
        check_vma=False,
    )
```

```python
import functools

import jax
import jax.numpy as jnp
from jax import lax
from jax.experimental import pallas as pl
from jax.experimental.pallas import tpu as pltpu
from jax.sharding import PartitionSpec as P

LANES = 128
MISC = 8
VMEM_LIMIT = 48 * 1024 * 1024
NT = (((1,), (1,)), ((), ()))


def lane_iota(shape):
    return lax.broadcasted_iota(jnp.int32, shape, len(shape) - 1)


def split3(values):
    top = values.astype(jnp.bfloat16)
    rest = values - top.astype(jnp.float32)
    mid = rest.astype(jnp.bfloat16)
    low = (rest - mid.astype(jnp.float32)).astype(jnp.bfloat16)
    return jnp.concatenate([top, mid, low], axis=0)


def hot_matrix(row_of, size):
    index = lax.broadcasted_iota(jnp.int32, (size, row_of.shape[-1]), 0)
    return jnp.where(index == row_of, 1.0, 0.0).astype(jnp.bfloat16)


def pick_columns(masked, hot, rows):
    out = lax.dot_general(masked, hot, NT, preferred_element_type=jnp.float32)
    return [
        out[at : at + rows] + out[at + rows : at + 2 * rows] + out[at + 2 * rows : at + 3 * rows]
        for at in range(0, masked.shape[0], 3 * rows)
    ]


def only_where(split, key, wanted):
    return split * jnp.where(key == wanted, 1.0, 0.0).astype(jnp.bfloat16)


def loop_over(count, body):
    if count <= 8:
        for index in range(count):
            body(index)
    else:
        pl.loop(0, count)(body)


def half_levels(first, second):
    return jnp.where(lax.axis_index("lev") == 0, first, second)


def pack_kernel(
    levels, rows, devices, tr_hbm, wind_hbm, mass_hbm, owner_hbm, slot_hbm, diff_hbm, count_hbm,
    send_hbm, even_ref, odd_ref, shear_ref, edge_ref, active_ref,
    tr_ref, wind_ref, mass_ref, owner_ref, slot_ref, diff_ref, count_ref, send_ref, sems,
):
    faces = levels - 1
    half = levels // 2
    spans = diff_ref.shape[1] // LANES
    last = rows - 1
    head = MISC + half
    pairs = [
        (owner_hbm, owner_ref), (slot_hbm, slot_ref), (count_hbm, count_ref), (diff_hbm, diff_ref),
        (wind_hbm, wind_ref), (tr_hbm, tr_ref), (mass_hbm, mass_ref),
    ]
    copies = [
        pltpu.make_async_copy(source, target, sems.at[index])
        for index, (source, target) in enumerate(pairs)
    ]
    for copy in copies:
        copy.start()

    def tracer_row(j):
        return tr_ref[pl.ds(j, 2 * levels, stride=rows), :]

    def east_row(j):
        return wind_ref[pl.ds(j, levels, stride=rows), :]

    def north_row(j):
        return wind_ref[pl.ds(levels * rows + j, levels, stride=rows), :]

    def mass_row(j):
        return mass_ref[pl.ds(j, levels, stride=rows), :]

    copies[0].wait()
    owner_index = lax.broadcasted_iota(jnp.int32, (devices, LANES), 0)
    owned = [owner_index == owner_ref[j : j + 1, :] for j in range(rows)]
    upto = lax.broadcasted_iota(jnp.int32, (LANES, LANES), 0) <= lane_iota((LANES, LANES))
    counted = lax.dot_general(
        jnp.concatenate([jnp.where(hit, 1.0, 0.0) for hit in owned], axis=0).astype(jnp.bfloat16),
        jnp.where(upto, 1.0, 0.0).astype(jnp.bfloat16),
        (((1,), (0,)), ((), ())),
        preferred_element_type=jnp.float32,
    )
    before = jnp.full((devices, 1), -1.0, jnp.float32)
    ranks = []
    for j in range(rows):
        count = counted[j * devices : (j + 1) * devices]
        ranks.append(jnp.sum(jnp.where(owned[j], count + before, 0.0), axis=0, keepdims=True))
        before = before + count[:, LANES - 1 :]
    rank = jnp.concatenate(ranks, axis=1).astype(jnp.int32)
    owner = jnp.concatenate([owner_ref[j : j + 1, :] for j in range(rows)], axis=1)
    copies[1].wait()
    slots = jnp.concatenate([slot_ref[j : j + 1, :] for j in range(rows)], axis=1)

    copies[2].wait()
    copies[3].wait()
    diffs = half_levels(diff_ref[0:half], diff_ref[faces - half :])
    lane_half = lane_iota((half, LANES))
    lane_row = lane_iota((1, LANES))
    starts, start = [], 0
    for span in range(spans):
        starts.append(start)
        start = start + count_ref[span]
    for group in range(rows):
        if group < last:
            value = jnp.zeros((half, LANES), jnp.float32)
            for span in range(spans - 1):
                spot = lane_half + (group * LANES - starts[span])
                taken = jnp.take_along_axis(
                    diffs[:, span * LANES : (span + 1) * LANES], spot & (LANES - 1), axis=1
                )
                value = jnp.where((spot >= 0) & (spot < count_ref[span]), taken, value)
        else:
            value = diffs[:, (spans - 1) * LANES :]

        def store(dest):
            send_ref[dest, head + half * group : head + half * (group + 1)] = value

        loop_over(devices, store)
    put_diffs = pltpu.make_async_copy(
        send_ref.at[:, pl.ds(head, half * rows)],
        send_hbm.at[:, pl.ds(head, half * rows)],
        sems.at[len(pairs)],
    )
    put_diffs.start()
    start_row = jnp.zeros((1, LANES), jnp.float32)
    for span in range(spans):
        here = lax.convert_element_type(starts[span], jnp.float32)
        start_row = jnp.where(lane_row == span, here, start_row)
        active_ref[:, span * LANES : (span + 1) * LANES] = jnp.where(
            lane_row < count_ref[span], 1.0, 0.0
        )

    copies[4].wait()
    shears = []
    for j in range(rows):
        east, north = east_row(j), north_row(j)
        east_step = east[1:] - east[:-1]
        north_step = north[1:] - north[:-1]
        shear = east_step * east_step + north_step * north_step
        shears.append(half_levels(shear[:half], shear[faces - half :]))
    shear = jnp.concatenate(shears, axis=1)
    shear_ref[...] = shear

    copies[5].wait()
    turned = [
        jnp.transpose(jnp.concatenate([tracer_row(j), east_row(j), north_row(j)], axis=0))
        for j in range(rows)
    ]
    misc = jnp.concatenate(
        [
            start_row,
            turned[last][LANES - 1 :],
            turned[last][0:1],
            turned[0][LANES - 1 :],
            turned[0][0:1],
            jnp.zeros((2, LANES), jnp.float32),
        ],
        axis=0,
    )

    extra = jnp.concatenate(
        [slots.astype(jnp.float32) + 1.0, jnp.zeros((7, rows * LANES), jnp.float32)], axis=0
    )
    split = split3(jnp.concatenate([shear, extra], axis=0))
    hot = hot_matrix(rank, LANES)

    def fill(dest, grouped):
        send_ref[dest, 0:1] = grouped[half : half + 1] - 1.0
        send_ref[dest, 1:MISC] = misc
        send_ref[dest, MISC:head] = grouped[:half]

    if devices <= 8:
        masked = [only_where(split, owner, dest) for dest in range(devices)]
        for dest, grouped in enumerate(
            pick_columns(jnp.concatenate(masked, axis=0), hot, half + 8)
        ):
            fill(dest, grouped)
    else:
        pl.loop(0, devices)(
            lambda dest: fill(dest, pick_columns(only_where(split, owner, dest), hot, half + 8)[0])
        )
    put_head = pltpu.make_async_copy(
        send_ref.at[:, pl.ds(0, head)], send_hbm.at[:, pl.ds(0, head)], sems.at[len(pairs) + 1]
    )
    put_head.start()

    copies[6].wait()
    masses = jnp.transpose(jnp.concatenate([mass_row(j) for j in range(rows)], axis=0))
    edge_rows = [[], [], [], []]
    for j in range(rows):
        west_mass = pltpu.roll(masses[0:1], (2 * levels - j * levels) % LANES, 1)
        east_mass = pltpu.roll(masses[LANES - 1 :], (3 * levels - j * levels) % LANES, 1)
        edge_rows[0].append(
            jnp.where(lane_row >= 3 * levels, east_mass, turned[j][LANES - 2 : LANES - 1])
        )
        edge_rows[1].append(turned[j][LANES - 1 :])
        edge_rows[2].append(turned[j][0:1])
        edge_rows[3].append(jnp.where(lane_row >= 2 * levels, west_mass, turned[j][1:2]))
    edge_ref[...] = jnp.concatenate([row for group in edge_rows for row in group], axis=0)

    def put_rows(ref, far, near):
        two, lev = 2 * levels, levels
        ref[0:two] = tracer_row(far)
        ref[two : 2 * two] = tracer_row(near)
        ref[2 * two : 2 * two + lev] = east_row(near)
        ref[2 * two + lev : 2 * two + 2 * lev] = north_row(far)
        ref[2 * two + 2 * lev : 2 * two + 3 * lev] = north_row(near)
        ref[2 * two + 3 * lev : 2 * two + 4 * lev] = mass_row(near)

    even = lax.rem(lax.axis_index("lat"), 2) == 0

    @pl.when(even)
    def _():
        put_rows(even_ref, last - 1, last)
        put_rows(odd_ref, 1, 0)

    @pl.when(jnp.logical_not(even))
    def _():
        put_rows(even_ref, 1, 0)
        put_rows(odd_ref, last - 1, last)

    put_diffs.wait()
    put_head.wait()


def source_term(shear):
    return 2.0 * shear / (0.05 + shear)


def select_kernel(
    levels, rows, devices, recv_ref, owner_ref, slot_ref, diff_ref, active_ref, shear_ref,
    after_ref, mine_ref, start_ref, arrived_ref,
):
    faces = levels - 1
    half = levels // 2
    slot_total = diff_ref.shape[1]
    spans = slot_total // LANES
    cols = rows * LANES

    owner = owner_ref[...]
    slot = slot_ref[...]
    span = slot // LANES
    start_ref[...] = jnp.zeros((rows, LANES), jnp.float32)

    def look_up(source):
        table = jnp.broadcast_to(recv_ref[source, 1:2, :], (rows, LANES))
        start_ref[...] = jnp.where(
            owner == source, jnp.take_along_axis(table, span, axis=1), start_ref[...]
        )

    loop_over(devices, look_up)
    place = start_ref[...].astype(jnp.int32) + (slot - span * LANES)
    group_of = owner * rows + place // LANES
    position = place & (LANES - 1)

    mine_ref[:, 0:cols] = jnp.zeros((half, cols), jnp.float32)

    def gather(source):
        for j in range(rows):
            spot = jnp.broadcast_to(position[j : j + 1], (half, LANES))
            found = mine_ref[:, j * LANES : (j + 1) * LANES]
            for group in range(rows):
                held = recv_ref[source, MISC + half * (group + 1) : MISC + half * (group + 2), :]
                taken = jnp.take_along_axis(held, spot, axis=1)
                found = jnp.where(group_of[j : j + 1] == source * rows + group, taken, found)
            mine_ref[:, j * LANES : (j + 1) * LANES] = found

    loop_over(devices, gather)
    mine_ref[:, 0:cols] = 0.5 * mine_ref[:, 0:cols] + source_term(shear_ref[...])

    def place(slot_row, values):
        split = split3(values)
        masked = [only_where(split, slot_row >> 7, index) for index in range(spans)]
        hot = hot_matrix(slot_row & (LANES - 1), LANES)
        return jnp.concatenate(
            pick_columns(jnp.concatenate(masked, axis=0), hot, half), axis=1
        )

    def slots_of(source):
        return recv_ref[source, 0:1, :].astype(jnp.int32)

    def shears_of(source):
        return recv_ref[source, MISC : MISC + half, :]

    if devices <= 8:
        arrived_ref[...] = place(
            jnp.concatenate([slots_of(source) for source in range(devices)], axis=1),
            jnp.concatenate([shears_of(source) for source in range(devices)], axis=1),
        )
    else:
        arrived_ref[...] = jnp.zeros((half, slot_total), jnp.float32)

        @pl.loop(0, devices)
        def _(source):
            arrived_ref[...] += place(slots_of(source), shears_of(source))

    old = half_levels(diff_ref[0:half], diff_ref[faces - half :])
    new = 0.5 * old + source_term(arrived_ref[...])
    mine_ref[:, cols:] = jnp.where(active_ref[...] > 0.0, new, old)


def advect_kernel(
    levels, rows, lat_count, lon_count, tr_ref, wind_ref, mass_ref, even_ref, odd_ref, recv_ref,
    own_ref, west_ref, east_ref, out_ref,
):
    lev, two = levels, 2 * levels
    lat, lon = lax.axis_index("lat"), lax.axis_index("lon")
    first, final = lat == 0, lat == lat_count - 1
    lane_row = lane_iota((1, LANES))

    def block(lat_index, lon_index):
        return lat_index * lon_count + lon_index

    west_lon = lax.rem(lon + lon_count - 1, lon_count)
    east_lon = lax.rem(lon + 1, lon_count)
    south_lat = jnp.maximum(lat - 1, 0)
    north_lat = jnp.minimum(lat + 1, lat_count - 1)

    def edge(ref, group):
        return ref[group * rows : (group + 1) * rows, :]

    def corner(lat_index, lon_index, row):
        return recv_ref[block(lat_index, lon_index), row : row + 1, :]

    def east_of(row):
        return jnp.where(lane_row < lev, pltpu.roll(row, 2 * lev, 1), pltpu.roll(row, 3 * lev, 1))

    def north_of(row):
        return jnp.where(lane_row < lev, pltpu.roll(row, lev, 1), pltpu.roll(row, 2 * lev, 1))

    def upwind(wind, here, ahead):
        return jnp.maximum(wind, 0.0) * here + jnp.minimum(wind, 0.0) * ahead

    def beside(column, west_east, west_value, here_east, east_value, mass):
        fluxes = upwind(north_of(column[: rows + 1]), column[: rows + 1], column[1:])
        index = lax.broadcasted_iota(jnp.int32, (rows + 1, LANES), 0)
        closed = ((index == 0) & first) | ((index == rows) & final)
        fluxes = jnp.where(closed, 0.0, fluxes)
        here = column[1 : rows + 1]
        zonal = upwind(here_east, here, east_value) - upwind(west_east, west_value, here)
        return here - mass * (zonal + fluxes[1:] - fluxes[:-1])

    far_west, far_east = edge(west_ref, 0), edge(east_ref, 3)
    own_first, own_last = edge(own_ref, 2), edge(own_ref, 1)
    west = jnp.concatenate(
        [corner(south_lat, west_lon, 2), edge(west_ref, 1), corner(north_lat, west_lon, 4)], axis=0
    )
    east = jnp.concatenate(
        [corner(south_lat, east_lon, 3), edge(east_ref, 2), corner(north_lat, east_lon, 5)], axis=0
    )
    west_mid, east_mid = west[1 : rows + 1], east[1 : rows + 1]
    west_new = beside(
        west, east_of(far_west), far_west, east_of(west_mid), own_first, north_of(far_west)
    )
    east_new = beside(
        east, east_of(own_last), own_last, east_of(east_mid), far_east, east_of(far_east)
    )
    filler = jnp.zeros((LANES - 2 * (rows + 2) - 2 * rows, LANES), jnp.float32)
    turned = jnp.transpose(jnp.concatenate([west, east, west_new, east_new, filler], axis=0))

    def column(index, start, size):
        return jnp.broadcast_to(turned[start : start + size, index : index + 1], (size, LANES))

    def place(value, lane, index, start, size):
        return jnp.where(lane_row == lane, column(index, start, size), value)

    even = lax.rem(lat, 2) == 0

    def low(start, size):
        return jnp.where(even, odd_ref[start : start + size], even_ref[start : start + size])

    def high(start, size):
        return jnp.where(even, even_ref[start : start + size], odd_ref[start : start + size])

    tracer = {-2: low(0, two), -1: low(two, two)}
    east_wind = {-1: low(2 * two, lev)}
    north_wind = {-2: low(2 * two + lev, lev), -1: low(2 * two + 2 * lev, lev)}
    mass = {-1: low(2 * two + 3 * lev, lev)}
    for j in range(rows):
        tracer[j] = tr_ref[pl.ds(j, two, stride=rows), :]
        east_wind[j] = wind_ref[pl.ds(j, lev, stride=rows), :]
        north_wind[j] = wind_ref[pl.ds(levels * rows + j, lev, stride=rows), :]
        mass[j] = mass_ref[pl.ds(j, lev, stride=rows), :]
    tracer[rows], tracer[rows + 1] = high(two, two), high(0, two)
    east_wind[rows] = high(2 * two, lev)
    north_wind[rows] = high(2 * two + 2 * lev, lev)
    mass[rows] = high(2 * two + 3 * lev, lev)

    west_wind = {
        j: place(pltpu.roll(east_wind[j], 1, 1), 0, j + 1, two, lev) for j in range(-1, rows + 1)
    }

    def substep(field, row_range, west_index, east_index, start):
        fluxes = {}
        for j in range(row_range[0] - 1, row_range[-1] + 1):
            flux = upwind(north_wind[j], field[j], field[j + 1])
            if j == -1:
                flux = jnp.where(first, 0.0, flux)
            if j == rows - 1:
                flux = jnp.where(final, 0.0, flux)
            fluxes[j] = flux
        result = {}
        for j in row_range:
            here = field[j]
            ahead = place(pltpu.roll(here, LANES - 1, 1), LANES - 1, east_index(j), start, lev)
            behind = place(pltpu.roll(here, 1, 1), 0, west_index(j), start, lev)
            zonal = upwind(east_wind[j], here, ahead) - upwind(west_wind[j], behind, here)
            result[j] = here - mass[j] * (zonal + fluxes[j] - fluxes[j - 1])
        return result

    for t in range(2):
        start = t * lev
        field = {j: value[start : start + lev] for j, value in tracer.items()}
        once = substep(
            field, range(-1, rows + 1), lambda j: j + 1, lambda j: rows + 2 + j + 1, start
        )
        base = 2 * (rows + 2)
        twice = substep(once, range(rows), lambda j: base + j, lambda j: base + rows + j, start)
        for j in range(rows):
            out_ref[pl.ds(t * rows + j, lev, stride=2 * rows), :] = twice[j]


def solve_kernel(
    levels, rows, adv_ref, mine_ref, other_ref, out_hbm, diff_hbm, out_ref, diff_ref, kv_ref, sems
):
    faces = levels - 1
    half = levels // 2
    cols = rows * LANES
    width = 2 * rows
    low = half_levels(mine_ref[...], other_ref[...])
    high = half_levels(other_ref[...], mine_ref[...])
    diff_ref[0:half] = low[:, cols:]
    diff_ref[half:] = high[1:, cols:]
    put_diff = pltpu.make_async_copy(diff_ref, diff_hbm, sems.at[0])
    put_diff.start()
    for j in range(rows):
        here = slice(j * LANES, (j + 1) * LANES)
        for t in range(2):
            kv_ref[pl.ds(t * rows + j, half, stride=width), :] = low[:, here]
            kv_ref[pl.ds((faces - half) * width + t * rows + j, half, stride=width), :] = high[:, here]

    def face(level):
        return kv_ref[level * width : (level + 1) * width]

    def eliminate(order, outer_face, inner_face):
        ratios, sweeps = {}, {}
        last_level = None
        for level in order:
            rhs = adv_ref[level * width : (level + 1) * width]
            inner = inner_face(level)
            pivot = 1.0 + inner
            if last_level is not None:
                outer = outer_face(level)
                pivot = pivot + outer - outer * ratios[last_level]
                rhs = rhs + outer * sweeps[last_level]
            inverse = 1.0 / pivot
            ratios[level] = inner * inverse
            sweeps[level] = rhs * inverse
            last_level = level
        return ratios, sweeps

    down, down_sweep = eliminate(range(half), lambda k: face(k - 1), face)
    up, up_sweep = eliminate(range(levels - 1, half - 1, -1), face, lambda k: face(k - 1))

    def put(level, value):
        for t in range(2):
            out_ref[(t * levels + level) * rows : (t * levels + level + 1) * rows] = value[
                t * rows : (t + 1) * rows
            ]

    below = (down_sweep[half - 1] + down[half - 1] * up_sweep[half]) / (
        1.0 - down[half - 1] * up[half]
    )
    above = up_sweep[half] + up[half] * below
    put(half - 1, below)
    put(half, above)
    for step in range(1, half):
        below = down_sweep[half - 1 - step] + down[half - 1 - step] * below
        above = up_sweep[half + step] + up[half + step] * above
        put(half - 1 - step, below)
        put(half + step, above)
    put_out = pltpu.make_async_copy(out_ref, out_hbm, sems.at[1])
    put_out.start()
    put_diff.wait()
    put_out.wait()


def call(kernel, outs, in_specs, out_specs, scratch=()):
    return pl.pallas_call(
        kernel,
        out_shape=[jax.ShapeDtypeStruct(shape, jnp.float32) for shape in outs],
        in_specs=in_specs,
        out_specs=out_specs,
        scratch_shapes=list(scratch),
        compiler_params=pltpu.CompilerParams(vmem_limit_bytes=VMEM_LIMIT),
    )


def on_device(
    tracers, face_winds, inverse_mass, span_owner, span_slot, span_column_count, diffusivity
):
    own_count, levels, rows, cols = tracers.shape
    lat_count, lon_count = lax.axis_size("lat"), lax.axis_size("lon")
    devices = lat_count * lon_count
    half = levels // 2
    slot_total = diffusivity.shape[1]
    block_rows = MISC + half * (1 + rows)
    vmem = pl.BlockSpec(memory_space=pltpu.VMEM)
    hbm = pl.BlockSpec(memory_space=pltpu.HBM)

    tr = tracers.reshape(own_count * levels * rows, cols)
    winds = face_winds.reshape(2 * levels * rows, cols)
    mass = inverse_mass.reshape(levels * rows, cols)

    send, to_even, to_odd, shear, edges, active = call(
        functools.partial(pack_kernel, levels, rows, devices),
        [
            (devices, block_rows, LANES),
            (8 * levels, LANES),
            (8 * levels, LANES),
            (half, rows * LANES),
            (4 * rows, LANES),
            (1, slot_total),
        ],
        [hbm] * 7,
        [hbm] + [vmem] * 5,
        [
            pltpu.VMEM(tr.shape, jnp.float32),
            pltpu.VMEM(winds.shape, jnp.float32),
            pltpu.VMEM(mass.shape, jnp.float32),
            pltpu.VMEM(span_owner.shape, jnp.int32),
            pltpu.VMEM(span_slot.shape, jnp.int32),
            pltpu.VMEM(diffusivity.shape, jnp.float32),
            pltpu.SMEM(span_column_count.shape, jnp.int32),
            pltpu.VMEM((devices, block_rows, LANES), jnp.float32),
            pltpu.SemaphoreType.DMA((9,)),
        ],
    )(
        *(
            pltpu.with_memory_space_constraint(value, pltpu.HBM)
            for value in (tr, winds, mass, span_owner, span_slot, diffusivity, span_column_count)
        )
    )
    recv = lax.all_to_all(send, ("lat", "lon"), split_axis=0, concat_axis=0, tiled=True)
    even_pairs = [(i, i + 1) for i in range(0, lat_count - 1, 2)]
    odd_pairs = [(i, i + 1) for i in range(1, lat_count - 1, 2)]
    from_even = lax.ppermute(to_even, "lat", even_pairs + [(b, a) for a, b in even_pairs])
    from_odd = lax.ppermute(to_odd, "lat", odd_pairs + [(b, a) for a, b in odd_pairs])
    to_east = [(i, (i + 1) % lon_count) for i in range(lon_count)]
    to_west = [(target, source) for source, target in to_east]
    west_edges = lax.ppermute(edges, "lon", to_east)
    east_edges = west_edges if lon_count == 2 else lax.ppermute(edges, "lon", to_west)
    (mine,) = call(
        functools.partial(select_kernel, levels, rows, devices),
        [(half, rows * LANES + slot_total)],
        [vmem] * 6 + [pl.BlockSpec(memory_space=pl.ANY)],
        [vmem],
        [
            pltpu.VMEM((rows, LANES), jnp.float32),
            pltpu.VMEM((half, slot_total), jnp.float32),
        ],
    )(recv, span_owner, span_slot, diffusivity, active, shear, west_edges)
    other = lax.ppermute(mine, "lev", [(0, 1), (1, 0)])
    (advected,) = call(
        functools.partial(advect_kernel, levels, rows, lat_count, lon_count),
        [(levels * own_count * rows, LANES)],
        [vmem] * 9,
        [vmem],
    )(tr, winds, mass, from_even, from_odd, recv, edges, west_edges, east_edges)
    out, diff_out = call(
        functools.partial(solve_kernel, levels, rows),
        [(own_count * levels * rows, cols), (levels - 1, slot_total)],
        [vmem] * 3,
        [hbm] * 2,
        [
            pltpu.VMEM((own_count * levels * rows, cols), jnp.float32),
            pltpu.VMEM((levels - 1, slot_total), jnp.float32),
            pltpu.VMEM((levels * 2 * rows, LANES), jnp.float32),
            pltpu.SemaphoreType.DMA((2,)),
        ],
    )(advected, mine, other)
    return out.reshape(own_count, levels, rows, cols), diff_out


def solution(mesh):
    placed = (
        P("lev", "ens", "lat", "lon"),
        P(None, "ens", "lat", "lon"),
        P("ens", "lat", "lon"),
        P("lat", "lon"),
        P("lat", "lon"),
        P(("lat", "lon")),
        P("ens", ("lat", "lon")),
    )
    return jax.shard_map(
        on_device,
        mesh=mesh,
        in_specs=placed,
        out_specs=(P("lev", "ens", "lat", "lon"), P("ens", ("lat", "lon"))),
        check_vma=False,
    )
```

```python
import functools

import jax
import jax.numpy as jnp
from jax import lax
from jax.experimental import pallas as pl
from jax.experimental.pallas import tpu as pltpu
from jax.sharding import PartitionSpec as P

LANES = 128
MISC = 8
VMEM_LIMIT = 48 * 1024 * 1024
NT = (((1,), (1,)), ((), ()))


def lane_iota(shape):
    return lax.broadcasted_iota(jnp.int32, shape, len(shape) - 1)


def split3(values):
    top = values.astype(jnp.bfloat16)
    rest = values - top.astype(jnp.float32)
    mid = rest.astype(jnp.bfloat16)
    low = (rest - mid.astype(jnp.float32)).astype(jnp.bfloat16)
    return jnp.concatenate([top, mid, low], axis=0)


def hot_matrix(row_of, size):
    index = lax.broadcasted_iota(jnp.int32, (size, row_of.shape[-1]), 0)
    return jnp.where(index == row_of, 1.0, 0.0).astype(jnp.bfloat16)


def pick_columns(masked, hot, rows):
    out = lax.dot_general(masked, hot, NT, preferred_element_type=jnp.float32)
    return [
        out[at : at + rows] + out[at + rows : at + 2 * rows] + out[at + 2 * rows : at + 3 * rows]
        for at in range(0, masked.shape[0], 3 * rows)
    ]


def fold(count, body, start):
    if count > 8:
        return lax.fori_loop(0, count, body, start)
    for index in range(count):
        start = body(index, start)
    return start


def only_where(split, key, wanted):
    return split * jnp.where(key == wanted, 1.0, 0.0).astype(jnp.bfloat16)


def loop_over(count, body):
    if count <= 8:
        for index in range(count):
            body(index)
    else:
        pl.loop(0, count)(body)


def upwind(wind, here, ahead):
    return jnp.maximum(wind, 0.0) * here + jnp.minimum(wind, 0.0) * ahead


def half_levels(first, second):
    return jnp.where(lax.axis_index("lev") == 0, first, second)


def pack_kernel(
    levels, rows, devices, tr_hbm, wind_hbm, mass_hbm, owner_hbm, slot_hbm, diff_hbm, count_hbm,
    send_hbm, even_ref, odd_ref, shear_ref, edge_ref, active_ref,
    tr_ref, wind_ref, mass_ref, owner_ref, slot_ref, diff_ref, count_ref, send_ref, sems,
):
    faces = levels - 1
    half = levels // 2
    spans = diff_ref.shape[1] // LANES
    last = rows - 1
    head = MISC + half
    pairs = [
        (owner_hbm, owner_ref), (slot_hbm, slot_ref), (count_hbm, count_ref), (diff_hbm, diff_ref),
        (wind_hbm, wind_ref), (tr_hbm, tr_ref), (mass_hbm, mass_ref),
    ]
    copies = [
        pltpu.make_async_copy(source, target, sems.at[index])
        for index, (source, target) in enumerate(pairs)
    ]
    for copy in copies:
        copy.start()

    def tracer_row(j):
        return tr_ref[pl.ds(j, 2 * levels, stride=rows), :]

    def east_row(j):
        return wind_ref[pl.ds(j, levels, stride=rows), :]

    def north_row(j):
        return wind_ref[pl.ds(levels * rows + j, levels, stride=rows), :]

    def mass_row(j):
        return mass_ref[pl.ds(j, levels, stride=rows), :]

    copies[0].wait()
    owner_index = lax.broadcasted_iota(jnp.int32, (devices, LANES), 0)
    owned = [owner_index == owner_ref[j : j + 1, :] for j in range(rows)]
    upto = lax.broadcasted_iota(jnp.int32, (LANES, LANES), 0) <= lane_iota((LANES, LANES))
    counted = lax.dot_general(
        jnp.concatenate([jnp.where(hit, 1.0, 0.0) for hit in owned], axis=0).astype(jnp.bfloat16),
        jnp.where(upto, 1.0, 0.0).astype(jnp.bfloat16),
        (((1,), (0,)), ((), ())),
        preferred_element_type=jnp.float32,
    )
    before = jnp.full((devices, 1), -1.0, jnp.float32)
    ranks = []
    for j in range(rows):
        count = counted[j * devices : (j + 1) * devices]
        ranks.append(jnp.sum(jnp.where(owned[j], count + before, 0.0), axis=0, keepdims=True))
        before = before + count[:, LANES - 1 :]
    rank = jnp.concatenate(ranks, axis=1).astype(jnp.int32)
    owner = jnp.concatenate([owner_ref[j : j + 1, :] for j in range(rows)], axis=1)
    copies[1].wait()
    slots = jnp.concatenate([slot_ref[j : j + 1, :] for j in range(rows)], axis=1)

    copies[2].wait()
    copies[3].wait()
    diffs = half_levels(diff_ref[0:half], diff_ref[faces - half :])
    lane_half = lane_iota((half, LANES))
    lane_row = lane_iota((1, LANES))
    starts, start = [], 0
    for span in range(spans):
        starts.append(start)
        start = start + count_ref[span]
    for group in range(rows):
        if group < last:
            value = jnp.zeros((half, LANES), jnp.float32)
            for span in range(spans - 1):
                spot = lane_half + (group * LANES - starts[span])
                taken = jnp.take_along_axis(
                    diffs[:, span * LANES : (span + 1) * LANES], spot & (LANES - 1), axis=1
                )
                value = jnp.where((spot >= 0) & (spot < count_ref[span]), taken, value)
        else:
            value = diffs[:, (spans - 1) * LANES :]

        def store(dest):
            send_ref[dest, head + half * group : head + half * (group + 1)] = value

        loop_over(devices, store)
    put_diffs = pltpu.make_async_copy(
        send_ref.at[:, pl.ds(head, half * rows)],
        send_hbm.at[:, pl.ds(head, half * rows)],
        sems.at[len(pairs)],
    )
    put_diffs.start()
    start_row = jnp.zeros((1, LANES), jnp.float32)
    for span in range(spans):
        here = lax.convert_element_type(starts[span], jnp.float32)
        start_row = jnp.where(lane_row == span, here, start_row)
        active_ref[:, span * LANES : (span + 1) * LANES] = jnp.where(
            lane_row < count_ref[span], 1.0, 0.0
        )

    copies[4].wait()
    shears = []
    for j in range(rows):
        east, north = east_row(j), north_row(j)
        east_step = east[1:] - east[:-1]
        north_step = north[1:] - north[:-1]
        shear = east_step * east_step + north_step * north_step
        shears.append(half_levels(shear[:half], shear[faces - half :]))
    shear = jnp.concatenate(shears, axis=1)
    shear_ref[...] = shear

    copies[5].wait()

    def turn(j):
        return jnp.transpose(jnp.concatenate([tracer_row(j), east_row(j), north_row(j)], axis=0))

    turned = {j: turn(j) for j in (0, last)}
    misc = jnp.concatenate(
        [
            start_row,
            turned[last][LANES - 1 :],
            turned[last][0:1],
            turned[0][LANES - 1 :],
            turned[0][0:1],
            jnp.zeros((2, LANES), jnp.float32),
        ],
        axis=0,
    )

    extra = jnp.concatenate(
        [slots.astype(jnp.float32) + 1.0, jnp.zeros((7, rows * LANES), jnp.float32)], axis=0
    )
    split = split3(jnp.concatenate([shear, extra], axis=0))
    hot = hot_matrix(rank, LANES)

    def fill(dest, grouped):
        send_ref[dest, 0:1] = grouped[half : half + 1] - 1.0
        send_ref[dest, 1:MISC] = misc
        send_ref[dest, MISC:head] = grouped[:half]

    if devices <= 8:
        masked = [only_where(split, owner, dest) for dest in range(devices)]
        for dest, grouped in enumerate(
            pick_columns(jnp.concatenate(masked, axis=0), hot, half + 8)
        ):
            fill(dest, grouped)
    else:
        pl.loop(0, devices)(
            lambda dest: fill(dest, pick_columns(only_where(split, owner, dest), hot, half + 8)[0])
        )
    put_head = pltpu.make_async_copy(
        send_ref.at[:, pl.ds(0, head)], send_hbm.at[:, pl.ds(0, head)], sems.at[len(pairs) + 1]
    )
    put_head.start()

    copies[6].wait()
    masses = jnp.transpose(jnp.concatenate([mass_row(j) for j in range(rows)], axis=0))
    turned.update({j: turn(j) for j in range(1, last)})
    edge_rows = [[], [], [], []]
    for j in range(rows):
        west_mass = pltpu.roll(masses[0:1], (2 * levels - j * levels) % LANES, 1)
        east_mass = pltpu.roll(masses[LANES - 1 :], (3 * levels - j * levels) % LANES, 1)
        edge_rows[0].append(
            jnp.where(lane_row >= 3 * levels, east_mass, turned[j][LANES - 2 : LANES - 1])
        )
        edge_rows[1].append(turned[j][LANES - 1 :])
        edge_rows[2].append(turned[j][0:1])
        edge_rows[3].append(jnp.where(lane_row >= 2 * levels, west_mass, turned[j][1:2]))
    edge_ref[...] = jnp.concatenate([row for group in edge_rows for row in group], axis=0)

    lane_level = lane_iota((levels, LANES))

    def partly_advected(t, near, beyond, sign):
        here = tr_ref[pl.ds(t * levels * rows + near, levels, stride=rows), :]
        other = tr_ref[pl.ds(t * levels * rows + beyond, levels, stride=rows), :]
        ahead = jnp.where(lane_level == LANES - 1, 0.0, pltpu.roll(here, LANES - 1, 1))
        flux = upwind(east_row(near), here, ahead)
        zonal = flux - jnp.where(lane_level == 0, 0.0, pltpu.roll(flux, 1, 1))
        if sign > 0:
            merid = upwind(north_row(near), here, other)
        else:
            merid = -upwind(north_row(beyond), other, here)
        return here, here - mass_row(near) * (zonal + merid)

    wind = north_row(last)
    ahead_wind = jnp.maximum(wind, 0.0)
    to_north, to_south = [], []
    for t in range(2):
        here, new = partly_advected(t, last, last - 1, -1)
        to_north += [ahead_wind * here, ahead_wind * new]
        to_south += partly_advected(t, 0, 1, 1)
    to_north.append(jnp.where(wind < 0.0, wind, ahead_wind * mass_row(last)))
    to_south.append(mass_row(0))
    even = lax.rem(lax.axis_index("lat"), 2) == 0
    for index, (north, south) in enumerate(zip(to_north, to_south)):
        here = slice(index * levels, (index + 1) * levels)
        even_ref[here] = jnp.where(even, north, south)
        odd_ref[here] = jnp.where(even, south, north)

    put_diffs.wait()
    put_head.wait()


def source_term(shear):
    return 2.0 * shear / (0.05 + shear)


def select_kernel(
    levels, rows, devices, recv_ref, owner_ref, slot_ref, diff_ref, active_ref, shear_ref,
    after_ref, mine_ref,
):
    faces = levels - 1
    half = levels // 2
    slot_total = diff_ref.shape[1]
    spans = slot_total // LANES
    cols = rows * LANES

    owner = owner_ref[...]
    slot = slot_ref[...]
    span = slot // LANES

    def look_up(source, start):
        table = jnp.broadcast_to(recv_ref[source, 1:2, :], (rows, LANES))
        return jnp.where(owner == source, jnp.take_along_axis(table, span, axis=1), start)

    start = fold(devices, look_up, jnp.zeros((rows, LANES), jnp.float32))
    place = start.astype(jnp.int32) + (slot - span * LANES)
    group_of = owner * rows + place // LANES
    position = place & (LANES - 1)

    def gather(source, found):
        result = []
        for j in range(rows):
            spot = jnp.broadcast_to(position[j : j + 1], (half, LANES))
            value = found[j]
            for group in range(rows):
                held = recv_ref[source, MISC + half * (group + 1) : MISC + half * (group + 2), :]
                taken = jnp.take_along_axis(held, spot, axis=1)
                value = jnp.where(group_of[j : j + 1] == source * rows + group, taken, value)
            result.append(value)
        return tuple(result)

    found = fold(devices, gather, (jnp.zeros((half, LANES), jnp.float32),) * rows)
    for j in range(rows):
        here = slice(j * LANES, (j + 1) * LANES)
        mine_ref[:, here] = 0.5 * found[j] + source_term(shear_ref[:, here])

    def place_columns(slot_row, values):
        split = split3(values)
        masked = [only_where(split, slot_row >> 7, index) for index in range(spans)]
        hot = hot_matrix(slot_row & (LANES - 1), LANES)
        return jnp.concatenate(
            pick_columns(jnp.concatenate(masked, axis=0), hot, half), axis=1
        )

    def slots_of(source):
        return recv_ref[source, 0:1, :].astype(jnp.int32)

    def shears_of(source):
        return recv_ref[source, MISC : MISC + half, :]

    if devices <= 8:
        arrived = place_columns(
            jnp.concatenate([slots_of(source) for source in range(devices)], axis=1),
            jnp.concatenate([shears_of(source) for source in range(devices)], axis=1),
        )
    else:
        arrived = lax.fori_loop(
            0,
            devices,
            lambda source, total: total + place_columns(slots_of(source), shears_of(source)),
            jnp.zeros((half, slot_total), jnp.float32),
        )
    old = half_levels(diff_ref[0:half], diff_ref[faces - half :])
    new = 0.5 * old + source_term(arrived)
    mine_ref[:, cols:] = jnp.where(active_ref[...] > 0.0, new, old)


def advect_kernel(
    levels, rows, lat_count, lon_count, tr_ref, wind_ref, mass_ref, even_ref, odd_ref, recv_ref,
    own_ref, west_ref, east_ref, out_ref,
):
    lev, two = levels, 2 * levels
    lat, lon = lax.axis_index("lat"), lax.axis_index("lon")
    first, final = lat == 0, lat == lat_count - 1
    lane_row = lane_iota((1, LANES))
    west_lon = lax.rem(lon + lon_count - 1, lon_count)
    east_lon = lax.rem(lon + 1, lon_count)
    south_lat = jnp.maximum(lat - 1, 0)
    north_lat = jnp.minimum(lat + 1, lat_count - 1)

    def edge(ref, group):
        return ref[group * rows : (group + 1) * rows, :]

    def corner(lat_index, lon_index, row):
        return recv_ref[lat_index * lon_count + lon_index, row : row + 1, :]

    def east_of(row):
        return jnp.where(lane_row < lev, pltpu.roll(row, 2 * lev, 1), pltpu.roll(row, 3 * lev, 1))

    def north_of(row):
        return jnp.where(lane_row < lev, pltpu.roll(row, lev, 1), pltpu.roll(row, 2 * lev, 1))

    def beside(column, west_east, west_value, here_east, east_value, mass):
        fluxes = upwind(north_of(column[: rows + 1]), column[: rows + 1], column[1:])
        index = lax.broadcasted_iota(jnp.int32, (rows + 1, LANES), 0)
        closed = ((index == 0) & first) | ((index == rows) & final)
        fluxes = jnp.where(closed, 0.0, fluxes)
        here = column[1 : rows + 1]
        zonal = upwind(here_east, here, east_value) - upwind(west_east, west_value, here)
        return here - mass * (zonal + fluxes[1:] - fluxes[:-1])

    far_west, far_east = edge(west_ref, 0), edge(east_ref, 3)
    own_first, own_last = edge(own_ref, 2), edge(own_ref, 1)
    west_mid, east_mid = edge(west_ref, 1), edge(east_ref, 2)
    south_west, south_east = corner(south_lat, west_lon, 2), corner(south_lat, east_lon, 3)
    north_west, north_east = corner(north_lat, west_lon, 4), corner(north_lat, east_lon, 5)
    west_new = beside(
        jnp.concatenate([south_west, west_mid, north_west], axis=0),
        east_of(far_west), far_west, east_of(west_mid), own_first, north_of(far_west),
    )
    east_new = beside(
        jnp.concatenate([south_east, east_mid, north_east], axis=0),
        east_of(own_last), own_last, east_of(east_mid), far_east, east_of(far_east),
    )

    def end_fluxes(lat_index, row, west_cell, east_cell):
        own_end, own_start = corner(lat_index, lon, row), corner(lat_index, lon, row + 1)
        return [
            upwind(east_of(west_cell), west_cell, own_start),
            jnp.minimum(east_of(own_end), 0.0) * east_cell,
        ]

    ends = end_fluxes(south_lat, 2, south_west, south_east)
    ends += end_fluxes(north_lat, 4, north_west, north_east)
    used = [west_mid, east_mid, west_new, east_new] + ends
    filler = jnp.zeros((LANES - 4 * rows - 4, LANES), jnp.float32)
    turned = jnp.transpose(jnp.concatenate(used + [filler], axis=0))

    def column(index, start, size):
        return jnp.broadcast_to(turned[start : start + size, index : index + 1], (size, LANES))

    def put(value, lane, index, start):
        return jnp.where(lane_row == lane, column(index, start, lev), value)

    even = lax.rem(lat, 2) == 0

    def low(index):
        here = slice(index * lev, (index + 1) * lev)
        return jnp.where(even, odd_ref[here], even_ref[here])

    def high(index):
        here = slice(index * lev, (index + 1) * lev)
        return jnp.where(even, even_ref[here], odd_ref[here])

    east_wind = [wind_ref[pl.ds(j, lev, stride=rows), :] for j in range(rows)]
    north_wind = [wind_ref[pl.ds(lev * rows + j, lev, stride=rows), :] for j in range(rows)]
    mass = [mass_ref[pl.ds(j, lev, stride=rows), :] for j in range(rows)]
    west_wind = [put(pltpu.roll(east_wind[j], 1, 1), 0, j, two) for j in range(rows)]
    low_wind, low_share = jnp.minimum(low(4), 0.0), jnp.maximum(low(4), 0.0)
    high_mass = high(4)

    def substep(field, west_index, east_index, start, low_flux, high_flux):
        fluxes = [jnp.where(first, 0.0, low_flux)]
        for j in range(rows - 1):
            fluxes.append(upwind(north_wind[j], field[j], field[j + 1]))
        fluxes.append(jnp.where(final, 0.0, high_flux))
        result = []
        for j in range(rows):
            here = field[j]
            ahead = put(pltpu.roll(here, LANES - 1, 1), LANES - 1, east_index + j, start)
            behind = put(pltpu.roll(here, 1, 1), 0, west_index + j, start)
            zonal = upwind(east_wind[j], here, ahead) - upwind(west_wind[j], behind, here)
            result.append(here - mass[j] * (zonal + fluxes[j + 1] - fluxes[j]))
        return result

    for t in range(2):
        start = t * lev

        def left_out(index):
            zero = jnp.zeros((lev, LANES), jnp.float32)
            return put(put(zero, 0, index, start) * -1.0, LANES - 1, index + 1, start)

        field = [tr_ref[pl.ds(t * lev * rows + j, lev, stride=rows), :] for j in range(rows)]
        low_flux = low(2 * t) + low_wind * field[0]
        high_flux = upwind(north_wind[rows - 1], field[rows - 1], high(2 * t))
        once = substep(field, 0, rows, start, low_flux, high_flux)
        low_new = low(2 * t + 1) - low_share * (low_flux + left_out(4 * rows))
        high_new = high(2 * t + 1) - high_mass * (left_out(4 * rows + 2) - high_flux)
        twice = substep(
            once, 2 * rows, 3 * rows, start,
            low_new + low_wind * once[0],
            upwind(north_wind[rows - 1], once[rows - 1], high_new),
        )
        for j in range(rows):
            out_ref[pl.ds(t * rows + j, lev, stride=2 * rows), :] = twice[j]


def solve_kernel(
    levels, rows, adv_ref, mine_ref, other_ref, out_hbm, diff_hbm, out_ref, diff_ref, kv_ref, sems
):
    faces = levels - 1
    half = levels // 2
    cols = rows * LANES
    width = 2 * rows
    low = half_levels(mine_ref[...], other_ref[...])
    high = half_levels(other_ref[...], mine_ref[...])
    diff_ref[0:half] = low[:, cols:]
    diff_ref[half:] = high[1:, cols:]
    put_diff = pltpu.make_async_copy(diff_ref, diff_hbm, sems.at[0])
    put_diff.start()
    for j in range(rows):
        here = slice(j * LANES, (j + 1) * LANES)
        for t in range(2):
            kv_ref[pl.ds(t * rows + j, half, stride=width), :] = low[:, here]
            kv_ref[pl.ds((faces - half) * width + t * rows + j, half, stride=width), :] = high[:, here]

    def face(level):
        return kv_ref[level * width : (level + 1) * width]

    def eliminate(order, outer_face, inner_face):
        ratios, sweeps = {}, {}
        last_level = None
        for level in order:
            rhs = adv_ref[level * width : (level + 1) * width]
            inner = inner_face(level)
            pivot = 1.0 + inner
            if last_level is not None:
                outer = outer_face(level)
                pivot = pivot + outer - outer * ratios[last_level]
                rhs = rhs + outer * sweeps[last_level]
            inverse = 1.0 / pivot
            ratios[level] = inner * inverse
            sweeps[level] = rhs * inverse
            last_level = level
        return ratios, sweeps

    down, down_sweep = eliminate(range(half), lambda k: face(k - 1), face)
    up, up_sweep = eliminate(range(levels - 1, half - 1, -1), face, lambda k: face(k - 1))

    def put(level, value):
        for t in range(2):
            out_ref[(t * levels + level) * rows : (t * levels + level + 1) * rows] = value[
                t * rows : (t + 1) * rows
            ]

    below = (down_sweep[half - 1] + down[half - 1] * up_sweep[half]) / (
        1.0 - down[half - 1] * up[half]
    )
    above = up_sweep[half] + up[half] * below
    put(half - 1, below)
    put(half, above)
    for step in range(1, half):
        below = down_sweep[half - 1 - step] + down[half - 1 - step] * below
        above = up_sweep[half + step] + up[half + step] * above
        put(half - 1 - step, below)
        put(half + step, above)
    put_out = pltpu.make_async_copy(out_ref, out_hbm, sems.at[1])
    put_out.start()
    put_diff.wait()
    put_out.wait()


def call(kernel, outs, in_specs, out_specs, scratch=()):
    return pl.pallas_call(
        kernel,
        out_shape=[jax.ShapeDtypeStruct(shape, jnp.float32) for shape in outs],
        in_specs=in_specs,
        out_specs=out_specs,
        scratch_shapes=list(scratch),
        compiler_params=pltpu.CompilerParams(vmem_limit_bytes=VMEM_LIMIT),
    )


def on_device(
    tracers, face_winds, inverse_mass, span_owner, span_slot, span_column_count, diffusivity
):
    own_count, levels, rows, cols = tracers.shape
    lat_count, lon_count = lax.axis_size("lat"), lax.axis_size("lon")
    devices = lat_count * lon_count
    half = levels // 2
    slot_total = diffusivity.shape[1]
    block_rows = MISC + half * (1 + rows)
    vmem = pl.BlockSpec(memory_space=pltpu.VMEM)
    hbm = pl.BlockSpec(memory_space=pltpu.HBM)

    tr = tracers.reshape(own_count * levels * rows, cols)
    winds = face_winds.reshape(2 * levels * rows, cols)
    mass = inverse_mass.reshape(levels * rows, cols)

    send, to_even, to_odd, shear, edges, active = call(
        functools.partial(pack_kernel, levels, rows, devices),
        [
            (devices, block_rows, LANES),
            (5 * levels, LANES),
            (5 * levels, LANES),
            (half, rows * LANES),
            (4 * rows, LANES),
            (1, slot_total),
        ],
        [hbm] * 7,
        [hbm] + [vmem] * 5,
        [
            pltpu.VMEM(tr.shape, jnp.float32),
            pltpu.VMEM(winds.shape, jnp.float32),
            pltpu.VMEM(mass.shape, jnp.float32),
            pltpu.VMEM(span_owner.shape, jnp.int32),
            pltpu.VMEM(span_slot.shape, jnp.int32),
            pltpu.VMEM(diffusivity.shape, jnp.float32),
            pltpu.SMEM(span_column_count.shape, jnp.int32),
            pltpu.VMEM((devices, block_rows, LANES), jnp.float32),
            pltpu.SemaphoreType.DMA((9,)),
        ],
    )(
        *(
            pltpu.with_memory_space_constraint(value, pltpu.HBM)
            for value in (tr, winds, mass, span_owner, span_slot, diffusivity, span_column_count)
        )
    )
    recv = lax.all_to_all(send, ("lat", "lon"), split_axis=0, concat_axis=0, tiled=True)
    even_pairs = [(i, i + 1) for i in range(0, lat_count - 1, 2)]
    odd_pairs = [(i, i + 1) for i in range(1, lat_count - 1, 2)]
    from_even = lax.ppermute(to_even, "lat", even_pairs + [(b, a) for a, b in even_pairs])
    from_odd = lax.ppermute(to_odd, "lat", odd_pairs + [(b, a) for a, b in odd_pairs])
    to_east = [(i, (i + 1) % lon_count) for i in range(lon_count)]
    to_west = [(target, source) for source, target in to_east]
    west_edges = lax.ppermute(edges, "lon", to_east)
    east_edges = west_edges if lon_count == 2 else lax.ppermute(edges, "lon", to_west)
    (mine,) = call(
        functools.partial(select_kernel, levels, rows, devices),
        [(half, rows * LANES + slot_total)],
        [vmem] * 6 + [pl.BlockSpec(memory_space=pl.ANY)],
        [vmem],
    )(recv, span_owner, span_slot, diffusivity, active, shear, west_edges)
    other = lax.ppermute(mine, "lev", [(0, 1), (1, 0)])
    (advected,) = call(
        functools.partial(advect_kernel, levels, rows, lat_count, lon_count),
        [(levels * own_count * rows, LANES)],
        [vmem] * 9,
        [vmem],
    )(tr, winds, mass, from_even, from_odd, recv, edges, west_edges, east_edges)
    out, diff_out = call(
        functools.partial(solve_kernel, levels, rows),
        [(own_count * levels * rows, cols), (levels - 1, slot_total)],
        [vmem] * 3,
        [hbm] * 2,
        [
            pltpu.VMEM((own_count * levels * rows, cols), jnp.float32),
            pltpu.VMEM((levels - 1, slot_total), jnp.float32),
            pltpu.VMEM((levels * 2 * rows, LANES), jnp.float32),
            pltpu.SemaphoreType.DMA((2,)),
        ],
    )(advected, mine, other)
    return out.reshape(own_count, levels, rows, cols), diff_out


def solution(mesh):
    placed = (
        P("lev", "ens", "lat", "lon"),
        P(None, "ens", "lat", "lon"),
        P("ens", "lat", "lon"),
        P("lat", "lon"),
        P("lat", "lon"),
        P(("lat", "lon")),
        P("ens", ("lat", "lon")),
    )
    return jax.shard_map(
        on_device,
        mesh=mesh,
        in_specs=placed,
        out_specs=(P("lev", "ens", "lat", "lon"), P("ens", ("lat", "lon"))),
        check_vma=False,
    )
```

```python
import functools

import jax
import jax.numpy as jnp
from jax import lax
from jax.experimental import pallas as pl
from jax.experimental.pallas import tpu as pltpu
from jax.sharding import PartitionSpec as P

LANES = 128
VMEM_LIMIT = 48 * 1024 * 1024
NT = (((1,), (1,)), ((), ()))


def lane_iota(shape):
    return lax.broadcasted_iota(jnp.int32, shape, len(shape) - 1)


def split3(values):
    top = values.astype(jnp.bfloat16)
    rest = values - top.astype(jnp.float32)
    mid = rest.astype(jnp.bfloat16)
    low = (rest - mid.astype(jnp.float32)).astype(jnp.bfloat16)
    return jnp.concatenate([top, mid, low], axis=0)


def hot_matrix(row_of, size):
    index = lax.broadcasted_iota(jnp.int32, (size, row_of.shape[-1]), 0)
    return jnp.where(index == row_of, 1.0, 0.0).astype(jnp.bfloat16)


def pick_columns(masked, hot, rows):
    out = lax.dot_general(masked, hot, NT, preferred_element_type=jnp.float32)
    return [
        out[at : at + rows] + out[at + rows : at + 2 * rows] + out[at + 2 * rows : at + 3 * rows]
        for at in range(0, masked.shape[0], 3 * rows)
    ]


def fold(count, body, start):
    if count > 8:
        return lax.fori_loop(0, count, body, start)
    for index in range(count):
        start = body(index, start)
    return start


def only_where(split, key, wanted):
    return split * jnp.where(key == wanted, 1.0, 0.0).astype(jnp.bfloat16)


def loop_over(count, body):
    if count <= 8:
        for index in range(count):
            body(index)
    else:
        pl.loop(0, count)(body)


def upwind(wind, here, ahead):
    return jnp.maximum(wind, 0.0) * here + jnp.minimum(wind, 0.0) * ahead


def half_levels(first, second):
    return jnp.where(lax.axis_index("lev") == 0, first, second)


def own_faces(values):
    middle = values.shape[0] // 2
    second = jnp.concatenate([values[middle + 1 :], values[middle : middle + 1]], axis=0)
    return half_levels(values[: middle + 1], second)


def pack_kernel(
    levels, rows, devices, tr_hbm, wind_hbm, mass_hbm, owner_hbm, slot_hbm, diff_hbm, count_hbm,
    send_hbm, even_ref, odd_ref, shear_ref, edge_ref, active_ref, asked_ref, rank_ref,
    owner_ref, old_ref, tr_ref, wind_ref, mass_ref,
    slot_ref, diff_ref, count_ref, part_ref, send_ref, sems,
):
    half = levels // 2
    spans = diff_ref.shape[1] // LANES
    last = rows - 1
    part = part_ref.shape[1]
    offset = pl.multiple_of(lax.axis_index("lev") * (levels * rows - part), 8)
    pairs = [
        (owner_hbm, owner_ref), (slot_hbm, slot_ref),
        (wind_hbm.at[pl.ds(offset, part)], part_ref.at[0]),
        (wind_hbm.at[pl.ds(levels * rows + offset, part)], part_ref.at[1]),
        (count_hbm, count_ref), (diff_hbm, diff_ref),
        (tr_hbm, tr_ref), (wind_hbm, wind_ref), (mass_hbm, mass_ref),
    ]
    copies = [
        pltpu.make_async_copy(source, target, sems.at[index])
        for index, (source, target) in enumerate(pairs)
    ]
    for copy in copies:
        copy.start()

    def tracer_row(j):
        return tr_ref[pl.ds(j, 2 * levels, stride=rows), :]

    def east_row(j):
        return wind_ref[pl.ds(j, levels, stride=rows), :]

    def north_row(j):
        return wind_ref[pl.ds(levels * rows + j, levels, stride=rows), :]

    def mass_row(j):
        return mass_ref[pl.ds(j, levels, stride=rows), :]

    copies[0].wait()
    owner_index = lax.broadcasted_iota(jnp.int32, (devices, LANES), 0)
    owned = [owner_index == owner_ref[j : j + 1, :] for j in range(rows)]
    upto = lax.broadcasted_iota(jnp.int32, (LANES, LANES), 0) <= lane_iota((LANES, LANES))
    counted = lax.dot_general(
        jnp.concatenate([jnp.where(hit, 1.0, 0.0) for hit in owned], axis=0).astype(jnp.bfloat16),
        jnp.where(upto, 1.0, 0.0).astype(jnp.bfloat16),
        (((1,), (0,)), ((), ())),
        preferred_element_type=jnp.float32,
    )
    before = jnp.full((devices, 1), -1.0, jnp.float32)
    ranks = []
    for j in range(rows):
        count = counted[j * devices : (j + 1) * devices]
        ranks.append(jnp.sum(jnp.where(owned[j], count + before, 0.0), axis=0, keepdims=True))
        before = before + count[:, LANES - 1 :]
    rank = jnp.concatenate(ranks, axis=1).astype(jnp.int32)
    for j in range(rows):
        rank_ref[j : j + 1, :] = rank[:, j * LANES : (j + 1) * LANES]
    owner = jnp.concatenate([owner_ref[j : j + 1, :] for j in range(rows)], axis=1)
    copies[1].wait()
    slots = jnp.concatenate([slot_ref[j : j + 1, :] for j in range(rows)], axis=1)

    copies[2].wait()
    copies[3].wait()
    held = part // rows
    shears = []
    for j in range(rows):
        east = part_ref[0, pl.ds(j, held, stride=rows), :]
        north = part_ref[1, pl.ds(j, held, stride=rows), :]
        east_step = east[1:] - east[:-1]
        north_step = north[1:] - north[:-1]
        shear = east_step * east_step + north_step * north_step
        second = jnp.concatenate([shear[2 : half + 1], shear[1:2]], axis=0)
        shears.append(half_levels(shear[:half], second))
    shear = jnp.concatenate(shears, axis=1)
    shear_ref[...] = shear

    extra = jnp.concatenate(
        [slots.astype(jnp.float32) + 1.0, jnp.zeros((7, rows * LANES), jnp.float32)], axis=0
    )
    split = split3(jnp.concatenate([shear, extra], axis=0))
    hot = hot_matrix(rank, LANES)
    lane_half = lane_iota((half, LANES))
    lane_row = lane_iota((1, LANES))
    middle = lax.broadcasted_iota(jnp.int32, (half, LANES), 0) == half - 1
    in_half = half_levels(lane_half, LANES - 1 - lane_half) < LANES // 2
    kept = jnp.logical_or(jnp.logical_not(middle), in_half)

    def fill(dest, grouped):
        slot_row = grouped[half : half + 1] - 1.0
        send_ref[dest, 0:half] = jnp.where(kept, grouped[:half], 0.0)
        send_ref[dest, 2 * half - 1 : 2 * half] = slot_row
        asked_ref[pl.ds(dest, 1), :] = slot_row.astype(jnp.int32)

    copies[4].wait()
    copies[5].wait()
    diffs = own_faces(diff_ref[...])
    old_ref[...] = diffs
    starts, start = [], 0
    for span in range(spans):
        starts.append(start)
        start = start + count_ref[span]
    packed = []
    for group in range(last):
        value = jnp.zeros((half, LANES), jnp.float32)
        for span in range(spans - 1):
            spot = lane_half + (group * LANES - starts[span])
            taken = jnp.take_along_axis(
                diffs[:, span * LANES : (span + 1) * LANES], spot & (LANES - 1), axis=1
            )
            value = jnp.where((spot >= 0) & (spot < count_ref[span]), taken, value)
        packed.append(value)
    packed.append(diffs[:, (spans - 1) * LANES :])
    start_row = jnp.zeros((1, LANES), jnp.float32)
    for span in range(spans):
        here = lax.convert_element_type(starts[span], jnp.float32)
        start_row = jnp.where(lane_row == span, here, start_row)
        active_ref[:, span * LANES : (span + 1) * LANES] = jnp.where(
            lane_row < count_ref[span], 1.0, 0.0
        )
    last_rows = [packed[0][half - 1 :], start_row]
    for group in range(rows // 2):
        last_rows.append(
            half_levels(packed[group][half - 1 :], packed[group + rows // 2][half - 1 :])
        )
    chunks = [
        jnp.where(middle, last_row, value) for value, last_row in zip(packed, last_rows)
    ]

    def store(dest):
        for group, chunk in enumerate(chunks):
            send_ref[dest, half * (group + 1) : half * (group + 2)] = chunk

    def put(start, size, sem):
        copy = pltpu.make_async_copy(
            send_ref.at[:, pl.ds(start, size)], send_hbm.at[:, pl.ds(start, size)], sems.at[sem]
        )
        copy.start()
        return copy

    loop_over(devices, store)
    put_tail = put(2 * half, half * (rows - 1), len(pairs))
    if devices <= 8:
        masked = [only_where(split, owner, dest) for dest in range(devices)]
        for dest, grouped in enumerate(
            pick_columns(jnp.concatenate(masked, axis=0), hot, half + 8)
        ):
            fill(dest, grouped)
    else:
        pl.loop(0, devices)(
            lambda dest: fill(dest, pick_columns(only_where(split, owner, dest), hot, half + 8)[0])
        )
    put_head = put(0, 2 * half, len(pairs) + 1)

    copies[6].wait()
    copies[7].wait()
    turned = [
        jnp.transpose(jnp.concatenate([tracer_row(j), east_row(j), north_row(j)], axis=0))
        for j in range(rows)
    ]
    corners = jnp.concatenate(
        [
            turned[last][LANES - 1 :],
            turned[last][0:1],
            turned[0][LANES - 1 :],
            turned[0][0:1],
            jnp.zeros((4, LANES), jnp.float32),
        ],
        axis=0,
    )
    corner_at = half * (rows + 1)

    def add_corners(dest):
        send_ref[dest, corner_at : corner_at + 8] = corners

    loop_over(devices, add_corners)
    put_corners = put(corner_at, 8, len(pairs) + 2)
    copies[8].wait()
    masses = jnp.transpose(jnp.concatenate([mass_row(j) for j in range(rows)], axis=0))
    edge_rows = [[], [], [], []]
    for j in range(rows):
        west_mass = pltpu.roll(masses[0:1], (2 * levels - j * levels) % LANES, 1)
        east_mass = pltpu.roll(masses[LANES - 1 :], (3 * levels - j * levels) % LANES, 1)
        edge_rows[0].append(
            jnp.where(lane_row >= 3 * levels, east_mass, turned[j][LANES - 2 : LANES - 1])
        )
        edge_rows[1].append(turned[j][LANES - 1 :])
        edge_rows[2].append(turned[j][0:1])
        edge_rows[3].append(jnp.where(lane_row >= 2 * levels, west_mass, turned[j][1:2]))
    edge_ref[...] = jnp.concatenate([row for group in edge_rows for row in group], axis=0)

    lane_level = lane_iota((levels, LANES))

    def partly_advected(t, near, beyond, sign):
        here = tr_ref[pl.ds(t * levels * rows + near, levels, stride=rows), :]
        other = tr_ref[pl.ds(t * levels * rows + beyond, levels, stride=rows), :]
        ahead = jnp.where(lane_level == LANES - 1, 0.0, pltpu.roll(here, LANES - 1, 1))
        flux = upwind(east_row(near), here, ahead)
        zonal = flux - jnp.where(lane_level == 0, 0.0, pltpu.roll(flux, 1, 1))
        if sign > 0:
            merid = upwind(north_row(near), here, other)
        else:
            merid = -upwind(north_row(beyond), other, here)
        return here, here - mass_row(near) * (zonal + merid)

    wind = north_row(last)
    ahead_wind = jnp.maximum(wind, 0.0)
    to_north, to_south = [], []
    for t in range(2):
        here, new = partly_advected(t, last, last - 1, -1)
        to_north += [ahead_wind * here, ahead_wind * new]
        to_south += partly_advected(t, 0, 1, 1)
    to_north.append(jnp.where(wind < 0.0, wind, ahead_wind * mass_row(last)))
    to_south.append(mass_row(0))
    even = lax.rem(lax.axis_index("lat"), 2) == 0
    for index, (north, south) in enumerate(zip(to_north, to_south)):
        here = slice(index * levels, (index + 1) * levels)
        even_ref[here] = jnp.where(even, north, south)
        odd_ref[here] = jnp.where(even, south, north)

    put_tail.wait()
    put_head.wait()
    put_corners.wait()


def from_side(lat, south, even_round, odd_round, here):
    even = lax.rem(lat, 2) == 0
    if south:
        return jnp.where(even, odd_round[here], even_round[here])
    return jnp.where(even, even_round[here], odd_round[here])


def source_term(shear):
    return 2.0 * shear / (0.05 + shear)


def select_kernel(
    levels, rows, devices, recv_ref, owner_ref, rank_ref, asked_ref, old_ref, active_ref, shear_ref,
    after_ref, mine_ref, lane_ref, group_ref, middle_ref,
):
    half = levels // 2
    slot_total = old_ref.shape[1]
    spans = slot_total // LANES
    cols = rows * LANES
    row_index = lax.broadcasted_iota(jnp.int32, (half, 1), 0)
    shared = row_index == half - 1
    counts = jnp.where(shared, half_levels(1.0, 0.0), 1.0)

    asked = asked_ref[...]
    span = jnp.maximum(asked >> 7, 0)
    start = jnp.take_along_axis(recv_ref[:, 3 * half - 1, :], span, axis=1).astype(jnp.int32)
    place = start + (asked & (LANES - 1))
    lane = place & (LANES - 1)
    group = jnp.where(asked < 0, -1, place >> 7)
    middle = jnp.zeros((devices, LANES), jnp.float32)
    for index in range(rows // 2):
        held = recv_ref[:, half * (index + 4) - 1, :]
        wanted = half_levels(index, index + rows // 2)
        middle = jnp.where(group == wanted, jnp.take_along_axis(held, lane, axis=1), middle)
    lane_ref[...] = lane
    group_ref[...] = group
    middle_ref[...] = middle

    def gather(source, found):
        spot = jnp.broadcast_to(lane_ref[pl.ds(source, 1), :], (half, LANES))
        kind = group_ref[pl.ds(source, 1), :]
        value = jnp.zeros((half, LANES), jnp.float32)
        for index in range(rows):
            held = recv_ref[source, half * (index + 1) : half * (index + 2), :]
            value = jnp.where(kind == index, jnp.take_along_axis(held, spot, axis=1), value)
        value = jnp.where(shared, middle_ref[pl.ds(source, 1), :], value)
        return tuple(
            jnp.where(
                owner_ref[j : j + 1, :] == source,
                jnp.take_along_axis(
                    value, jnp.broadcast_to(rank_ref[j : j + 1, :], (half, LANES)), axis=1
                ),
                found[j],
            )
            for j in range(rows)
        )

    found = fold(devices, gather, (jnp.zeros((half, LANES), jnp.float32),) * rows)
    for j in range(rows):
        here = slice(j * LANES, (j + 1) * LANES)
        mine_ref[:, here] = 0.5 * found[j] + counts * source_term(shear_ref[:, here])

    def place_columns(slot_row, values):
        split = split3(values)
        masked = [only_where(split, slot_row >> 7, index) for index in range(spans)]
        hot = hot_matrix(slot_row & (LANES - 1), LANES)
        return jnp.concatenate(
            pick_columns(jnp.concatenate(masked, axis=0), hot, half), axis=1
        )

    def slots_of(source):
        return recv_ref[source, 2 * half - 1 : 2 * half, :].astype(jnp.int32)

    def shears_of(source):
        return recv_ref[source, 0:half, :]

    if devices <= 8:
        arrived = place_columns(
            jnp.concatenate([slots_of(source) for source in range(devices)], axis=1),
            jnp.concatenate([shears_of(source) for source in range(devices)], axis=1),
        )
    else:
        arrived = lax.fori_loop(
            0,
            devices,
            lambda source, total: total + place_columns(slots_of(source), shears_of(source)),
            jnp.zeros((half, slot_total), jnp.float32),
        )
    old = counts * old_ref[...]
    new = 0.5 * old + source_term(arrived)
    mine_ref[:, cols:] = jnp.where(active_ref[...] > 0.0, new, old)


def advect_kernel(
    levels, rows, lat_count, lon_count, tr_ref, wind_ref, mass_ref, even_ref, odd_ref, recv_ref,
    own_ref, west_ref, east_ref, out_ref,
):
    lev, two = levels, 2 * levels
    lat, lon = lax.axis_index("lat"), lax.axis_index("lon")
    first, final = lat == 0, lat == lat_count - 1
    west_lon = lax.rem(lon + lon_count - 1, lon_count)
    east_lon = lax.rem(lon + 1, lon_count)
    south_lat = jnp.maximum(lat - 1, 0)
    north_lat = jnp.minimum(lat + 1, lat_count - 1)
    lane_row = lane_iota((1, LANES))

    def edge(ref, group):
        return ref[group * rows : (group + 1) * rows, :]

    def corner(lat_index, lon_index, row, size=1):
        at = recv_ref.shape[1] - 8 + row
        return recv_ref[lat_index * lon_count + lon_index, at : at + size, :]

    def from_south(here):
        return from_side(lat, True, even_ref, odd_ref, here)

    def from_north(here):
        return from_side(lat, False, even_ref, odd_ref, here)

    def east_of(row):
        return jnp.where(lane_row < lev, pltpu.roll(row, 2 * lev, 1), pltpu.roll(row, 3 * lev, 1))

    def north_of(row):
        return jnp.where(lane_row < lev, pltpu.roll(row, lev, 1), pltpu.roll(row, 2 * lev, 1))

    def beside(column, west_east, west_value, here_east, east_value, mass):
        fluxes = upwind(north_of(column[: rows + 1]), column[: rows + 1], column[1:])
        index = lax.broadcasted_iota(jnp.int32, (rows + 1, LANES), 0)
        closed = ((index == 0) & first) | ((index == rows) & final)
        fluxes = jnp.where(closed, 0.0, fluxes)
        here = column[1 : rows + 1]
        zonal = upwind(here_east, here, east_value) - upwind(west_east, west_value, here)
        return here - mass * (zonal + fluxes[1:] - fluxes[:-1])

    far_west, far_east = edge(west_ref, 0), edge(east_ref, 3)
    own_first, own_last = edge(own_ref, 2), edge(own_ref, 1)
    west_mid, east_mid = edge(west_ref, 1), edge(east_ref, 2)
    south_west, south_east = corner(south_lat, west_lon, 0), corner(south_lat, east_lon, 1)
    north_west, north_east = corner(north_lat, west_lon, 2), corner(north_lat, east_lon, 3)
    west_new = beside(
        jnp.concatenate([south_west, west_mid, north_west], axis=0),
        east_of(far_west), far_west, east_of(west_mid), own_first, north_of(far_west),
    )
    east_new = beside(
        jnp.concatenate([south_east, east_mid, north_east], axis=0),
        east_of(own_last), own_last, east_of(east_mid), far_east, east_of(far_east),
    )

    def end_fluxes(own_ends, west_cell, east_cell):
        return [
            upwind(east_of(west_cell), west_cell, own_ends[1:]),
            jnp.minimum(east_of(own_ends[:1]), 0.0) * east_cell,
        ]

    south_ends = corner(south_lat, lon, 0, 2)
    north_ends = corner(north_lat, lon, 2, 2)
    ends = end_fluxes(south_ends, south_west, south_east)
    ends += end_fluxes(north_ends, north_west, north_east)
    used = [west_mid, east_mid, west_new, east_new] + ends
    filler = jnp.zeros((LANES - 4 * rows - 4, LANES), jnp.float32)
    turned = jnp.transpose(jnp.concatenate(used + [filler], axis=0))

    def column(index, start, size):
        return jnp.broadcast_to(turned[start : start + size, index : index + 1], (size, LANES))

    def put(value, lane, index, start):
        return jnp.where(lane_row == lane, column(index, start, lev), value)

    def low(index):
        return from_south(slice(index * lev, (index + 1) * lev))

    def high(index):
        return from_north(slice(index * lev, (index + 1) * lev))

    east_wind = [wind_ref[pl.ds(j, lev, stride=rows), :] for j in range(rows)]
    north_wind = [wind_ref[pl.ds(lev * rows + j, lev, stride=rows), :] for j in range(rows)]
    mass = [mass_ref[pl.ds(j, lev, stride=rows), :] for j in range(rows)]
    west_wind = [put(pltpu.roll(east_wind[j], 1, 1), 0, j, two) for j in range(rows)]
    low_wind, low_share = jnp.minimum(low(4), 0.0), jnp.maximum(low(4), 0.0)
    high_mass = high(4)

    def substep(field, west_index, east_index, start, low_flux, high_flux):
        fluxes = [jnp.where(first, 0.0, low_flux)]
        for j in range(rows - 1):
            fluxes.append(upwind(north_wind[j], field[j], field[j + 1]))
        fluxes.append(jnp.where(final, 0.0, high_flux))
        result = []
        for j in range(rows):
            here = field[j]
            ahead = put(pltpu.roll(here, LANES - 1, 1), LANES - 1, east_index + j, start)
            behind = put(pltpu.roll(here, 1, 1), 0, west_index + j, start)
            zonal = upwind(east_wind[j], here, ahead) - upwind(west_wind[j], behind, here)
            result.append(here - mass[j] * (zonal + fluxes[j + 1] - fluxes[j]))
        return result

    for t in range(2):
        start = t * lev

        def left_out(index):
            zero = jnp.zeros((lev, LANES), jnp.float32)
            return put(put(zero, 0, index, start) * -1.0, LANES - 1, index + 1, start)

        field = [tr_ref[pl.ds(t * lev * rows + j, lev, stride=rows), :] for j in range(rows)]
        low_flux = low(2 * t) + low_wind * field[0]
        high_flux = upwind(north_wind[rows - 1], field[rows - 1], high(2 * t))
        once = substep(field, 0, rows, start, low_flux, high_flux)
        low_new = low(2 * t + 1) - low_share * (low_flux + left_out(4 * rows))
        high_new = high(2 * t + 1) - high_mass * (left_out(4 * rows + 2) - high_flux)
        twice = substep(
            once, 2 * rows, 3 * rows, start,
            low_new + low_wind * once[0],
            upwind(north_wind[rows - 1], once[rows - 1], high_new),
        )
        for j in range(rows):
            out_ref[pl.ds(t * rows + j, lev, stride=2 * rows), :] = twice[j]


def solve_kernel(
    levels, rows, adv_ref, mine_ref, other_ref, out_hbm, diff_hbm, out_ref, diff_ref, kv_ref, sems
):
    half = levels // 2
    cols = rows * LANES
    width = 2 * rows
    low = half_levels(mine_ref[...], other_ref[...])
    high = half_levels(other_ref[...], mine_ref[...])
    shared = low[half - 1 :] + high[half - 1 :]
    diff_ref[0 : half - 1] = low[: half - 1, cols:]
    diff_ref[half - 1 : half] = shared[:, cols:]
    diff_ref[half:] = high[: half - 1, cols:]
    put_diff = pltpu.make_async_copy(diff_ref, diff_hbm, sems.at[0])
    put_diff.start()
    for j in range(rows):
        here = slice(j * LANES, (j + 1) * LANES)
        for t in range(2):
            at = t * rows + j
            kv_ref[pl.ds(at, half - 1, stride=width), :] = low[: half - 1, here]
            kv_ref[pl.ds((half - 1) * width + at, 1), :] = shared[:, here]
            kv_ref[pl.ds(half * width + at, half - 1, stride=width), :] = high[: half - 1, here]

    def face(level):
        return kv_ref[level * width : (level + 1) * width]

    def eliminate(order, outer_face, inner_face):
        ratios, sweeps = {}, {}
        last_level = None
        for level in order:
            rhs = adv_ref[level * width : (level + 1) * width]
            inner = inner_face(level)
            pivot = 1.0 + inner
            if last_level is not None:
                outer = outer_face(level)
                pivot = pivot + outer - outer * ratios[last_level]
                rhs = rhs + outer * sweeps[last_level]
            inverse = 1.0 / pivot
            ratios[level] = inner * inverse
            sweeps[level] = rhs * inverse
            last_level = level
        return ratios, sweeps

    down, down_sweep = eliminate(range(half), lambda k: face(k - 1), face)
    up, up_sweep = eliminate(range(levels - 1, half - 1, -1), face, lambda k: face(k - 1))

    def put(level, value):
        for t in range(2):
            out_ref[(t * levels + level) * rows : (t * levels + level + 1) * rows] = value[
                t * rows : (t + 1) * rows
            ]

    below = (down_sweep[half - 1] + down[half - 1] * up_sweep[half]) / (
        1.0 - down[half - 1] * up[half]
    )
    above = up_sweep[half] + up[half] * below
    put(half - 1, below)
    put(half, above)
    for step in range(1, half):
        below = down_sweep[half - 1 - step] + down[half - 1 - step] * below
        above = up_sweep[half + step] + up[half + step] * above
        put(half - 1 - step, below)
        put(half + step, above)
    put_out = pltpu.make_async_copy(out_ref, out_hbm, sems.at[1])
    put_out.start()
    put_diff.wait()
    put_out.wait()


def call(kernel, outs, in_specs, out_specs, scratch=(), aliases=None):
    return pl.pallas_call(
        kernel,
        out_shape=[
            jax.ShapeDtypeStruct(out, jnp.float32) if isinstance(out, tuple) else out
            for out in outs
        ],
        in_specs=in_specs,
        out_specs=out_specs,
        scratch_shapes=list(scratch),
        input_output_aliases=aliases or {},
        compiler_params=pltpu.CompilerParams(vmem_limit_bytes=VMEM_LIMIT),
    )


def on_device(
    tracers, face_winds, inverse_mass, span_owner, span_slot, span_column_count, diffusivity
):
    own_count, levels, rows, cols = tracers.shape
    lat_count, lon_count = lax.axis_size("lat"), lax.axis_size("lon")
    devices = lat_count * lon_count
    half = levels // 2
    slot_total = diffusivity.shape[1]
    block_rows = half * (1 + rows) + 8
    vmem = pl.BlockSpec(memory_space=pltpu.VMEM)
    hbm = pl.BlockSpec(memory_space=pltpu.HBM)

    tr = tracers.reshape(own_count * levels * rows, cols)
    winds = face_winds.reshape(2 * levels * rows, cols)
    mass = inverse_mass.reshape(levels * rows, cols)

    outs = [
        (devices, block_rows, LANES),
        (5 * levels, LANES),
        (5 * levels, LANES),
        (half, rows * LANES),
        (4 * rows, LANES),
        (1, slot_total),
        jax.ShapeDtypeStruct((devices, LANES), jnp.int32),
        jax.ShapeDtypeStruct((rows, LANES), jnp.int32),
        jax.ShapeDtypeStruct((rows, LANES), jnp.int32),
        (half, slot_total),
        tr.shape,
        winds.shape,
        mass.shape,
    ]
    send, to_even, to_odd, shear, edges, active, asked, rank, owner, old, tr, winds, mass = call(
        functools.partial(pack_kernel, levels, rows, devices),
        outs,
        [hbm] * 7,
        [hbm] + [vmem] * (len(outs) - 1),
        [
            pltpu.VMEM(span_slot.shape, jnp.int32),
            pltpu.VMEM(diffusivity.shape, jnp.float32),
            pltpu.SMEM(span_column_count.shape, jnp.int32),
            pltpu.VMEM((2, (half + 2) * rows, LANES), jnp.float32),
            pltpu.VMEM((devices, block_rows, LANES), jnp.float32),
            pltpu.SemaphoreType.DMA((12,)),
        ],
    )(
        *(
            pltpu.with_memory_space_constraint(value, pltpu.HBM)
            for value in (tr, winds, mass, span_owner, span_slot, diffusivity, span_column_count)
        )
    )
    recv = lax.all_to_all(send, ("lat", "lon"), split_axis=0, concat_axis=0, tiled=True)
    from_lat = []
    for first, values in enumerate((to_even, to_odd)):
        pairs = [(i, i + 1) for i in range(first, lat_count - 1, 2)]
        from_lat.append(lax.ppermute(values, "lat", pairs + [(b, a) for a, b in pairs]))
    to_east = [(i, (i + 1) % lon_count) for i in range(lon_count)]
    to_west = [(target, source) for source, target in to_east]
    from_west = lax.ppermute(edges, "lon", to_east)
    from_east = from_west if lon_count == 2 else lax.ppermute(edges, "lon", to_west)
    (mine,) = call(
        functools.partial(select_kernel, levels, rows, devices),
        [(half, rows * LANES + slot_total)],
        [vmem] * 7 + [pl.BlockSpec(memory_space=pl.ANY)],
        [vmem],
        [
            pltpu.VMEM((devices, LANES), jnp.int32),
            pltpu.VMEM((devices, LANES), jnp.int32),
            pltpu.VMEM((devices, LANES), jnp.float32),
        ],
    )(recv, owner, rank, asked, old, active, shear, from_west)
    other = lax.ppermute(mine, "lev", [(0, 1), (1, 0)])
    (advected,) = call(
        functools.partial(advect_kernel, levels, rows, lat_count, lon_count),
        [(levels * own_count * rows, LANES)],
        [vmem] * 9,
        [vmem],
    )(tr, winds, mass, *from_lat, recv, edges, from_west, from_east)
    out, diff_out = call(
        functools.partial(solve_kernel, levels, rows),
        [(own_count * levels * rows, cols), (levels - 1, slot_total)],
        [vmem] * 3,
        [hbm] * 2,
        [
            pltpu.VMEM((own_count * levels * rows, cols), jnp.float32),
            pltpu.VMEM((levels - 1, slot_total), jnp.float32),
            pltpu.VMEM((levels * 2 * rows, LANES), jnp.float32),
            pltpu.SemaphoreType.DMA((2,)),
        ],
    )(advected, mine, other)
    return out.reshape(own_count, levels, rows, cols), diff_out


def solution(mesh):
    placed = (
        P("lev", "ens", "lat", "lon"),
        P(None, "ens", "lat", "lon"),
        P("ens", "lat", "lon"),
        P("lat", "lon"),
        P("lat", "lon"),
        P(("lat", "lon")),
        P("ens", ("lat", "lon")),
    )
    return jax.shard_map(
        on_device,
        mesh=mesh,
        in_specs=placed,
        out_specs=(P("lev", "ens", "lat", "lon"), P("ens", ("lat", "lon"))),
        check_vma=False,
    )
```

```python
import functools

import jax
import jax.numpy as jnp
from jax import lax
from jax.experimental import pallas as pl
from jax.experimental.pallas import tpu as pltpu
from jax.sharding import PartitionSpec as P

LANES = 128
VMEM_LIMIT = 48 * 1024 * 1024
NT = (((1,), (1,)), ((), ()))


def lane_iota(shape):
    return lax.broadcasted_iota(jnp.int32, shape, len(shape) - 1)


def split3(values):
    top = values.astype(jnp.bfloat16)
    rest = values - top.astype(jnp.float32)
    mid = rest.astype(jnp.bfloat16)
    low = (rest - mid.astype(jnp.float32)).astype(jnp.bfloat16)
    return jnp.concatenate([top, mid, low], axis=0)


def hot_matrix(row_of, size):
    index = lax.broadcasted_iota(jnp.int32, (size, row_of.shape[-1]), 0)
    return jnp.where(index == row_of, 1.0, 0.0).astype(jnp.bfloat16)


def pick_columns(masked, hot, rows):
    out = lax.dot_general(masked, hot, NT, preferred_element_type=jnp.float32)
    return [
        out[at : at + rows] + out[at + rows : at + 2 * rows] + out[at + 2 * rows : at + 3 * rows]
        for at in range(0, masked.shape[0], 3 * rows)
    ]


def fold(count, body, start):
    if count > 8:
        return lax.fori_loop(0, count, body, start)
    for index in range(count):
        start = body(index, start)
    return start


def only_where(split, key, wanted):
    return split * jnp.where(key == wanted, 1.0, 0.0).astype(jnp.bfloat16)


def loop_over(count, body):
    if count <= 8:
        for index in range(count):
            body(index)
    else:
        pl.loop(0, count)(body)


def upwind(wind, here, ahead):
    return jnp.maximum(wind, 0.0) * here + jnp.minimum(wind, 0.0) * ahead


def half_levels(first, second):
    return jnp.where(lax.axis_index("lev") == 0, first, second)


def own_faces(values):
    middle = values.shape[0] // 2
    second = jnp.concatenate([values[middle + 1 :], values[middle : middle + 1]], axis=0)
    return half_levels(values[: middle + 1], second)


def turn(levels, rows, tr_ref, wind_ref, j):
    fields = [
        tr_ref[pl.ds(j, 2 * levels, stride=rows), :],
        wind_ref[pl.ds(j, levels, stride=rows), :],
        wind_ref[pl.ds(levels * rows + j, levels, stride=rows), :],
    ]
    return jnp.transpose(jnp.concatenate(fields, axis=0))


def pack_kernel(
    levels, rows, devices, lon_count,
    tr_hbm, wind_hbm, mass_hbm, owner_hbm, slot_hbm, diff_hbm, count_hbm,
    send_hbm, shear_ref, active_ref, rank_ref, owner_ref, slot_ref, diff_ref, tr_ref, wind_ref, mass_ref,
    count_ref, send_ref, sems,
):
    half = levels // 2
    spans = diff_ref.shape[1] // LANES
    last = rows - 1
    lane_half = lane_iota((half, LANES))
    lane_row = lane_iota((1, LANES))
    bottom = lax.broadcasted_iota(jnp.int32, (half, LANES), 0) == half - 1
    pairs = [
        (owner_hbm, owner_ref), (slot_hbm, slot_ref), (wind_hbm, wind_ref), (count_hbm, count_ref),
        (diff_hbm, diff_ref), (tr_hbm, tr_ref), (mass_hbm, mass_ref),
    ]
    copies = [
        pltpu.make_async_copy(source, target, sems.at[index])
        for index, (source, target) in enumerate(pairs)
    ]
    for copy in copies:
        copy.start()

    def put(start, size, sem):
        copy = pltpu.make_async_copy(
            send_ref.at[:, pl.ds(start, size)], send_hbm.at[:, pl.ds(start, size)], sems.at[sem]
        )
        copy.start()
        return copy

    copies[0].wait()
    owner_index = lax.broadcasted_iota(jnp.int32, (devices, LANES), 0)
    owned = [owner_index == owner_ref[j : j + 1, :] for j in range(rows)]
    upto = lax.broadcasted_iota(jnp.int32, (LANES, LANES), 0) <= lane_iota((LANES, LANES))
    counted = lax.dot_general(
        jnp.concatenate([jnp.where(hit, 1.0, 0.0) for hit in owned], axis=0).astype(jnp.bfloat16),
        jnp.where(upto, 1.0, 0.0).astype(jnp.bfloat16),
        (((1,), (0,)), ((), ())),
        preferred_element_type=jnp.float32,
    )
    before = jnp.full((devices, 1), -1.0, jnp.float32)
    ranks = []
    for j in range(rows):
        count = counted[j * devices : (j + 1) * devices]
        rank = jnp.sum(jnp.where(owned[j], count + before, 0.0), axis=0, keepdims=True)
        ranks.append(rank.astype(jnp.int32))
        rank_ref[j : j + 1, :] = ranks[j]
        before = before + count[:, LANES - 1 :]
    owner = jnp.concatenate([owner_ref[j : j + 1, :] for j in range(rows)] * 2, axis=1)

    part = LANES // 2
    place = jnp.concatenate(ranks, axis=1) - half_levels(0, part)
    inside = (place >= 0) & (place < part)
    hot = hot_matrix(
        jnp.concatenate([jnp.where(inside, place, -1), jnp.where(inside, place + part, -1)], axis=1),
        LANES,
    )
    copies[1].wait()
    copies[2].wait()
    lower, upper = [], []
    for j in range(rows):
        east = wind_ref[pl.ds(j, levels, stride=rows), :]
        north = wind_ref[pl.ds(levels * rows + j, levels, stride=rows), :]
        east_step = east[1:] - east[:-1]
        north_step = north[1:] - north[:-1]
        shear = east_step * east_step + north_step * north_step
        slot = slot_ref[j : j + 1, :].astype(jnp.float32) + 1.0
        lower.append(shear[:half])
        upper.append(jnp.concatenate([shear[half:], slot], axis=0))
        shear_ref[:, j * LANES : (j + 1) * LANES] = own_faces(shear)
    split = split3(jnp.concatenate(lower + upper, axis=1))

    copies[3].wait()
    copies[4].wait()
    diffs = own_faces(diff_ref[...])
    starts, start = [], 0
    for span in range(spans):
        starts.append(start)
        start = start + count_ref[span]
    packed = []
    for group in range(last):
        value = jnp.zeros((half, LANES), jnp.float32)
        for span in range(spans - 1):
            spot = lane_half + (group * LANES - starts[span])
            taken = jnp.take_along_axis(
                diffs[:, span * LANES : (span + 1) * LANES], spot & (LANES - 1), axis=1
            )
            value = jnp.where((spot >= 0) & (spot < count_ref[span]), taken, value)
        packed.append(value)
    packed.append(diffs[:, (spans - 1) * LANES :])
    start_row = jnp.zeros((1, LANES), jnp.float32)
    for span in range(spans):
        here = lax.convert_element_type(starts[span], jnp.float32)
        start_row = jnp.where(lane_row == 3 * levels + span, here, start_row)
        active_ref[:, span * LANES : (span + 1) * LANES] = jnp.where(
            lane_row < count_ref[span], 1.0, 0.0
        )
    chunks = packed[:2]
    for group in range(rows // 2):
        shared = half_levels(packed[group][half - 1 :], packed[group + rows // 2][half - 1 :])
        chunks.append(jnp.where(bottom, shared, packed[group + 2]))

    def store_late(dest):
        for group in range(2, rows):
            send_ref[dest, half * (group + 1) : half * (group + 2)] = chunks[group]

    loop_over(devices, store_late)
    puts = [put(3 * half, half * (rows - 2), len(pairs))]

    copies[5].wait()
    ends = []
    for j in (0, last):
        turned = turn(levels, rows, tr_ref, wind_ref, j)
        east_end, west_end = turned[LANES - 1 :], turned[0:1]
        tracers = jnp.where(lane_row < part, east_end, pltpu.roll(west_end, part, 1))
        winds = jnp.where(
            lane_row < part,
            pltpu.roll(east_end, part, 1),
            jnp.where(lane_row < 3 * levels, pltpu.roll(west_end, 3 * levels, 1), start_row),
        )
        ends.append(
            [jnp.where(bottom, row, chunk) for row, chunk in zip((tracers, winds), chunks)]
        )

    def store_early(dest):
        northward = dest // lon_count > lax.axis_index("lat")
        for group in range(2):
            send_ref[dest, half * (group + 1) : half * (group + 2)] = jnp.where(
                northward, ends[1][group], ends[0][group]
            )

    loop_over(devices, store_early)
    puts.append(put(half, 2 * half, len(pairs) + 1))
    unasked = jnp.where(bottom & (lane_half >= part), 1.0, 0.0)

    def fill(dest, grouped):
        send_ref[dest, 0:half] = grouped - unasked

    if devices <= 8:
        masked = [only_where(split, owner, dest) for dest in range(devices)]
        for dest, grouped in enumerate(pick_columns(jnp.concatenate(masked, axis=0), hot, half)):
            fill(dest, grouped)
    else:
        pl.loop(0, devices)(
            lambda dest: fill(dest, pick_columns(only_where(split, owner, dest), hot, half)[0])
        )
    puts.append(put(0, half, len(pairs) + 2))
    copies[6].wait()
    for copy in puts:
        copy.wait()


def halo_kernel(
    levels, rows, devices, tr_ref, wind_ref, mass_ref, owner_ref, slot_ref, rank_ref,
    even_ref, odd_ref, edge_ref, asked_ref,
):
    last = rows - 1

    def flat(ref):
        return jnp.concatenate([ref[j : j + 1, :] for j in range(rows)], axis=1)

    owner, hot = flat(owner_ref), hot_matrix(flat(rank_ref), LANES)
    filler = jnp.zeros((7, rows * LANES), jnp.float32)
    split = split3(jnp.concatenate([flat(slot_ref).astype(jnp.float32) + 1.0, filler], axis=0))

    def ask(dest):
        (found,) = pick_columns(only_where(split, owner, dest), hot, 8)
        asked_ref[pl.ds(dest, 1), :] = found[0:1].astype(jnp.int32) - 1

    loop_over(devices, ask)
    lane_row = lane_iota((1, LANES))

    def east_row(j):
        return wind_ref[pl.ds(j, levels, stride=rows), :]

    def north_row(j):
        return wind_ref[pl.ds(levels * rows + j, levels, stride=rows), :]

    def mass_row(j):
        return mass_ref[pl.ds(j, levels, stride=rows), :]

    turned = [turn(levels, rows, tr_ref, wind_ref, j) for j in range(rows)]
    masses = jnp.transpose(jnp.concatenate([mass_row(j) for j in range(rows)], axis=0))
    edge_rows = [[], [], [], []]
    for j in range(rows):
        west_mass = pltpu.roll(masses[0:1], (2 * levels - j * levels) % LANES, 1)
        east_mass = pltpu.roll(masses[LANES - 1 :], (3 * levels - j * levels) % LANES, 1)
        edge_rows[0].append(
            jnp.where(lane_row >= 3 * levels, east_mass, turned[j][LANES - 2 : LANES - 1])
        )
        edge_rows[1].append(turned[j][LANES - 1 :])
        edge_rows[2].append(turned[j][0:1])
        edge_rows[3].append(jnp.where(lane_row >= 2 * levels, west_mass, turned[j][1:2]))
    edge_ref[...] = jnp.concatenate([row for group in edge_rows for row in group], axis=0)

    lane_level = lane_iota((levels, LANES))

    def partly_advected(t, near, beyond, sign):
        here = tr_ref[pl.ds(t * levels * rows + near, levels, stride=rows), :]
        other = tr_ref[pl.ds(t * levels * rows + beyond, levels, stride=rows), :]
        ahead = jnp.where(lane_level == LANES - 1, 0.0, pltpu.roll(here, LANES - 1, 1))
        flux = upwind(east_row(near), here, ahead)
        zonal = flux - jnp.where(lane_level == 0, 0.0, pltpu.roll(flux, 1, 1))
        if sign > 0:
            merid = upwind(north_row(near), here, other)
        else:
            merid = -upwind(north_row(beyond), other, here)
        return here, here - mass_row(near) * (zonal + merid)

    wind = north_row(last)
    ahead_wind = jnp.maximum(wind, 0.0)
    to_north, to_south = [], []
    for t in range(2):
        here, new = partly_advected(t, last, last - 1, -1)
        to_north += [ahead_wind * here, ahead_wind * new]
        to_south += partly_advected(t, 0, 1, 1)
    to_north.append(jnp.where(wind < 0.0, wind, ahead_wind * mass_row(last)))
    to_south.append(mass_row(0))
    even = lax.rem(lax.axis_index("lat"), 2) == 0
    for index, (north, south) in enumerate(zip(to_north, to_south)):
        here = slice(index * levels, (index + 1) * levels)
        even_ref[here] = jnp.where(even, north, south)
        odd_ref[here] = jnp.where(even, south, north)


def neighbour_blocks(lat_count, lon_count):
    lat, lon = lax.axis_index("lat"), lax.axis_index("lon")
    west, east = lax.rem(lon + lon_count - 1, lon_count), lax.rem(lon + 1, lon_count)
    south, north = jnp.maximum(lat - 1, 0), jnp.minimum(lat + 1, lat_count - 1)
    return [at * lon_count + index for at in (south, north) for index in (west, lon, east)]


def from_side(lat, south, even_round, odd_round, here):
    even = lax.rem(lat, 2) == 0
    if south:
        return jnp.where(even, odd_round[here], even_round[here])
    return jnp.where(even, even_round[here], odd_round[here])


def source_term(shear):
    return 2.0 * shear / (0.05 + shear)


def select_kernel(
    levels, rows, devices, recv_ref, owner_ref, rank_ref, asked_ref, shear_ref,
    side_ref, even_ref, odd_ref, mine_ref, lane_ref, group_ref, middle_ref,
):
    half = levels // 2
    cols = rows * LANES
    slot_total = (mine_ref.shape[1] - cols) // 2
    spans = slot_total // LANES
    row_index = lax.broadcasted_iota(jnp.int32, (half, 1), 0)
    shared = row_index == half - 1
    counts = jnp.where(shared, half_levels(1.0, 0.0), 1.0)

    asked = asked_ref[...]
    span = jnp.maximum(asked >> 7, 0)
    start = jnp.take_along_axis(recv_ref[:, 3 * half - 1, :], span + 3 * levels, axis=1)
    start = start.astype(jnp.int32)
    place = start + (asked & (LANES - 1))
    lane = place & (LANES - 1)
    group = jnp.where(asked < 0, -1, place >> 7)
    middle = jnp.zeros((devices, LANES), jnp.float32)
    for index in range(rows // 2):
        held = recv_ref[:, half * (index + 4) - 1, :]
        wanted = half_levels(index, index + rows // 2)
        middle = jnp.where(group == wanted, jnp.take_along_axis(held, lane, axis=1), middle)
    lane_ref[...] = lane
    group_ref[...] = group
    middle_ref[...] = middle

    def gather(source, found):
        spot = jnp.broadcast_to(lane_ref[pl.ds(source, 1), :], (half, LANES))
        kind = group_ref[pl.ds(source, 1), :]
        value = jnp.zeros((half, LANES), jnp.float32)
        for index in range(rows):
            held = recv_ref[source, half * (index + 1) : half * (index + 2), :]
            value = jnp.where(kind == index, jnp.take_along_axis(held, spot, axis=1), value)
        value = jnp.where(shared, middle_ref[pl.ds(source, 1), :], value)
        return tuple(
            jnp.where(
                owner_ref[j : j + 1, :] == source,
                jnp.take_along_axis(
                    value, jnp.broadcast_to(rank_ref[j : j + 1, :], (half, LANES)), axis=1
                ),
                found[j],
            )
            for j in range(rows)
        )

    found = fold(devices, gather, (jnp.zeros((half, LANES), jnp.float32),) * rows)
    for j in range(rows):
        here = slice(j * LANES, (j + 1) * LANES)
        mine_ref[:, here] = 0.5 * found[j] + counts * source_term(shear_ref[:, here])

    bottom = lax.broadcasted_iota(jnp.int32, (half, LANES), 0) == half - 1
    first_half = lane_iota((1, LANES)) < LANES // 2

    def arrived(source):
        slots = recv_ref[source, half - 1 : half, :]
        slots = jnp.where(first_half, pltpu.roll(slots, LANES // 2, 1), slots).astype(jnp.int32)
        shears = recv_ref[source, 0:half, :]
        lower = jnp.where(first_half, shears, 0.0)
        upper = jnp.where(jnp.logical_or(first_half, bottom), 0.0, shears)
        return slots, jnp.concatenate([lower, upper], axis=0)

    def place_columns(slots, values):
        split = split3(values)
        masked = [only_where(split, slots >> 7, index) for index in range(spans)]
        hot = hot_matrix(slots & (LANES - 1), LANES)
        placed = pick_columns(jnp.concatenate(masked, axis=0), hot, levels)
        return jnp.concatenate(
            [value[:half] for value in placed] + [value[half:] for value in placed], axis=1
        )

    if devices <= 8:
        slots, values = zip(*(arrived(source) for source in range(devices)))
        mine_ref[:, cols:] = place_columns(
            jnp.concatenate(slots, axis=1), jnp.concatenate(values, axis=1)
        )
    else:
        mine_ref[:, cols:] = lax.fori_loop(
            0,
            devices,
            lambda source, total: total + place_columns(*arrived(source)),
            jnp.zeros((half, 2 * slot_total), jnp.float32),
        )


def advect_kernel(
    levels, rows, lat_count, lon_count, tr_ref, wind_ref, mass_ref, even_ref, odd_ref, recv_ref,
    own_ref, west_ref, east_ref, out_ref,
):
    lev, two = levels, 2 * levels
    lat = lax.axis_index("lat")
    first, final = lat == 0, lat == lat_count - 1
    lane_row = lane_iota((1, LANES))

    def edge(ref, group):
        return ref[group * rows : (group + 1) * rows, :]

    blocks = neighbour_blocks(lat_count, lon_count)
    tracers, winds = (
        jnp.concatenate([recv_ref[block, row : row + 1, :] for block in blocks], axis=0)
        for row in (lev - 1, 3 * (lev // 2) - 1)
    )
    in_first = lane_iota((len(blocks), LANES)) < two
    last_cells = jnp.where(in_first, tracers, pltpu.roll(winds, two, 1))
    first_cells = jnp.where(in_first, pltpu.roll(tracers, two, 1), pltpu.roll(winds, lev, 1))

    def from_south(here):
        return from_side(lat, True, even_ref, odd_ref, here)

    def from_north(here):
        return from_side(lat, False, even_ref, odd_ref, here)

    def east_of(row):
        return jnp.where(lane_row < lev, pltpu.roll(row, 2 * lev, 1), pltpu.roll(row, 3 * lev, 1))

    def north_of(row):
        return jnp.where(lane_row < lev, pltpu.roll(row, lev, 1), pltpu.roll(row, 2 * lev, 1))

    def beside(column, west_east, west_value, here_east, east_value, mass):
        fluxes = upwind(north_of(column[: rows + 1]), column[: rows + 1], column[1:])
        index = lax.broadcasted_iota(jnp.int32, (rows + 1, LANES), 0)
        closed = ((index == 0) & first) | ((index == rows) & final)
        fluxes = jnp.where(closed, 0.0, fluxes)
        here = column[1 : rows + 1]
        zonal = upwind(here_east, here, east_value) - upwind(west_east, west_value, here)
        return here - mass * (zonal + fluxes[1:] - fluxes[:-1])

    far_west, far_east = edge(west_ref, 0), edge(east_ref, 3)
    own_first, own_last = edge(own_ref, 2), edge(own_ref, 1)
    west_mid, east_mid = edge(west_ref, 1), edge(east_ref, 2)
    south_west, south_east = last_cells[0:1], first_cells[2:3]
    north_west, north_east = last_cells[3:4], first_cells[5:6]
    west_new = beside(
        jnp.concatenate([south_west, west_mid, north_west], axis=0),
        east_of(far_west), far_west, east_of(west_mid), own_first, north_of(far_west),
    )
    east_new = beside(
        jnp.concatenate([south_east, east_mid, north_east], axis=0),
        east_of(own_last), own_last, east_of(east_mid), far_east, east_of(far_east),
    )

    def end_fluxes(index, west_cell, east_cell):
        own_end, own_start = last_cells[index : index + 1], first_cells[index : index + 1]
        return [
            upwind(east_of(west_cell), west_cell, own_start),
            jnp.minimum(east_of(own_end), 0.0) * east_cell,
        ]

    ends = end_fluxes(1, south_west, south_east) + end_fluxes(4, north_west, north_east)
    used = [west_mid, east_mid, west_new, east_new] + ends
    filler = jnp.zeros((LANES - 4 * rows - 4, LANES), jnp.float32)
    turned = jnp.transpose(jnp.concatenate(used + [filler], axis=0))

    def column(index, start, size):
        return jnp.broadcast_to(turned[start : start + size, index : index + 1], (size, LANES))

    def put(value, lane, index, start):
        return jnp.where(lane_row == lane, column(index, start, lev), value)

    def low(index):
        return from_south(slice(index * lev, (index + 1) * lev))

    def high(index):
        return from_north(slice(index * lev, (index + 1) * lev))

    east_wind = [wind_ref[pl.ds(j, lev, stride=rows), :] for j in range(rows)]
    north_wind = [wind_ref[pl.ds(lev * rows + j, lev, stride=rows), :] for j in range(rows)]
    mass = [mass_ref[pl.ds(j, lev, stride=rows), :] for j in range(rows)]
    west_wind = [put(pltpu.roll(east_wind[j], 1, 1), 0, j, two) for j in range(rows)]
    low_wind, low_share = jnp.minimum(low(4), 0.0), jnp.maximum(low(4), 0.0)
    high_mass = high(4)

    def substep(field, west_index, east_index, start, low_flux, high_flux):
        fluxes = [jnp.where(first, 0.0, low_flux)]
        for j in range(rows - 1):
            fluxes.append(upwind(north_wind[j], field[j], field[j + 1]))
        fluxes.append(jnp.where(final, 0.0, high_flux))
        result = []
        for j in range(rows):
            here = field[j]
            ahead = put(pltpu.roll(here, LANES - 1, 1), LANES - 1, east_index + j, start)
            behind = put(pltpu.roll(here, 1, 1), 0, west_index + j, start)
            zonal = upwind(east_wind[j], here, ahead) - upwind(west_wind[j], behind, here)
            result.append(here - mass[j] * (zonal + fluxes[j + 1] - fluxes[j]))
        return result

    for t in range(2):
        start = t * lev

        def left_out(index):
            zero = jnp.zeros((lev, LANES), jnp.float32)
            return put(put(zero, 0, index, start) * -1.0, LANES - 1, index + 1, start)

        field = [tr_ref[pl.ds(t * lev * rows + j, lev, stride=rows), :] for j in range(rows)]
        low_flux = low(2 * t) + low_wind * field[0]
        high_flux = upwind(north_wind[rows - 1], field[rows - 1], high(2 * t))
        once = substep(field, 0, rows, start, low_flux, high_flux)
        low_new = low(2 * t + 1) - low_share * (low_flux + left_out(4 * rows))
        high_new = high(2 * t + 1) - high_mass * (left_out(4 * rows + 2) - high_flux)
        twice = substep(
            once, 2 * rows, 3 * rows, start,
            low_new + low_wind * once[0],
            upwind(north_wind[rows - 1], once[rows - 1], high_new),
        )
        for j in range(rows):
            out_ref[pl.ds(t * rows + j, lev, stride=2 * rows), :] = twice[j]


def solve_kernel(
    levels, rows, adv_ref, mine_ref, other_ref, old_ref, active_ref, out_hbm, diff_hbm,
    out_ref, diff_ref, kv_ref, sems,
):
    half = levels // 2
    cols = rows * LANES
    width = 2 * rows
    slot_total = old_ref.shape[1]
    active = active_ref[...] > 0.0
    shear = mine_ref[:, cols:] + other_ref[:, cols:]

    def update(start, size, shear):
        old = old_ref[start : start + size]
        new = 0.5 * old + source_term(shear)
        diff_ref[start : start + size] = jnp.where(active, new, old)

    update(0, half, shear[:, :slot_total])
    update(half, half - 1, shear[: half - 1, slot_total:])
    put_diff = pltpu.make_async_copy(diff_ref, diff_hbm, sems.at[0])
    put_diff.start()
    low = half_levels(mine_ref[:, :cols], other_ref[:, :cols])
    high = half_levels(other_ref[:, :cols], mine_ref[:, :cols])
    shared = low[half - 1 :] + high[half - 1 :]
    for j in range(rows):
        here = slice(j * LANES, (j + 1) * LANES)
        for t in range(2):
            at = t * rows + j
            kv_ref[pl.ds(at, half - 1, stride=width), :] = low[: half - 1, here]
            kv_ref[pl.ds((half - 1) * width + at, 1), :] = shared[:, here]
            kv_ref[pl.ds(half * width + at, half - 1, stride=width), :] = high[: half - 1, here]

    def face(level):
        return kv_ref[level * width : (level + 1) * width]

    def eliminate(order, outer_face, inner_face):
        ratios, sweeps = {}, {}
        last_level = None
        for level in order:
            rhs = adv_ref[level * width : (level + 1) * width]
            inner = inner_face(level)
            pivot = 1.0 + inner
            if last_level is not None:
                outer = outer_face(level)
                pivot = pivot + outer - outer * ratios[last_level]
                rhs = rhs + outer * sweeps[last_level]
            inverse = 1.0 / pivot
            ratios[level] = inner * inverse
            sweeps[level] = rhs * inverse
            last_level = level
        return ratios, sweeps

    down, down_sweep = eliminate(range(half), lambda k: face(k - 1), face)
    up, up_sweep = eliminate(range(levels - 1, half - 1, -1), face, lambda k: face(k - 1))

    def put(level, value):
        for t in range(2):
            out_ref[(t * levels + level) * rows : (t * levels + level + 1) * rows] = value[
                t * rows : (t + 1) * rows
            ]

    below = (down_sweep[half - 1] + down[half - 1] * up_sweep[half]) / (
        1.0 - down[half - 1] * up[half]
    )
    above = up_sweep[half] + up[half] * below
    put(half - 1, below)
    put(half, above)
    for step in range(1, half):
        below = down_sweep[half - 1 - step] + down[half - 1 - step] * below
        above = up_sweep[half + step] + up[half + step] * above
        put(half - 1 - step, below)
        put(half + step, above)
    put_out = pltpu.make_async_copy(out_ref, out_hbm, sems.at[1])
    put_out.start()
    put_diff.wait()
    put_out.wait()


def call(kernel, outs, in_specs, out_specs, scratch=(), aliases=None):
    return pl.pallas_call(
        kernel,
        out_shape=[
            jax.ShapeDtypeStruct(out, jnp.float32) if isinstance(out, tuple) else out
            for out in outs
        ],
        in_specs=in_specs,
        out_specs=out_specs,
        scratch_shapes=list(scratch),
        input_output_aliases=aliases or {},
        compiler_params=pltpu.CompilerParams(vmem_limit_bytes=VMEM_LIMIT),
    )


def on_device(
    tracers, face_winds, inverse_mass, span_owner, span_slot, span_column_count, diffusivity
):
    own_count, levels, rows, cols = tracers.shape
    lat_count, lon_count = lax.axis_size("lat"), lax.axis_size("lon")
    devices = lat_count * lon_count
    half = levels // 2
    slot_total = diffusivity.shape[1]
    block_rows = half * (1 + rows)
    vmem = pl.BlockSpec(memory_space=pltpu.VMEM)
    hbm = pl.BlockSpec(memory_space=pltpu.HBM)

    tr = tracers.reshape(own_count * levels * rows, cols)
    winds = face_winds.reshape(2 * levels * rows, cols)
    mass = inverse_mass.reshape(levels * rows, cols)

    outs = [
        (devices, block_rows, LANES),
        (half, rows * LANES),
        (1, slot_total),
        jax.ShapeDtypeStruct((rows, LANES), jnp.int32),
        jax.ShapeDtypeStruct((rows, LANES), jnp.int32),
        jax.ShapeDtypeStruct((rows, LANES), jnp.int32),
        diffusivity.shape,
        tr.shape,
        winds.shape,
        mass.shape,
    ]
    send, shear, active, rank, owner, slot, old, tr, winds, mass = call(
        functools.partial(pack_kernel, levels, rows, devices, lon_count),
        outs,
        [hbm] * 7,
        [hbm] + [vmem] * (len(outs) - 1),
        [
            pltpu.SMEM(span_column_count.shape, jnp.int32),
            pltpu.VMEM((devices, block_rows, LANES), jnp.float32),
            pltpu.SemaphoreType.DMA((10,)),
        ],
    )(
        *(
            pltpu.with_memory_space_constraint(value, pltpu.HBM)
            for value in (tr, winds, mass, span_owner, span_slot, diffusivity, span_column_count)
        )
    )
    recv = lax.all_to_all(send, ("lat", "lon"), split_axis=0, concat_axis=0, tiled=True)
    to_even, to_odd, edges, asked = call(
        functools.partial(halo_kernel, levels, rows, devices),
        [
            (5 * levels, LANES),
            (5 * levels, LANES),
            (4 * rows, LANES),
            jax.ShapeDtypeStruct((devices, LANES), jnp.int32),
        ],
        [vmem] * 6,
        [vmem] * 4,
    )(tr, winds, mass, owner, slot, rank)
    from_lat = []
    for first, values in enumerate((to_even, to_odd)):
        pairs = [(i, i + 1) for i in range(first, lat_count - 1, 2)]
        from_lat.append(lax.ppermute(values, "lat", pairs + [(b, a) for a, b in pairs]))
    to_east = [(i, (i + 1) % lon_count) for i in range(lon_count)]
    to_west = [(target, source) for source, target in to_east]
    from_west = lax.ppermute(edges, "lon", to_east)
    from_east = from_west if lon_count == 2 else lax.ppermute(edges, "lon", to_west)
    (mine,) = call(
        functools.partial(select_kernel, levels, rows, devices),
        [(half, rows * LANES + 2 * slot_total)],
        [vmem] * 5 + [pl.BlockSpec(memory_space=pl.ANY)] * 3,
        [vmem],
        [
            pltpu.VMEM((devices, LANES), jnp.int32),
            pltpu.VMEM((devices, LANES), jnp.int32),
            pltpu.VMEM((devices, LANES), jnp.float32),
        ],
    )(recv, owner, rank, asked, shear, from_west, *from_lat)
    other = lax.ppermute(mine, "lev", [(0, 1), (1, 0)])
    (advected,) = call(
        functools.partial(advect_kernel, levels, rows, lat_count, lon_count),
        [(levels * own_count * rows, LANES)],
        [vmem] * 9,
        [vmem],
    )(tr, winds, mass, *from_lat, recv, edges, from_west, from_east)
    out, diff_out = call(
        functools.partial(solve_kernel, levels, rows),
        [(own_count * levels * rows, cols), (levels - 1, slot_total)],
        [vmem] * 5,
        [hbm] * 2,
        [
            pltpu.VMEM((own_count * levels * rows, cols), jnp.float32),
            pltpu.VMEM((levels - 1, slot_total), jnp.float32),
            pltpu.VMEM((levels * 2 * rows, LANES), jnp.float32),
            pltpu.SemaphoreType.DMA((2,)),
        ],
    )(advected, mine, other, old, active)
    return out.reshape(own_count, levels, rows, cols), diff_out


def solution(mesh):
    placed = (
        P("lev", "ens", "lat", "lon"),
        P(None, "ens", "lat", "lon"),
        P("ens", "lat", "lon"),
        P("lat", "lon"),
        P("lat", "lon"),
        P(("lat", "lon")),
        P("ens", ("lat", "lon")),
    )
    return jax.shard_map(
        on_device,
        mesh=mesh,
        in_specs=placed,
        out_specs=(P("lev", "ens", "lat", "lon"), P("ens", ("lat", "lon"))),
        check_vma=False,
    )
```

```python
import functools

import jax
import jax.numpy as jnp
from jax import lax
from jax.experimental import pallas as pl
from jax.experimental.pallas import tpu as pltpu
from jax.sharding import PartitionSpec as P

LANES = 128
ORDERS = {8: (4, 6, 1, 0, 7, 5, 2, 3)}
VMEM_LIMIT = 48 * 1024 * 1024
NT = (((1,), (1,)), ((), ()))


def device_of(devices, block):
    return ORDERS[devices][block] if devices in ORDERS else block


def block_of(devices, device):
    if devices not in ORDERS:
        return device
    return sum(jnp.where(device == held, block, 0) for block, held in enumerate(ORDERS[devices]))


def lane_iota(shape):
    return lax.broadcasted_iota(jnp.int32, shape, len(shape) - 1)


def split3(values):
    top = values.astype(jnp.bfloat16)
    rest = values - top.astype(jnp.float32)
    mid = rest.astype(jnp.bfloat16)
    low = (rest - mid.astype(jnp.float32)).astype(jnp.bfloat16)
    return jnp.concatenate([top, mid, low], axis=0)


def hot_matrix(row_of, size):
    index = lax.broadcasted_iota(jnp.int32, (size, row_of.shape[-1]), 0)
    return jnp.where(index == row_of, 1.0, 0.0).astype(jnp.bfloat16)


def pick_columns(masked, hot, rows):
    out = lax.dot_general(masked, hot, NT, preferred_element_type=jnp.float32)
    return [
        out[at : at + rows] + out[at + rows : at + 2 * rows] + out[at + 2 * rows : at + 3 * rows]
        for at in range(0, masked.shape[0], 3 * rows)
    ]


def fold(count, body, start):
    if count > 8:
        return lax.fori_loop(0, count, body, start)
    for index in range(count):
        start = body(index, start)
    return start


def only_where(split, key, wanted):
    return split * jnp.where(key == wanted, 1.0, 0.0).astype(jnp.bfloat16)


def loop_over(count, body):
    if count <= 8:
        for index in range(count):
            body(index)
    else:
        pl.loop(0, count)(body)


def upwind(wind, here, ahead):
    return jnp.maximum(wind, 0.0) * here + jnp.minimum(wind, 0.0) * ahead


def half_levels(first, second):
    return jnp.where(lax.axis_index("lev") == 0, first, second)


def own_faces(values):
    middle = values.shape[0] // 2
    second = jnp.concatenate([values[middle + 1 :], values[middle : middle + 1]], axis=0)
    return half_levels(values[: middle + 1], second)


def turn(levels, rows, tr_ref, wind_ref, j):
    fields = [
        tr_ref[pl.ds(j, 2 * levels, stride=rows), :],
        wind_ref[pl.ds(j, levels, stride=rows), :],
        wind_ref[pl.ds(levels * rows + j, levels, stride=rows), :],
    ]
    return jnp.transpose(jnp.concatenate(fields, axis=0))


def pack_kernel(
    levels, rows, devices, lon_count,
    tr_hbm, wind_hbm, mass_hbm, owner_hbm, slot_hbm, diff_hbm, count_hbm,
    send_hbm, shear_ref, active_ref, rank_ref, owner_ref, slot_ref, diff_ref, tr_ref, wind_ref, mass_ref,
    count_ref, send_ref, sems,
):
    half = levels // 2
    spans = diff_ref.shape[1] // LANES
    last = rows - 1
    lane_half = lane_iota((half, LANES))
    lane_row = lane_iota((1, LANES))
    bottom = lax.broadcasted_iota(jnp.int32, (half, LANES), 0) == half - 1
    pairs = [
        (owner_hbm, owner_ref), (slot_hbm, slot_ref), (wind_hbm, wind_ref), (count_hbm, count_ref),
        (diff_hbm, diff_ref), (tr_hbm, tr_ref), (mass_hbm, mass_ref),
    ]
    copies = [
        pltpu.make_async_copy(source, target, sems.at[index])
        for index, (source, target) in enumerate(pairs)
    ]
    for copy in copies:
        copy.start()

    def put(start, size, sem):
        copy = pltpu.make_async_copy(
            send_ref.at[:, pl.ds(start, size)], send_hbm.at[:, pl.ds(start, size)], sems.at[sem]
        )
        copy.start()
        return copy

    copies[0].wait()
    owner_index = lax.broadcasted_iota(jnp.int32, (devices, LANES), 0)
    owned = [owner_index == owner_ref[j : j + 1, :] for j in range(rows)]
    upto = lax.broadcasted_iota(jnp.int32, (LANES, LANES), 0) <= lane_iota((LANES, LANES))
    counted = lax.dot_general(
        jnp.concatenate([jnp.where(hit, 1.0, 0.0) for hit in owned], axis=0).astype(jnp.bfloat16),
        jnp.where(upto, 1.0, 0.0).astype(jnp.bfloat16),
        (((1,), (0,)), ((), ())),
        preferred_element_type=jnp.float32,
    )
    before = jnp.full((devices, 1), -1.0, jnp.float32)
    ranks = []
    for j in range(rows):
        count = counted[j * devices : (j + 1) * devices]
        rank = jnp.sum(jnp.where(owned[j], count + before, 0.0), axis=0, keepdims=True)
        ranks.append(rank.astype(jnp.int32))
        rank_ref[j : j + 1, :] = ranks[j]
        before = before + count[:, LANES - 1 :]
    owner = jnp.concatenate([owner_ref[j : j + 1, :] for j in range(rows)] * 2, axis=1)

    part = LANES // 2
    place = jnp.concatenate(ranks, axis=1) - half_levels(0, part)
    inside = (place >= 0) & (place < part)
    hot = hot_matrix(
        jnp.concatenate([jnp.where(inside, place, -1), jnp.where(inside, place + part, -1)], axis=1),
        LANES,
    )
    for index in range(1, 6):
        copies[index].wait()
    lower, upper = [], []
    for j in range(rows):
        east = wind_ref[pl.ds(j, levels, stride=rows), :]
        north = wind_ref[pl.ds(levels * rows + j, levels, stride=rows), :]
        east_step = east[1:] - east[:-1]
        north_step = north[1:] - north[:-1]
        shear = east_step * east_step + north_step * north_step
        slot = slot_ref[j : j + 1, :].astype(jnp.float32) + 1.0
        lower.append(shear[:half])
        upper.append(jnp.concatenate([shear[half:], slot], axis=0))
        shear_ref[:, j * LANES : (j + 1) * LANES] = own_faces(shear)
    split = split3(jnp.concatenate(lower + upper, axis=1))

    diffs = own_faces(diff_ref[...])
    starts, start = [], 0
    for span in range(spans):
        starts.append(start)
        start = start + count_ref[span]
    packed = []
    for group in range(last):
        value = jnp.zeros((half, LANES), jnp.float32)
        for span in range(spans - 1):
            spot = lane_half + (group * LANES - starts[span])
            taken = jnp.take_along_axis(
                diffs[:, span * LANES : (span + 1) * LANES], spot & (LANES - 1), axis=1
            )
            value = jnp.where((spot >= 0) & (spot < count_ref[span]), taken, value)
        packed.append(value)
    packed.append(diffs[:, (spans - 1) * LANES :])
    start_row = jnp.zeros((1, LANES), jnp.float32)
    for span in range(spans):
        here = lax.convert_element_type(starts[span], jnp.float32)
        start_row = jnp.where(lane_row == 3 * levels + span, here, start_row)
        active_ref[:, span * LANES : (span + 1) * LANES] = jnp.where(
            lane_row < count_ref[span], 1.0, 0.0
        )
    chunks = packed[:2]
    for group in range(rows // 2):
        shared = half_levels(packed[group][half - 1 :], packed[group + rows // 2][half - 1 :])
        chunks.append(jnp.where(bottom, shared, packed[group + 2]))

    def store_late(dest):
        for group in range(2, rows):
            send_ref[dest, half * (group + 1) : half * (group + 2)] = chunks[group]

    loop_over(devices, store_late)
    puts = [put(3 * half, half * (rows - 2), len(pairs))]

    ends = []
    for j in (0, last):
        turned = turn(levels, rows, tr_ref, wind_ref, j)
        east_end, west_end = turned[LANES - 1 :], turned[0:1]
        tracers = jnp.where(lane_row < part, east_end, pltpu.roll(west_end, part, 1))
        winds = jnp.where(
            lane_row < part,
            pltpu.roll(east_end, part, 1),
            jnp.where(lane_row < 3 * levels, pltpu.roll(west_end, 3 * levels, 1), start_row),
        )
        ends.append(
            [jnp.where(bottom, row, chunk) for row, chunk in zip((tracers, winds), chunks)]
        )

    def store_early(dest):
        northward = device_of(devices, dest) // lon_count > lax.axis_index("lat")
        for group in range(2):
            send_ref[dest, half * (group + 1) : half * (group + 2)] = jnp.where(
                northward, ends[1][group], ends[0][group]
            )

    loop_over(devices, store_early)
    puts.append(put(half, 2 * half, len(pairs) + 1))
    unasked = jnp.where(bottom & (lane_half >= part), 1.0, 0.0)

    def fill(dest, grouped):
        send_ref[dest, 0:half] = grouped - unasked

    if devices <= 8:
        masked = [only_where(split, owner, device_of(devices, dest)) for dest in range(devices)]
        for dest, grouped in enumerate(pick_columns(jnp.concatenate(masked, axis=0), hot, half)):
            fill(dest, grouped)
    else:
        pl.loop(0, devices)(
            lambda dest: fill(
                dest, pick_columns(only_where(split, owner, device_of(devices, dest)), hot, half)[0]
            )
        )
    puts.append(put(0, half, len(pairs) + 2))
    copies[6].wait()
    for copy in puts:
        copy.wait()


def halo_kernel(
    levels, rows, devices, tr_ref, wind_ref, mass_ref, owner_ref, slot_ref, rank_ref,
    even_ref, odd_ref, edge_ref, asked_ref,
):
    last = rows - 1

    def flat(ref):
        return jnp.concatenate([ref[j : j + 1, :] for j in range(rows)], axis=1)

    owner, hot = flat(owner_ref), hot_matrix(flat(rank_ref), LANES)
    filler = jnp.zeros((7, rows * LANES), jnp.float32)
    split = split3(jnp.concatenate([flat(slot_ref).astype(jnp.float32) + 1.0, filler], axis=0))

    def ask(dest):
        (found,) = pick_columns(only_where(split, owner, device_of(devices, dest)), hot, 8)
        asked_ref[pl.ds(dest, 1), :] = found[0:1].astype(jnp.int32) - 1

    loop_over(devices, ask)
    lane_row = lane_iota((1, LANES))

    def east_row(j):
        return wind_ref[pl.ds(j, levels, stride=rows), :]

    def north_row(j):
        return wind_ref[pl.ds(levels * rows + j, levels, stride=rows), :]

    def mass_row(j):
        return mass_ref[pl.ds(j, levels, stride=rows), :]

    turned = [turn(levels, rows, tr_ref, wind_ref, j) for j in range(rows)]
    masses = jnp.transpose(jnp.concatenate([mass_row(j) for j in range(rows)], axis=0))
    edge_rows = [[], [], [], []]
    for j in range(rows):
        west_mass = pltpu.roll(masses[0:1], (2 * levels - j * levels) % LANES, 1)
        east_mass = pltpu.roll(masses[LANES - 1 :], (3 * levels - j * levels) % LANES, 1)
        edge_rows[0].append(
            jnp.where(lane_row >= 3 * levels, east_mass, turned[j][LANES - 2 : LANES - 1])
        )
        edge_rows[1].append(turned[j][LANES - 1 :])
        edge_rows[2].append(turned[j][0:1])
        edge_rows[3].append(jnp.where(lane_row >= 2 * levels, west_mass, turned[j][1:2]))
    edge_ref[...] = jnp.concatenate([row for group in edge_rows for row in group], axis=0)

    lane_level = lane_iota((levels, LANES))

    def partly_advected(t, near, beyond, sign):
        here = tr_ref[pl.ds(t * levels * rows + near, levels, stride=rows), :]
        other = tr_ref[pl.ds(t * levels * rows + beyond, levels, stride=rows), :]
        ahead = jnp.where(lane_level == LANES - 1, 0.0, pltpu.roll(here, LANES - 1, 1))
        flux = upwind(east_row(near), here, ahead)
        zonal = flux - jnp.where(lane_level == 0, 0.0, pltpu.roll(flux, 1, 1))
        if sign > 0:
            merid = upwind(north_row(near), here, other)
        else:
            merid = -upwind(north_row(beyond), other, here)
        return here, here - mass_row(near) * (zonal + merid)

    wind = north_row(last)
    ahead_wind = jnp.maximum(wind, 0.0)
    to_north, to_south = [], []
    for t in range(2):
        here, new = partly_advected(t, last, last - 1, -1)
        to_north += [ahead_wind * here, ahead_wind * new]
        to_south += partly_advected(t, 0, 1, 1)
    to_north.append(jnp.where(wind < 0.0, wind, ahead_wind * mass_row(last)))
    to_south.append(mass_row(0))
    even = lax.rem(lax.axis_index("lat"), 2) == 0
    for index, (north, south) in enumerate(zip(to_north, to_south)):
        here = slice(index * levels, (index + 1) * levels)
        even_ref[here] = jnp.where(even, north, south)
        odd_ref[here] = jnp.where(even, south, north)


def neighbour_blocks(lat_count, lon_count):
    lat, lon = lax.axis_index("lat"), lax.axis_index("lon")
    west, east = lax.rem(lon + lon_count - 1, lon_count), lax.rem(lon + 1, lon_count)
    south, north = jnp.maximum(lat - 1, 0), jnp.minimum(lat + 1, lat_count - 1)
    return [
        block_of(lat_count * lon_count, at * lon_count + index)
        for at in (south, north)
        for index in (west, lon, east)
    ]


def from_side(lat, south, even_round, odd_round, here):
    even = lax.rem(lat, 2) == 0
    if south:
        return jnp.where(even, odd_round[here], even_round[here])
    return jnp.where(even, even_round[here], odd_round[here])


def source_term(shear):
    return 2.0 * shear / (0.05 + shear)


def select_kernel(
    levels, rows, devices, recv_ref, owner_ref, rank_ref, asked_ref, shear_ref,
    side_ref, even_ref, odd_ref, mine_ref, lane_ref, group_ref, middle_ref,
):
    half = levels // 2
    cols = rows * LANES
    slot_total = (mine_ref.shape[1] - cols) // 2
    spans = slot_total // LANES
    row_index = lax.broadcasted_iota(jnp.int32, (half, 1), 0)
    shared = row_index == half - 1
    counts = jnp.where(shared, half_levels(1.0, 0.0), 1.0)

    asked = asked_ref[...]
    span = jnp.maximum(asked >> 7, 0)
    start = jnp.take_along_axis(recv_ref[:, 3 * half - 1, :], span + 3 * levels, axis=1)
    start = start.astype(jnp.int32)
    place = start + (asked & (LANES - 1))
    lane = place & (LANES - 1)
    group = jnp.where(asked < 0, -1, place >> 7)
    middle = jnp.zeros((devices, LANES), jnp.float32)
    for index in range(rows // 2):
        held = recv_ref[:, half * (index + 4) - 1, :]
        wanted = half_levels(index, index + rows // 2)
        middle = jnp.where(group == wanted, jnp.take_along_axis(held, lane, axis=1), middle)
    lane_ref[...] = lane
    group_ref[...] = group
    middle_ref[...] = middle

    def gather(source, found):
        spot = jnp.broadcast_to(lane_ref[pl.ds(source, 1), :], (half, LANES))
        kind = group_ref[pl.ds(source, 1), :]
        value = jnp.zeros((half, LANES), jnp.float32)
        for index in range(rows):
            held = recv_ref[source, half * (index + 1) : half * (index + 2), :]
            value = jnp.where(kind == index, jnp.take_along_axis(held, spot, axis=1), value)
        value = jnp.where(shared, middle_ref[pl.ds(source, 1), :], value)
        return tuple(
            jnp.where(
                owner_ref[j : j + 1, :] == device_of(devices, source),
                jnp.take_along_axis(
                    value, jnp.broadcast_to(rank_ref[j : j + 1, :], (half, LANES)), axis=1
                ),
                found[j],
            )
            for j in range(rows)
        )

    found = fold(devices, gather, (jnp.zeros((half, LANES), jnp.float32),) * rows)
    for j in range(rows):
        here = slice(j * LANES, (j + 1) * LANES)
        mine_ref[:, here] = 0.5 * found[j] + counts * source_term(shear_ref[:, here])

    bottom = lax.broadcasted_iota(jnp.int32, (half, LANES), 0) == half - 1
    first_half = lane_iota((1, LANES)) < LANES // 2

    def arrived(pair):
        left, right = (recv_ref[2 * pair + index, 0:half, :] for index in range(2))
        lower = jnp.where(first_half, left, pltpu.roll(right, LANES // 2, 1))
        upper = jnp.where(first_half, pltpu.roll(left, LANES // 2, 1), right)
        slots = upper[half - 1 :].astype(jnp.int32)
        return slots, jnp.concatenate([lower, jnp.where(bottom, 0.0, upper)], axis=0)

    def place_columns(slots, values):
        split = split3(values)
        masked = [only_where(split, slots >> 7, index) for index in range(spans)]
        hot = hot_matrix(slots & (LANES - 1), LANES)
        placed = pick_columns(jnp.concatenate(masked, axis=0), hot, levels)
        return jnp.concatenate(
            [value[:half] for value in placed] + [value[half:] for value in placed], axis=1
        )

    if devices <= 8:
        slots, values = zip(*(arrived(pair) for pair in range(devices // 2)))
        mine_ref[:, cols:] = place_columns(
            jnp.concatenate(slots, axis=1), jnp.concatenate(values, axis=1)
        )
    else:
        mine_ref[:, cols:] = lax.fori_loop(
            0,
            devices // 2,
            lambda pair, total: total + place_columns(*arrived(pair)),
            jnp.zeros((half, 2 * slot_total), jnp.float32),
        )


def advect_kernel(
    levels, rows, lat_count, lon_count, tr_ref, wind_ref, mass_ref, even_ref, odd_ref, recv_ref,
    own_ref, west_ref, east_ref, out_ref,
):
    lev, two = levels, 2 * levels
    lat = lax.axis_index("lat")
    first, final = lat == 0, lat == lat_count - 1
    lane_row = lane_iota((1, LANES))

    def edge(ref, group):
        return ref[group * rows : (group + 1) * rows, :]

    blocks = neighbour_blocks(lat_count, lon_count)
    tracers, winds = (
        jnp.concatenate([recv_ref[block, row : row + 1, :] for block in blocks], axis=0)
        for row in (lev - 1, 3 * (lev // 2) - 1)
    )
    in_first = lane_iota((len(blocks), LANES)) < two
    last_cells = jnp.where(in_first, tracers, pltpu.roll(winds, two, 1))
    first_cells = jnp.where(in_first, pltpu.roll(tracers, two, 1), pltpu.roll(winds, lev, 1))

    def from_south(here):
        return from_side(lat, True, even_ref, odd_ref, here)

    def from_north(here):
        return from_side(lat, False, even_ref, odd_ref, here)

    def east_of(row):
        return jnp.where(lane_row < lev, pltpu.roll(row, 2 * lev, 1), pltpu.roll(row, 3 * lev, 1))

    def north_of(row):
        return jnp.where(lane_row < lev, pltpu.roll(row, lev, 1), pltpu.roll(row, 2 * lev, 1))

    def beside(column, west_east, west_value, here_east, east_value, mass):
        fluxes = upwind(north_of(column[: rows + 1]), column[: rows + 1], column[1:])
        index = lax.broadcasted_iota(jnp.int32, (rows + 1, LANES), 0)
        closed = ((index == 0) & first) | ((index == rows) & final)
        fluxes = jnp.where(closed, 0.0, fluxes)
        here = column[1 : rows + 1]
        zonal = upwind(here_east, here, east_value) - upwind(west_east, west_value, here)
        return here - mass * (zonal + fluxes[1:] - fluxes[:-1])

    far_west, far_east = edge(west_ref, 0), edge(east_ref, 3)
    own_first, own_last = edge(own_ref, 2), edge(own_ref, 1)
    west_mid, east_mid = edge(west_ref, 1), edge(east_ref, 2)
    south_west, south_east = last_cells[0:1], first_cells[2:3]
    north_west, north_east = last_cells[3:4], first_cells[5:6]
    west_new = beside(
        jnp.concatenate([south_west, west_mid, north_west], axis=0),
        east_of(far_west), far_west, east_of(west_mid), own_first, north_of(far_west),
    )
    east_new = beside(
        jnp.concatenate([south_east, east_mid, north_east], axis=0),
        east_of(own_last), own_last, east_of(east_mid), far_east, east_of(far_east),
    )

    def end_fluxes(index, west_cell, east_cell):
        own_end, own_start = last_cells[index : index + 1], first_cells[index : index + 1]
        return [
            upwind(east_of(west_cell), west_cell, own_start),
            jnp.minimum(east_of(own_end), 0.0) * east_cell,
        ]

    ends = end_fluxes(1, south_west, south_east) + end_fluxes(4, north_west, north_east)
    used = [west_mid, east_mid, west_new, east_new] + ends
    filler = jnp.zeros((LANES - 4 * rows - 4, LANES), jnp.float32)
    turned = jnp.transpose(jnp.concatenate(used + [filler], axis=0))

    def column(index, start, size):
        return jnp.broadcast_to(turned[start : start + size, index : index + 1], (size, LANES))

    def put(value, lane, index, start):
        return jnp.where(lane_row == lane, column(index, start, lev), value)

    def low(index):
        return from_south(slice(index * lev, (index + 1) * lev))

    def high(index):
        return from_north(slice(index * lev, (index + 1) * lev))

    east_wind = [wind_ref[pl.ds(j, lev, stride=rows), :] for j in range(rows)]
    north_wind = [wind_ref[pl.ds(lev * rows + j, lev, stride=rows), :] for j in range(rows)]
    mass = [mass_ref[pl.ds(j, lev, stride=rows), :] for j in range(rows)]
    west_wind = [put(pltpu.roll(east_wind[j], 1, 1), 0, j, two) for j in range(rows)]
    low_wind, low_share = jnp.minimum(low(4), 0.0), jnp.maximum(low(4), 0.0)
    high_mass = high(4)

    def substep(field, west_index, east_index, start, low_flux, high_flux):
        fluxes = [jnp.where(first, 0.0, low_flux)]
        for j in range(rows - 1):
            fluxes.append(upwind(north_wind[j], field[j], field[j + 1]))
        fluxes.append(jnp.where(final, 0.0, high_flux))
        result = []
        for j in range(rows):
            here = field[j]
            ahead = put(pltpu.roll(here, LANES - 1, 1), LANES - 1, east_index + j, start)
            behind = put(pltpu.roll(here, 1, 1), 0, west_index + j, start)
            zonal = upwind(east_wind[j], here, ahead) - upwind(west_wind[j], behind, here)
            result.append(here - mass[j] * (zonal + fluxes[j + 1] - fluxes[j]))
        return result

    for t in range(2):
        start = t * lev

        def left_out(index):
            zero = jnp.zeros((lev, LANES), jnp.float32)
            return put(put(zero, 0, index, start) * -1.0, LANES - 1, index + 1, start)

        field = [tr_ref[pl.ds(t * lev * rows + j, lev, stride=rows), :] for j in range(rows)]
        low_flux = low(2 * t) + low_wind * field[0]
        high_flux = upwind(north_wind[rows - 1], field[rows - 1], high(2 * t))
        once = substep(field, 0, rows, start, low_flux, high_flux)
        low_new = low(2 * t + 1) - low_share * (low_flux + left_out(4 * rows))
        high_new = high(2 * t + 1) - high_mass * (left_out(4 * rows + 2) - high_flux)
        twice = substep(
            once, 2 * rows, 3 * rows, start,
            low_new + low_wind * once[0],
            upwind(north_wind[rows - 1], once[rows - 1], high_new),
        )
        for j in range(rows):
            out_ref[pl.ds(t * rows + j, lev, stride=2 * rows), :] = twice[j]


def solve_kernel(
    levels, rows, adv_ref, mine_ref, other_ref, old_ref, active_ref, out_hbm, diff_hbm,
    out_ref, diff_ref, kv_ref, sems,
):
    half = levels // 2
    cols = rows * LANES
    width = 2 * rows
    slot_total = old_ref.shape[1]
    active = active_ref[...] > 0.0
    shear = mine_ref[:, cols:] + other_ref[:, cols:]

    def update(start, size, shear):
        old = old_ref[start : start + size]
        new = 0.5 * old + source_term(shear)
        diff_ref[start : start + size] = jnp.where(active, new, old)

    update(0, half, shear[:, :slot_total])
    update(half, half - 1, shear[: half - 1, slot_total:])
    put_diff = pltpu.make_async_copy(diff_ref, diff_hbm, sems.at[0])
    put_diff.start()
    low = half_levels(mine_ref[:, :cols], other_ref[:, :cols])
    high = half_levels(other_ref[:, :cols], mine_ref[:, :cols])
    shared = low[half - 1 :] + high[half - 1 :]
    for j in range(rows):
        here = slice(j * LANES, (j + 1) * LANES)
        for t in range(2):
            at = t * rows + j
            kv_ref[pl.ds(at, half - 1, stride=width), :] = low[: half - 1, here]
            kv_ref[pl.ds((half - 1) * width + at, 1), :] = shared[:, here]
            kv_ref[pl.ds(half * width + at, half - 1, stride=width), :] = high[: half - 1, here]

    def face(level):
        return kv_ref[level * width : (level + 1) * width]

    def eliminate(order, outer_face, inner_face):
        ratios, sweeps = {}, {}
        last_level = None
        for level in order:
            rhs = adv_ref[level * width : (level + 1) * width]
            inner = inner_face(level)
            pivot = 1.0 + inner
            if last_level is not None:
                outer = outer_face(level)
                pivot = pivot + outer - outer * ratios[last_level]
                rhs = rhs + outer * sweeps[last_level]
            inverse = 1.0 / pivot
            ratios[level] = inner * inverse
            sweeps[level] = rhs * inverse
            last_level = level
        return ratios, sweeps

    down, down_sweep = eliminate(range(half), lambda k: face(k - 1), face)
    up, up_sweep = eliminate(range(levels - 1, half - 1, -1), face, lambda k: face(k - 1))

    def put(level, value):
        for t in range(2):
            out_ref[(t * levels + level) * rows : (t * levels + level + 1) * rows] = value[
                t * rows : (t + 1) * rows
            ]

    below = (down_sweep[half - 1] + down[half - 1] * up_sweep[half]) / (
        1.0 - down[half - 1] * up[half]
    )
    above = up_sweep[half] + up[half] * below
    put(half - 1, below)
    put(half, above)
    for step in range(1, half):
        below = down_sweep[half - 1 - step] + down[half - 1 - step] * below
        above = up_sweep[half + step] + up[half + step] * above
        put(half - 1 - step, below)
        put(half + step, above)
    put_out = pltpu.make_async_copy(out_ref, out_hbm, sems.at[1])
    put_out.start()
    put_diff.wait()
    put_out.wait()


def call(kernel, outs, in_specs, out_specs, scratch=(), aliases=None):
    return pl.pallas_call(
        kernel,
        out_shape=[
            jax.ShapeDtypeStruct(out, jnp.float32) if isinstance(out, tuple) else out
            for out in outs
        ],
        in_specs=in_specs,
        out_specs=out_specs,
        scratch_shapes=list(scratch),
        input_output_aliases=aliases or {},
        compiler_params=pltpu.CompilerParams(vmem_limit_bytes=VMEM_LIMIT),
    )


def on_device(
    tracers, face_winds, inverse_mass, span_owner, span_slot, span_column_count, diffusivity
):
    own_count, levels, rows, cols = tracers.shape
    lat_count, lon_count = lax.axis_size("lat"), lax.axis_size("lon")
    devices = lat_count * lon_count
    half = levels // 2
    slot_total = diffusivity.shape[1]
    block_rows = half * (1 + rows)
    vmem = pl.BlockSpec(memory_space=pltpu.VMEM)
    hbm = pl.BlockSpec(memory_space=pltpu.HBM)

    tr = tracers.reshape(own_count * levels * rows, cols)
    winds = face_winds.reshape(2 * levels * rows, cols)
    mass = inverse_mass.reshape(levels * rows, cols)

    outs = [
        (devices, block_rows, LANES),
        (half, rows * LANES),
        (1, slot_total),
        jax.ShapeDtypeStruct((rows, LANES), jnp.int32),
        jax.ShapeDtypeStruct((rows, LANES), jnp.int32),
        jax.ShapeDtypeStruct((rows, LANES), jnp.int32),
        diffusivity.shape,
        tr.shape,
        winds.shape,
        mass.shape,
    ]
    send, shear, active, rank, owner, slot, old, tr, winds, mass = call(
        functools.partial(pack_kernel, levels, rows, devices, lon_count),
        outs,
        [hbm] * 7,
        [hbm] + [vmem] * (len(outs) - 1),
        [
            pltpu.SMEM(span_column_count.shape, jnp.int32),
            pltpu.VMEM((devices, block_rows, LANES), jnp.float32),
            pltpu.SemaphoreType.DMA((10,)),
        ],
    )(
        *(
            pltpu.with_memory_space_constraint(value, pltpu.HBM)
            for value in (tr, winds, mass, span_owner, span_slot, diffusivity, span_column_count)
        )
    )
    recv = lax.all_to_all(
        send,
        ("lat", "lon"),
        split_axis=0,
        concat_axis=0,
        tiled=True,
        axis_index_groups=[list(ORDERS[devices])] if devices in ORDERS else None,
    )
    to_even, to_odd, edges, asked = call(
        functools.partial(halo_kernel, levels, rows, devices),
        [
            (5 * levels, LANES),
            (5 * levels, LANES),
            (4 * rows, LANES),
            jax.ShapeDtypeStruct((devices, LANES), jnp.int32),
        ],
        [vmem] * 6,
        [vmem] * 4,
    )(tr, winds, mass, owner, slot, rank)
    from_lat = []
    for first, values in enumerate((to_even, to_odd)):
        pairs = [(i, i + 1) for i in range(first, lat_count - 1, 2)]
        from_lat.append(lax.ppermute(values, "lat", pairs + [(b, a) for a, b in pairs]))
    to_east = [(i, (i + 1) % lon_count) for i in range(lon_count)]
    to_west = [(target, source) for source, target in to_east]
    from_west = lax.ppermute(edges, "lon", to_east)
    from_east = from_west if lon_count == 2 else lax.ppermute(edges, "lon", to_west)
    (mine,) = call(
        functools.partial(select_kernel, levels, rows, devices),
        [(half, rows * LANES + 2 * slot_total)],
        [vmem] * 5 + [pl.BlockSpec(memory_space=pl.ANY)] * 3,
        [vmem],
        [
            pltpu.VMEM((devices, LANES), jnp.int32),
            pltpu.VMEM((devices, LANES), jnp.int32),
            pltpu.VMEM((devices, LANES), jnp.float32),
        ],
    )(recv, owner, rank, asked, shear, from_west, *from_lat)
    other = lax.ppermute(mine, "lev", [(0, 1), (1, 0)])
    (advected,) = call(
        functools.partial(advect_kernel, levels, rows, lat_count, lon_count),
        [(levels * own_count * rows, LANES)],
        [vmem] * 9,
        [vmem],
    )(tr, winds, mass, *from_lat, recv, edges, from_west, from_east)
    out, diff_out = call(
        functools.partial(solve_kernel, levels, rows),
        [(own_count * levels * rows, cols), (levels - 1, slot_total)],
        [vmem] * 5,
        [hbm] * 2,
        [
            pltpu.VMEM((own_count * levels * rows, cols), jnp.float32),
            pltpu.VMEM((levels - 1, slot_total), jnp.float32),
            pltpu.VMEM((levels * 2 * rows, LANES), jnp.float32),
            pltpu.SemaphoreType.DMA((2,)),
        ],
    )(advected, mine, other, old, active)
    return out.reshape(own_count, levels, rows, cols), diff_out


def solution(mesh):
    placed = (
        P("lev", "ens", "lat", "lon"),
        P(None, "ens", "lat", "lon"),
        P("ens", "lat", "lon"),
        P("lat", "lon"),
        P("lat", "lon"),
        P(("lat", "lon")),
        P("ens", ("lat", "lon")),
    )
    return jax.shard_map(
        on_device,
        mesh=mesh,
        in_specs=placed,
        out_specs=(P("lev", "ens", "lat", "lon"), P("ens", ("lat", "lon"))),
        check_vma=False,
    )
```

```python
import functools

import jax
import jax.numpy as jnp
from jax import lax
from jax.experimental import pallas as pl
from jax.experimental.pallas import tpu as pltpu
from jax.sharding import PartitionSpec as P

LANES = 128
ORDERS = {8: (4, 6, 1, 0, 7, 5, 2, 3)}
VMEM_LIMIT = 48 * 1024 * 1024
NT = (((1,), (1,)), ((), ()))


def device_of(devices, block):
    return ORDERS[devices][block] if devices in ORDERS else block


def block_of(devices, device):
    if devices not in ORDERS:
        return device
    return sum(jnp.where(device == held, block, 0) for block, held in enumerate(ORDERS[devices]))


def lane_iota(shape):
    return lax.broadcasted_iota(jnp.int32, shape, len(shape) - 1)


def split2(values):
    top = values.astype(jnp.bfloat16)
    rest = (values - top.astype(jnp.float32)).astype(jnp.bfloat16)
    return jnp.concatenate([top, rest], axis=0)


def hot_matrix(row_of, size):
    index = lax.broadcasted_iota(jnp.int32, (size, row_of.shape[-1]), 0)
    return jnp.where(index == row_of, 1.0, 0.0).astype(jnp.bfloat16)


def pick_columns(masked, hot, rows):
    out = lax.dot_general(masked, hot, NT, preferred_element_type=jnp.float32)
    return [
        out[at : at + rows] + out[at + rows : at + 2 * rows]
        for at in range(0, masked.shape[0], 2 * rows)
    ]


def fold(count, body, start):
    if count > 8:
        return lax.fori_loop(0, count, body, start)
    for index in range(count):
        start = body(index, start)
    return start


def only_where(split, key, wanted):
    return split * jnp.where(key == wanted, 1.0, 0.0).astype(jnp.bfloat16)


def loop_over(count, body):
    if count <= 8:
        for index in range(count):
            body(index)
    else:
        pl.loop(0, count)(body)


def upwind(wind, here, ahead):
    return jnp.maximum(wind, 0.0) * here + jnp.minimum(wind, 0.0) * ahead


def half_levels(first, second):
    return jnp.where(lax.axis_index("lev") == 0, first, second)


def own_faces(values):
    middle = values.shape[0] // 2
    second = jnp.concatenate([values[middle + 1 :], values[middle : middle + 1]], axis=0)
    return half_levels(values[: middle + 1], second)


def turn(levels, rows, tr_ref, wind_ref, j):
    fields = [
        tr_ref[pl.ds(j, 2 * levels, stride=rows), :],
        wind_ref[pl.ds(j, levels, stride=rows), :],
        wind_ref[pl.ds(levels * rows + j, levels, stride=rows), :],
    ]
    return jnp.transpose(jnp.concatenate(fields, axis=0))


def pack_kernel(
    levels, rows, devices, lon_count,
    tr_hbm, wind_hbm, mass_hbm, owner_hbm, slot_hbm, diff_hbm, count_hbm,
    send_hbm, shear_ref, active_ref, rank_ref, owner_ref, slot_ref, diff_ref, tr_ref, wind_ref, mass_ref,
    count_ref, send_ref, sems,
):
    half = levels // 2
    spans = diff_ref.shape[1] // LANES
    last = rows - 1
    lane_half = lane_iota((half, LANES))
    lane_row = lane_iota((1, LANES))
    bottom = lax.broadcasted_iota(jnp.int32, (half, LANES), 0) == half - 1
    pairs = [
        (owner_hbm, owner_ref), (slot_hbm, slot_ref), (wind_hbm, wind_ref), (count_hbm, count_ref),
        (diff_hbm, diff_ref), (tr_hbm, tr_ref), (mass_hbm, mass_ref),
    ]
    copies = [
        pltpu.make_async_copy(source, target, sems.at[index])
        for index, (source, target) in enumerate(pairs)
    ]
    for copy in copies:
        copy.start()

    def put(start, size, sem):
        copy = pltpu.make_async_copy(
            send_ref.at[:, pl.ds(start, size)], send_hbm.at[:, pl.ds(start, size)], sems.at[sem]
        )
        copy.start()
        return copy

    copies[0].wait()
    owner_index = lax.broadcasted_iota(jnp.int32, (devices, LANES), 0)
    owned = [owner_index == owner_ref[j : j + 1, :] for j in range(rows)]
    upto = lax.broadcasted_iota(jnp.int32, (LANES, LANES), 0) <= lane_iota((LANES, LANES))
    counted = lax.dot_general(
        jnp.concatenate([jnp.where(hit, 1.0, 0.0) for hit in owned], axis=0).astype(jnp.bfloat16),
        jnp.where(upto, 1.0, 0.0).astype(jnp.bfloat16),
        (((1,), (0,)), ((), ())),
        preferred_element_type=jnp.float32,
    )
    before = jnp.full((devices, 1), -1.0, jnp.float32)
    ranks = []
    for j in range(rows):
        count = counted[j * devices : (j + 1) * devices]
        rank = jnp.sum(jnp.where(owned[j], count + before, 0.0), axis=0, keepdims=True)
        ranks.append(rank.astype(jnp.int32))
        rank_ref[j : j + 1, :] = ranks[j]
        before = before + count[:, LANES - 1 :]
    owner = jnp.concatenate([owner_ref[j : j + 1, :] for j in range(rows)] * 2, axis=1)

    part = LANES // 2
    place = jnp.concatenate(ranks, axis=1) - half_levels(0, part)
    inside = (place >= 0) & (place < part)
    hot = hot_matrix(
        jnp.concatenate([jnp.where(inside, place, -1), jnp.where(inside, place + part, -1)], axis=1),
        LANES,
    )
    for index in range(1, 6):
        copies[index].wait()
    lower, upper = [], []
    for j in range(rows):
        east = wind_ref[pl.ds(j, levels, stride=rows), :]
        north = wind_ref[pl.ds(levels * rows + j, levels, stride=rows), :]
        east_step = east[1:] - east[:-1]
        north_step = north[1:] - north[:-1]
        shear = east_step * east_step + north_step * north_step
        slot = slot_ref[j : j + 1, :].astype(jnp.float32) + 1.0
        lower.append(shear[:half])
        upper.append(jnp.concatenate([shear[half:], slot], axis=0))
        shear_ref[:, j * LANES : (j + 1) * LANES] = own_faces(shear)
    split = split2(jnp.concatenate(lower + upper, axis=1))

    diffs = own_faces(diff_ref[...])
    starts, start = [], 0
    for span in range(spans):
        starts.append(start)
        start = start + count_ref[span]
    packed = []
    for group in range(last):
        value = jnp.zeros((half, LANES), jnp.float32)
        for span in range(spans - 1):
            spot = lane_half + (group * LANES - starts[span])
            taken = jnp.take_along_axis(
                diffs[:, span * LANES : (span + 1) * LANES], spot & (LANES - 1), axis=1
            )
            value = jnp.where((spot >= 0) & (spot < count_ref[span]), taken, value)
        packed.append(value)
    packed.append(diffs[:, (spans - 1) * LANES :])
    start_row = jnp.zeros((1, LANES), jnp.float32)
    for span in range(spans):
        here = lax.convert_element_type(starts[span], jnp.float32)
        start_row = jnp.where(lane_row == 3 * levels + span, here, start_row)
        active_ref[:, span * LANES : (span + 1) * LANES] = jnp.where(
            lane_row < count_ref[span], 1.0, 0.0
        )
    chunks = packed[:2]
    for group in range(rows // 2):
        shared = half_levels(packed[group][half - 1 :], packed[group + rows // 2][half - 1 :])
        chunks.append(jnp.where(bottom, shared, packed[group + 2]))

    def store_late(dest):
        for group in range(2, rows):
            send_ref[dest, half * (group + 1) : half * (group + 2)] = chunks[group]

    loop_over(devices, store_late)
    puts = [put(3 * half, half * (rows - 2), len(pairs))]

    ends = []
    for j in (0, last):
        turned = turn(levels, rows, tr_ref, wind_ref, j)
        east_end, west_end = turned[LANES - 1 :], turned[0:1]
        tracers = jnp.where(lane_row < part, east_end, pltpu.roll(west_end, part, 1))
        winds = jnp.where(
            lane_row < part,
            pltpu.roll(east_end, part, 1),
            jnp.where(lane_row < 3 * levels, pltpu.roll(west_end, 3 * levels, 1), start_row),
        )
        ends.append(
            [jnp.where(bottom, row, chunk) for row, chunk in zip((tracers, winds), chunks)]
        )

    def store_early(dest):
        northward = device_of(devices, dest) // lon_count > lax.axis_index("lat")
        for group in range(2):
            send_ref[dest, half * (group + 1) : half * (group + 2)] = jnp.where(
                northward, ends[1][group], ends[0][group]
            )

    loop_over(devices, store_early)
    puts.append(put(half, 2 * half, len(pairs) + 1))
    unasked = jnp.where(bottom & (lane_half >= part), 1.0, 0.0)

    def fill(dest, grouped):
        send_ref[dest, 0:half] = grouped - unasked

    if devices <= 8:
        masked = [only_where(split, owner, device_of(devices, dest)) for dest in range(devices)]
        for dest, grouped in enumerate(pick_columns(jnp.concatenate(masked, axis=0), hot, half)):
            fill(dest, grouped)
    else:
        pl.loop(0, devices)(
            lambda dest: fill(
                dest, pick_columns(only_where(split, owner, device_of(devices, dest)), hot, half)[0]
            )
        )
    puts.append(put(0, half, len(pairs) + 2))
    copies[6].wait()
    for copy in puts:
        copy.wait()


def mass_rows(levels, rows, mass_ref, j):
    return mass_ref[pl.ds(j, levels, stride=rows), :]


def lat_kernel(levels, rows, tr_ref, wind_ref, mass_ref, even_ref, odd_ref):
    last = rows - 1

    def east_row(j):
        return wind_ref[pl.ds(j, levels, stride=rows), :]

    def north_row(j):
        return wind_ref[pl.ds(levels * rows + j, levels, stride=rows), :]

    def mass_row(j):
        return mass_rows(levels, rows, mass_ref, j)

    lane_level = lane_iota((levels, LANES))

    def partly_advected(t, near, beyond, sign):
        here = tr_ref[pl.ds(t * levels * rows + near, levels, stride=rows), :]
        other = tr_ref[pl.ds(t * levels * rows + beyond, levels, stride=rows), :]
        ahead = jnp.where(lane_level == LANES - 1, 0.0, pltpu.roll(here, LANES - 1, 1))
        flux = upwind(east_row(near), here, ahead)
        zonal = flux - jnp.where(lane_level == 0, 0.0, pltpu.roll(flux, 1, 1))
        if sign > 0:
            merid = upwind(north_row(near), here, other)
        else:
            merid = -upwind(north_row(beyond), other, here)
        return here, here - mass_row(near) * (zonal + merid)

    wind = north_row(last)
    ahead_wind = jnp.maximum(wind, 0.0)
    to_north, to_south = [], []
    for t in range(2):
        here, new = partly_advected(t, last, last - 1, -1)
        to_north += [ahead_wind * here, ahead_wind * new]
        to_south += partly_advected(t, 0, 1, 1)
    to_north.append(jnp.where(wind < 0.0, wind, ahead_wind * mass_row(last)))
    to_south.append(mass_row(0))
    even = lax.rem(lax.axis_index("lat"), 2) == 0
    for index, (north, south) in enumerate(zip(to_north, to_south)):
        here = slice(index * levels, (index + 1) * levels)
        even_ref[here] = jnp.where(even, north, south)
        odd_ref[here] = jnp.where(even, south, north)


def edge_kernel(
    levels, rows, devices, tr_ref, wind_ref, mass_ref, owner_ref, slot_ref, rank_ref,
    edge_ref, asked_ref,
):
    lane_row = lane_iota((1, LANES))

    def mass_row(j):
        return mass_rows(levels, rows, mass_ref, j)

    def flat(ref):
        return jnp.concatenate([ref[j : j + 1, :] for j in range(rows)], axis=1)

    owner, hot = flat(owner_ref), hot_matrix(flat(rank_ref), LANES)
    filler = jnp.zeros((7, rows * LANES), jnp.float32)
    split = split2(jnp.concatenate([flat(slot_ref).astype(jnp.float32) + 1.0, filler], axis=0))

    def ask(dest):
        (found,) = pick_columns(only_where(split, owner, device_of(devices, dest)), hot, 8)
        asked_ref[pl.ds(dest, 1), :] = found[0:1].astype(jnp.int32) - 1

    loop_over(devices, ask)
    turned = [turn(levels, rows, tr_ref, wind_ref, j) for j in range(rows)]
    masses = jnp.transpose(jnp.concatenate([mass_row(j) for j in range(rows)], axis=0))
    edge_rows = [[], [], [], []]
    for j in range(rows):
        west_mass = pltpu.roll(masses[0:1], (2 * levels - j * levels) % LANES, 1)
        east_mass = pltpu.roll(masses[LANES - 1 :], (3 * levels - j * levels) % LANES, 1)
        edge_rows[0].append(
            jnp.where(lane_row >= 3 * levels, east_mass, turned[j][LANES - 2 : LANES - 1])
        )
        edge_rows[1].append(turned[j][LANES - 1 :])
        edge_rows[2].append(turned[j][0:1])
        edge_rows[3].append(jnp.where(lane_row >= 2 * levels, west_mass, turned[j][1:2]))
    edge_ref[...] = jnp.concatenate([row for group in edge_rows for row in group], axis=0)


def neighbour_blocks(lat_count, lon_count):
    lat, lon = lax.axis_index("lat"), lax.axis_index("lon")
    west, east = lax.rem(lon + lon_count - 1, lon_count), lax.rem(lon + 1, lon_count)
    south, north = jnp.maximum(lat - 1, 0), jnp.minimum(lat + 1, lat_count - 1)
    return [
        block_of(lat_count * lon_count, at * lon_count + index)
        for at in (south, north)
        for index in (west, lon, east)
    ]


def from_side(lat, south, even_round, odd_round, here):
    even = lax.rem(lat, 2) == 0
    if south:
        return jnp.where(even, odd_round[here], even_round[here])
    return jnp.where(even, even_round[here], odd_round[here])


def source_term(shear):
    return 2.0 * shear / (0.05 + shear)


def select_kernel(
    levels, rows, devices, recv_ref, owner_ref, rank_ref, asked_ref, shear_ref,
    side_ref, even_ref, odd_ref, mine_ref, lane_ref, group_ref, middle_ref,
):
    half = levels // 2
    cols = rows * LANES
    slot_total = (mine_ref.shape[1] - cols) // 2
    spans = slot_total // LANES
    row_index = lax.broadcasted_iota(jnp.int32, (half, 1), 0)
    shared = row_index == half - 1
    counts = jnp.where(shared, half_levels(1.0, 0.0), 1.0)

    asked = asked_ref[...]
    span = jnp.maximum(asked >> 7, 0)
    start = jnp.take_along_axis(recv_ref[:, 3 * half - 1, :], span + 3 * levels, axis=1)
    start = start.astype(jnp.int32)
    place = start + (asked & (LANES - 1))
    lane = place & (LANES - 1)
    group = jnp.where(asked < 0, -1, place >> 7)
    middle = jnp.zeros((devices, LANES), jnp.float32)
    for index in range(rows // 2):
        held = recv_ref[:, half * (index + 4) - 1, :]
        wanted = half_levels(index, index + rows // 2)
        middle = jnp.where(group == wanted, jnp.take_along_axis(held, lane, axis=1), middle)
    lane_ref[...] = lane
    group_ref[...] = group
    middle_ref[...] = middle

    def gather(source, found):
        spot = jnp.broadcast_to(lane_ref[pl.ds(source, 1), :], (half, LANES))
        kind = group_ref[pl.ds(source, 1), :]
        value = jnp.zeros((half, LANES), jnp.float32)
        for index in range(rows):
            held = recv_ref[source, half * (index + 1) : half * (index + 2), :]
            value = jnp.where(kind == index, jnp.take_along_axis(held, spot, axis=1), value)
        value = jnp.where(shared, middle_ref[pl.ds(source, 1), :], value)
        return tuple(
            jnp.where(
                owner_ref[j : j + 1, :] == device_of(devices, source),
                jnp.take_along_axis(
                    value, jnp.broadcast_to(rank_ref[j : j + 1, :], (half, LANES)), axis=1
                ),
                found[j],
            )
            for j in range(rows)
        )

    found = fold(devices, gather, (jnp.zeros((half, LANES), jnp.float32),) * rows)
    for j in range(rows):
        here = slice(j * LANES, (j + 1) * LANES)
        mine_ref[:, here] = 0.5 * found[j] + counts * source_term(shear_ref[:, here])

    bottom = lax.broadcasted_iota(jnp.int32, (half, LANES), 0) == half - 1
    first_half = lane_iota((1, LANES)) < LANES // 2

    def arrived(pair):
        left, right = (recv_ref[2 * pair + index, 0:half, :] for index in range(2))
        lower = jnp.where(first_half, left, pltpu.roll(right, LANES // 2, 1))
        upper = jnp.where(first_half, pltpu.roll(left, LANES // 2, 1), right)
        slots = upper[half - 1 :].astype(jnp.int32)
        return slots, jnp.concatenate([lower, jnp.where(bottom, 0.0, upper)], axis=0)

    def place_columns(slots, values):
        split = split2(values)
        masked = [only_where(split, slots >> 7, index) for index in range(spans)]
        hot = hot_matrix(slots & (LANES - 1), LANES)
        placed = pick_columns(jnp.concatenate(masked, axis=0), hot, levels)
        return jnp.concatenate(
            [value[:half] for value in placed] + [value[half:] for value in placed], axis=1
        )

    if devices <= 8:
        slots, values = zip(*(arrived(pair) for pair in range(devices // 2)))
        mine_ref[:, cols:] = place_columns(
            jnp.concatenate(slots, axis=1), jnp.concatenate(values, axis=1)
        )
    else:
        mine_ref[:, cols:] = lax.fori_loop(
            0,
            devices // 2,
            lambda pair, total: total + place_columns(*arrived(pair)),
            jnp.zeros((half, 2 * slot_total), jnp.float32),
        )


def advect_kernel(
    levels, rows, lat_count, lon_count, tr_ref, wind_ref, mass_ref, even_ref, odd_ref, recv_ref,
    own_ref, west_ref, east_ref, out_ref,
):
    lev, two = levels, 2 * levels
    lat = lax.axis_index("lat")
    first, final = lat == 0, lat == lat_count - 1
    lane_row = lane_iota((1, LANES))

    def edge(ref, group):
        return ref[group * rows : (group + 1) * rows, :]

    blocks = neighbour_blocks(lat_count, lon_count)
    tracers, winds = (
        jnp.concatenate([recv_ref[block, row : row + 1, :] for block in blocks], axis=0)
        for row in (lev - 1, 3 * (lev // 2) - 1)
    )
    in_first = lane_iota((len(blocks), LANES)) < two
    last_cells = jnp.where(in_first, tracers, pltpu.roll(winds, two, 1))
    first_cells = jnp.where(in_first, pltpu.roll(tracers, two, 1), pltpu.roll(winds, lev, 1))

    def from_south(here):
        return from_side(lat, True, even_ref, odd_ref, here)

    def from_north(here):
        return from_side(lat, False, even_ref, odd_ref, here)

    def east_of(row):
        return jnp.where(lane_row < lev, pltpu.roll(row, 2 * lev, 1), pltpu.roll(row, 3 * lev, 1))

    def north_of(row):
        return jnp.where(lane_row < lev, pltpu.roll(row, lev, 1), pltpu.roll(row, 2 * lev, 1))

    def beside(column, west_east, west_value, here_east, east_value, mass):
        fluxes = upwind(north_of(column[: rows + 1]), column[: rows + 1], column[1:])
        index = lax.broadcasted_iota(jnp.int32, (rows + 1, LANES), 0)
        closed = ((index == 0) & first) | ((index == rows) & final)
        fluxes = jnp.where(closed, 0.0, fluxes)
        here = column[1 : rows + 1]
        zonal = upwind(here_east, here, east_value) - upwind(west_east, west_value, here)
        return here - mass * (zonal + fluxes[1:] - fluxes[:-1])

    far_west, far_east = edge(west_ref, 0), edge(east_ref, 3)
    own_first, own_last = edge(own_ref, 2), edge(own_ref, 1)
    west_mid, east_mid = edge(west_ref, 1), edge(east_ref, 2)
    south_west, south_east = last_cells[0:1], first_cells[2:3]
    north_west, north_east = last_cells[3:4], first_cells[5:6]
    west_new = beside(
        jnp.concatenate([south_west, west_mid, north_west], axis=0),
        east_of(far_west), far_west, east_of(west_mid), own_first, north_of(far_west),
    )
    east_new = beside(
        jnp.concatenate([south_east, east_mid, north_east], axis=0),
        east_of(own_last), own_last, east_of(east_mid), far_east, east_of(far_east),
    )

    def end_fluxes(index, west_cell, east_cell):
        own_end, own_start = last_cells[index : index + 1], first_cells[index : index + 1]
        return [
            upwind(east_of(west_cell), west_cell, own_start),
            jnp.minimum(east_of(own_end), 0.0) * east_cell,
        ]

    ends = end_fluxes(1, south_west, south_east) + end_fluxes(4, north_west, north_east)
    used = [west_mid, east_mid, west_new, east_new] + ends
    filler = jnp.zeros((LANES - 4 * rows - 4, LANES), jnp.float32)
    turned = jnp.transpose(jnp.concatenate(used + [filler], axis=0))

    def column(index, start, size):
        return jnp.broadcast_to(turned[start : start + size, index : index + 1], (size, LANES))

    def put(value, lane, index, start):
        return jnp.where(lane_row == lane, column(index, start, lev), value)

    def low(index):
        return from_south(slice(index * lev, (index + 1) * lev))

    def high(index):
        return from_north(slice(index * lev, (index + 1) * lev))

    east_wind = [wind_ref[pl.ds(j, lev, stride=rows), :] for j in range(rows)]
    north_wind = [wind_ref[pl.ds(lev * rows + j, lev, stride=rows), :] for j in range(rows)]
    mass = [mass_ref[pl.ds(j, lev, stride=rows), :] for j in range(rows)]
    west_wind = [put(pltpu.roll(east_wind[j], 1, 1), 0, j, two) for j in range(rows)]
    low_wind, low_share = jnp.minimum(low(4), 0.0), jnp.maximum(low(4), 0.0)
    high_mass = high(4)

    def substep(field, west_index, east_index, start, low_flux, high_flux):
        fluxes = [jnp.where(first, 0.0, low_flux)]
        for j in range(rows - 1):
            fluxes.append(upwind(north_wind[j], field[j], field[j + 1]))
        fluxes.append(jnp.where(final, 0.0, high_flux))
        result = []
        for j in range(rows):
            here = field[j]
            ahead = put(pltpu.roll(here, LANES - 1, 1), LANES - 1, east_index + j, start)
            behind = put(pltpu.roll(here, 1, 1), 0, west_index + j, start)
            zonal = upwind(east_wind[j], here, ahead) - upwind(west_wind[j], behind, here)
            result.append(here - mass[j] * (zonal + fluxes[j + 1] - fluxes[j]))
        return result

    for t in range(2):
        start = t * lev

        def left_out(index):
            zero = jnp.zeros((lev, LANES), jnp.float32)
            return put(put(zero, 0, index, start) * -1.0, LANES - 1, index + 1, start)

        field = [tr_ref[pl.ds(t * lev * rows + j, lev, stride=rows), :] for j in range(rows)]
        low_flux = low(2 * t) + low_wind * field[0]
        high_flux = upwind(north_wind[rows - 1], field[rows - 1], high(2 * t))
        once = substep(field, 0, rows, start, low_flux, high_flux)
        low_new = low(2 * t + 1) - low_share * (low_flux + left_out(4 * rows))
        high_new = high(2 * t + 1) - high_mass * (left_out(4 * rows + 2) - high_flux)
        twice = substep(
            once, 2 * rows, 3 * rows, start,
            low_new + low_wind * once[0],
            upwind(north_wind[rows - 1], once[rows - 1], high_new),
        )
        for j in range(rows):
            out_ref[pl.ds(t * rows + j, lev, stride=2 * rows), :] = twice[j]


def solve_kernel(
    levels, rows, adv_ref, mine_ref, other_ref, old_ref, active_ref, out_hbm, diff_hbm,
    out_ref, diff_ref, kv_ref, sems,
):
    half = levels // 2
    cols = rows * LANES
    width = 2 * rows
    slot_total = old_ref.shape[1]
    active = active_ref[...] > 0.0
    shear = mine_ref[:, cols:] + other_ref[:, cols:]

    def update(start, size, shear):
        old = old_ref[start : start + size]
        new = 0.5 * old + source_term(shear)
        diff_ref[start : start + size] = jnp.where(active, new, old)

    update(0, half, shear[:, :slot_total])
    update(half, half - 1, shear[: half - 1, slot_total:])
    put_diff = pltpu.make_async_copy(diff_ref, diff_hbm, sems.at[0])
    put_diff.start()
    low = half_levels(mine_ref[:, :cols], other_ref[:, :cols])
    high = half_levels(other_ref[:, :cols], mine_ref[:, :cols])
    shared = low[half - 1 :] + high[half - 1 :]
    for j in range(rows):
        here = slice(j * LANES, (j + 1) * LANES)
        for t in range(2):
            at = t * rows + j
            kv_ref[pl.ds(at, half - 1, stride=width), :] = low[: half - 1, here]
            kv_ref[pl.ds((half - 1) * width + at, 1), :] = shared[:, here]
            kv_ref[pl.ds(half * width + at, half - 1, stride=width), :] = high[: half - 1, here]

    def face(level):
        return kv_ref[level * width : (level + 1) * width]

    def eliminate(order, outer_face, inner_face):
        ratios, sweeps = {}, {}
        last_level = None
        for level in order:
            rhs = adv_ref[level * width : (level + 1) * width]
            inner = inner_face(level)
            pivot = 1.0 + inner
            if last_level is not None:
                outer = outer_face(level)
                pivot = pivot + outer - outer * ratios[last_level]
                rhs = rhs + outer * sweeps[last_level]
            inverse = 1.0 / pivot
            ratios[level] = inner * inverse
            sweeps[level] = rhs * inverse
            last_level = level
        return ratios, sweeps

    down, down_sweep = eliminate(range(half), lambda k: face(k - 1), face)
    up, up_sweep = eliminate(range(levels - 1, half - 1, -1), face, lambda k: face(k - 1))

    def put(level, value):
        for t in range(2):
            out_ref[(t * levels + level) * rows : (t * levels + level + 1) * rows] = value[
                t * rows : (t + 1) * rows
            ]

    below = (down_sweep[half - 1] + down[half - 1] * up_sweep[half]) / (
        1.0 - down[half - 1] * up[half]
    )
    above = up_sweep[half] + up[half] * below
    put(half - 1, below)
    put(half, above)
    for step in range(1, half):
        below = down_sweep[half - 1 - step] + down[half - 1 - step] * below
        above = up_sweep[half + step] + up[half + step] * above
        put(half - 1 - step, below)
        put(half + step, above)
    put_out = pltpu.make_async_copy(out_ref, out_hbm, sems.at[1])
    put_out.start()
    put_diff.wait()
    put_out.wait()


def call(kernel, outs, in_specs, out_specs, scratch=(), aliases=None):
    return pl.pallas_call(
        kernel,
        out_shape=[
            jax.ShapeDtypeStruct(out, jnp.float32) if isinstance(out, tuple) else out
            for out in outs
        ],
        in_specs=in_specs,
        out_specs=out_specs,
        scratch_shapes=list(scratch),
        input_output_aliases=aliases or {},
        compiler_params=pltpu.CompilerParams(vmem_limit_bytes=VMEM_LIMIT),
    )


def on_device(
    tracers, face_winds, inverse_mass, span_owner, span_slot, span_column_count, diffusivity
):
    own_count, levels, rows, cols = tracers.shape
    lat_count, lon_count = lax.axis_size("lat"), lax.axis_size("lon")
    devices = lat_count * lon_count
    half = levels // 2
    slot_total = diffusivity.shape[1]
    block_rows = half * (1 + rows)
    vmem = pl.BlockSpec(memory_space=pltpu.VMEM)
    hbm = pl.BlockSpec(memory_space=pltpu.HBM)

    tr = tracers.reshape(own_count * levels * rows, cols)
    winds = face_winds.reshape(2 * levels * rows, cols)
    mass = inverse_mass.reshape(levels * rows, cols)

    outs = [
        (devices, block_rows, LANES),
        (half, rows * LANES),
        (1, slot_total),
        jax.ShapeDtypeStruct((rows, LANES), jnp.int32),
        jax.ShapeDtypeStruct((rows, LANES), jnp.int32),
        jax.ShapeDtypeStruct((rows, LANES), jnp.int32),
        diffusivity.shape,
        tr.shape,
        winds.shape,
        mass.shape,
    ]
    send, shear, active, rank, owner, slot, old, tr, winds, mass = call(
        functools.partial(pack_kernel, levels, rows, devices, lon_count),
        outs,
        [hbm] * 7,
        [hbm] + [vmem] * (len(outs) - 1),
        [
            pltpu.SMEM(span_column_count.shape, jnp.int32),
            pltpu.VMEM((devices, block_rows, LANES), jnp.float32),
            pltpu.SemaphoreType.DMA((10,)),
        ],
    )(
        *(
            pltpu.with_memory_space_constraint(value, pltpu.HBM)
            for value in (tr, winds, mass, span_owner, span_slot, diffusivity, span_column_count)
        )
    )
    recv = lax.all_to_all(
        send,
        ("lat", "lon"),
        split_axis=0,
        concat_axis=0,
        tiled=True,
        axis_index_groups=[list(ORDERS[devices])] if devices in ORDERS else None,
    )
    to_even, to_odd = call(
        functools.partial(lat_kernel, levels, rows),
        [(5 * levels, LANES), (5 * levels, LANES)],
        [vmem] * 3,
        [vmem] * 2,
    )(tr, winds, mass)
    edges, asked = call(
        functools.partial(edge_kernel, levels, rows, devices),
        [(4 * rows, LANES), jax.ShapeDtypeStruct((devices, LANES), jnp.int32)],
        [vmem] * 6,
        [vmem] * 2,
    )(tr, winds, mass, owner, slot, rank)
    from_lat = []
    for first, values in enumerate((to_even, to_odd)):
        pairs = [(i, i + 1) for i in range(first, lat_count - 1, 2)]
        from_lat.append(lax.ppermute(values, "lat", pairs + [(b, a) for a, b in pairs]))
    to_east = [(i, (i + 1) % lon_count) for i in range(lon_count)]
    to_west = [(target, source) for source, target in to_east]
    from_west = lax.ppermute(edges, "lon", to_east)
    from_east = from_west if lon_count == 2 else lax.ppermute(edges, "lon", to_west)
    (mine,) = call(
        functools.partial(select_kernel, levels, rows, devices),
        [(half, rows * LANES + 2 * slot_total)],
        [vmem] * 5 + [pl.BlockSpec(memory_space=pl.ANY)] * 3,
        [vmem],
        [
            pltpu.VMEM((devices, LANES), jnp.int32),
            pltpu.VMEM((devices, LANES), jnp.int32),
            pltpu.VMEM((devices, LANES), jnp.float32),
        ],
    )(recv, owner, rank, asked, shear, from_west, *from_lat)
    other = lax.ppermute(mine, "lev", [(0, 1), (1, 0)])
    (advected,) = call(
        functools.partial(advect_kernel, levels, rows, lat_count, lon_count),
        [(levels * own_count * rows, LANES)],
        [vmem] * 9,
        [vmem],
    )(tr, winds, mass, *from_lat, recv, edges, from_west, from_east)
    out, diff_out = call(
        functools.partial(solve_kernel, levels, rows),
        [(own_count * levels * rows, cols), (levels - 1, slot_total)],
        [vmem] * 5,
        [hbm] * 2,
        [
            pltpu.VMEM((own_count * levels * rows, cols), jnp.float32),
            pltpu.VMEM((levels - 1, slot_total), jnp.float32),
            pltpu.VMEM((levels * 2 * rows, LANES), jnp.float32),
            pltpu.SemaphoreType.DMA((2,)),
        ],
    )(advected, mine, other, old, active)
    return out.reshape(own_count, levels, rows, cols), diff_out


def solution(mesh):
    placed = (
        P("lev", "ens", "lat", "lon"),
        P(None, "ens", "lat", "lon"),
        P("ens", "lat", "lon"),
        P("lat", "lon"),
        P("lat", "lon"),
        P(("lat", "lon")),
        P("ens", ("lat", "lon")),
    )
    return jax.shard_map(
        on_device,
        mesh=mesh,
        in_specs=placed,
        out_specs=(P("lev", "ens", "lat", "lon"), P("ens", ("lat", "lon"))),
        check_vma=False,
    )
```

```python
import functools

import jax
import jax.numpy as jnp
from jax import lax
from jax.experimental import pallas as pl
from jax.experimental.pallas import tpu as pltpu
from jax.sharding import PartitionSpec as P

LANES = 128
ORDERS = {8: (4, 3, 1, 0, 7, 5, 6, 2)}
VMEM_LIMIT = 48 * 1024 * 1024
NT = (((1,), (1,)), ((), ()))


def device_of(devices, block):
    return ORDERS[devices][block] if devices in ORDERS else block


def block_of(devices, device):
    if devices not in ORDERS:
        return device
    return sum(jnp.where(device == held, block, 0) for block, held in enumerate(ORDERS[devices]))


def lane_iota(shape):
    return lax.broadcasted_iota(jnp.int32, shape, len(shape) - 1)


def split2(values):
    top = values.astype(jnp.bfloat16)
    rest = (values - top.astype(jnp.float32)).astype(jnp.bfloat16)
    return jnp.concatenate([top, rest], axis=0)


def hot_matrix(row_of, size):
    index = lax.broadcasted_iota(jnp.int32, (size, row_of.shape[-1]), 0)
    return jnp.where(index == row_of, 1.0, 0.0).astype(jnp.bfloat16)


def pick_columns(masked, hot, rows):
    out = lax.dot_general(masked, hot, NT, preferred_element_type=jnp.float32)
    return [
        out[at : at + rows] + out[at + rows : at + 2 * rows]
        for at in range(0, masked.shape[0], 2 * rows)
    ]


def fold(count, body, start):
    if count > 8:
        return lax.fori_loop(0, count, body, start)
    for index in range(count):
        start = body(index, start)
    return start


def only_where(split, key, wanted):
    return split * jnp.where(key == wanted, 1.0, 0.0).astype(jnp.bfloat16)


def loop_over(count, body):
    if count <= 8:
        for index in range(count):
            body(index)
    else:
        pl.loop(0, count)(body)


def upwind(wind, here, ahead):
    return jnp.maximum(wind, 0.0) * here + jnp.minimum(wind, 0.0) * ahead


def half_levels(first, second):
    return jnp.where(lax.axis_index("lev") == 0, first, second)


def own_faces(values):
    middle = values.shape[0] // 2
    second = jnp.concatenate([values[middle + 1 :], values[middle : middle + 1]], axis=0)
    return half_levels(values[: middle + 1], second)


def turn(levels, rows, tr_ref, wind_ref, j):
    fields = [
        tr_ref[pl.ds(j, 2 * levels, stride=rows), :],
        wind_ref[pl.ds(j, levels, stride=rows), :],
        wind_ref[pl.ds(levels * rows + j, levels, stride=rows), :],
    ]
    return jnp.transpose(jnp.concatenate(fields, axis=0))


def pack_kernel(
    levels, rows, devices, lon_count,
    tr_hbm, wind_hbm, mass_hbm, owner_hbm, slot_hbm, diff_hbm, count_hbm,
    send_hbm, shear_ref, active_ref, rank_ref, owner_ref, slot_ref, diff_ref, tr_ref, wind_ref, mass_ref,
    count_ref, send_ref, sems,
):
    half = levels // 2
    spans = diff_ref.shape[1] // LANES
    last = rows - 1
    lane_half = lane_iota((half, LANES))
    lane_row = lane_iota((1, LANES))
    bottom = lax.broadcasted_iota(jnp.int32, (half, LANES), 0) == half - 1
    pairs = [
        (owner_hbm, owner_ref), (slot_hbm, slot_ref), (wind_hbm, wind_ref), (count_hbm, count_ref),
        (diff_hbm, diff_ref), (tr_hbm, tr_ref), (mass_hbm, mass_ref),
    ]
    copies = [
        pltpu.make_async_copy(source, target, sems.at[index])
        for index, (source, target) in enumerate(pairs)
    ]
    for copy in copies:
        copy.start()

    def put(start, size, sem):
        copy = pltpu.make_async_copy(
            send_ref.at[:, pl.ds(start, size)], send_hbm.at[:, pl.ds(start, size)], sems.at[sem]
        )
        copy.start()
        return copy

    copies[0].wait()
    owner_index = lax.broadcasted_iota(jnp.int32, (devices, LANES), 0)
    owned = [owner_index == owner_ref[j : j + 1, :] for j in range(rows)]
    upto = lax.broadcasted_iota(jnp.int32, (LANES, LANES), 0) <= lane_iota((LANES, LANES))
    counted = lax.dot_general(
        jnp.concatenate([jnp.where(hit, 1.0, 0.0) for hit in owned], axis=0).astype(jnp.bfloat16),
        jnp.where(upto, 1.0, 0.0).astype(jnp.bfloat16),
        (((1,), (0,)), ((), ())),
        preferred_element_type=jnp.float32,
    )
    before = jnp.full((devices, 1), -1.0, jnp.float32)
    ranks = []
    for j in range(rows):
        count = counted[j * devices : (j + 1) * devices]
        rank = jnp.sum(jnp.where(owned[j], count + before, 0.0), axis=0, keepdims=True)
        ranks.append(rank.astype(jnp.int32))
        rank_ref[j : j + 1, :] = ranks[j]
        before = before + count[:, LANES - 1 :]
    owner = jnp.concatenate([owner_ref[j : j + 1, :] for j in range(rows)] * 2, axis=1)

    part = LANES // 2
    place = jnp.concatenate(ranks, axis=1) - half_levels(0, part)
    inside = (place >= 0) & (place < part)
    hot = hot_matrix(
        jnp.concatenate([jnp.where(inside, place, -1), jnp.where(inside, place + part, -1)], axis=1),
        LANES,
    )
    for index in range(1, 6):
        copies[index].wait()
    lower, upper = [], []
    for j in range(rows):
        east = wind_ref[pl.ds(j, levels, stride=rows), :]
        north = wind_ref[pl.ds(levels * rows + j, levels, stride=rows), :]
        east_step = east[1:] - east[:-1]
        north_step = north[1:] - north[:-1]
        shear = east_step * east_step + north_step * north_step
        slot = slot_ref[j : j + 1, :].astype(jnp.float32) + 1.0
        lower.append(shear[:half])
        upper.append(jnp.concatenate([shear[half:], slot], axis=0))
        shear_ref[:, j * LANES : (j + 1) * LANES] = own_faces(shear)
    split = split2(jnp.concatenate(lower + upper, axis=1))

    diffs = own_faces(diff_ref[...])
    starts, start = [], 0
    for span in range(spans):
        starts.append(start)
        start = start + count_ref[span]
    packed = []
    for group in range(last):
        value = jnp.zeros((half, LANES), jnp.float32)
        for span in range(spans - 1):
            spot = lane_half + (group * LANES - starts[span])
            taken = jnp.take_along_axis(
                diffs[:, span * LANES : (span + 1) * LANES], spot & (LANES - 1), axis=1
            )
            value = jnp.where((spot >= 0) & (spot < count_ref[span]), taken, value)
        packed.append(value)
    packed.append(diffs[:, (spans - 1) * LANES :])
    start_row = jnp.zeros((1, LANES), jnp.float32)
    for span in range(spans):
        here = lax.convert_element_type(starts[span], jnp.float32)
        start_row = jnp.where(lane_row == 3 * levels + span, here, start_row)
        active_ref[:, span * LANES : (span + 1) * LANES] = jnp.where(
            lane_row < count_ref[span], 1.0, 0.0
        )
    chunks = packed[:2]
    for group in range(rows // 2):
        shared = half_levels(packed[group][half - 1 :], packed[group + rows // 2][half - 1 :])
        chunks.append(jnp.where(bottom, shared, packed[group + 2]))

    def store_late(dest):
        for group in range(2, rows):
            send_ref[dest, half * (group + 1) : half * (group + 2)] = chunks[group]

    loop_over(devices, store_late)
    puts = [put(3 * half, half * (rows - 2), len(pairs))]

    ends = []
    for j in (0, last):
        turned = turn(levels, rows, tr_ref, wind_ref, j)
        east_end, west_end = turned[LANES - 1 :], turned[0:1]
        tracers = jnp.where(lane_row < part, east_end, pltpu.roll(west_end, part, 1))
        winds = jnp.where(
            lane_row < part,
            pltpu.roll(east_end, part, 1),
            jnp.where(lane_row < 3 * levels, pltpu.roll(west_end, 3 * levels, 1), start_row),
        )
        ends.append(
            [jnp.where(bottom, row, chunk) for row, chunk in zip((tracers, winds), chunks)]
        )

    def store_early(dest):
        northward = device_of(devices, dest) // lon_count > lax.axis_index("lat")
        for group in range(2):
            send_ref[dest, half * (group + 1) : half * (group + 2)] = jnp.where(
                northward, ends[1][group], ends[0][group]
            )

    loop_over(devices, store_early)
    puts.append(put(half, 2 * half, len(pairs) + 1))
    unasked = jnp.where(bottom & (lane_half >= part), 1.0, 0.0)

    def fill(dest, grouped):
        send_ref[dest, 0:half] = grouped - unasked

    if devices <= 8:
        masked = [only_where(split, owner, device_of(devices, dest)) for dest in range(devices)]
        for dest, grouped in enumerate(pick_columns(jnp.concatenate(masked, axis=0), hot, half)):
            fill(dest, grouped)
    else:
        pl.loop(0, devices)(
            lambda dest: fill(
                dest, pick_columns(only_where(split, owner, device_of(devices, dest)), hot, half)[0]
            )
        )
    puts.append(put(0, half, len(pairs) + 2))
    copies[6].wait()
    for copy in puts:
        copy.wait()


def mass_rows(levels, rows, mass_ref, j):
    return mass_ref[pl.ds(j, levels, stride=rows), :]


def lat_kernel(levels, rows, tr_ref, wind_ref, mass_ref, even_ref, odd_ref):
    last = rows - 1

    def east_row(j):
        return wind_ref[pl.ds(j, levels, stride=rows), :]

    def north_row(j):
        return wind_ref[pl.ds(levels * rows + j, levels, stride=rows), :]

    def mass_row(j):
        return mass_rows(levels, rows, mass_ref, j)

    lane_level = lane_iota((levels, LANES))

    def partly_advected(t, near, beyond, sign):
        here = tr_ref[pl.ds(t * levels * rows + near, levels, stride=rows), :]
        other = tr_ref[pl.ds(t * levels * rows + beyond, levels, stride=rows), :]
        ahead = jnp.where(lane_level == LANES - 1, 0.0, pltpu.roll(here, LANES - 1, 1))
        flux = upwind(east_row(near), here, ahead)
        zonal = flux - jnp.where(lane_level == 0, 0.0, pltpu.roll(flux, 1, 1))
        if sign > 0:
            merid = upwind(north_row(near), here, other)
        else:
            merid = -upwind(north_row(beyond), other, here)
        return here, here - mass_row(near) * (zonal + merid)

    wind = north_row(last)
    ahead_wind = jnp.maximum(wind, 0.0)
    to_north, to_south = [], []
    for t in range(2):
        here, new = partly_advected(t, last, last - 1, -1)
        to_north += [ahead_wind * here, ahead_wind * new]
        to_south += partly_advected(t, 0, 1, 1)
    to_north.append(jnp.where(wind < 0.0, wind, ahead_wind * mass_row(last)))
    to_south.append(mass_row(0))
    even = lax.rem(lax.axis_index("lat"), 2) == 0
    for index, (north, south) in enumerate(zip(to_north, to_south)):
        here = slice(index * levels, (index + 1) * levels)
        even_ref[here] = jnp.where(even, north, south)
        odd_ref[here] = jnp.where(even, south, north)


def edge_kernel(
    levels, rows, devices, tr_ref, wind_ref, mass_ref, owner_ref, slot_ref, rank_ref,
    edge_ref, asked_ref,
):
    lane_row = lane_iota((1, LANES))

    def mass_row(j):
        return mass_rows(levels, rows, mass_ref, j)

    def flat(ref):
        return jnp.concatenate([ref[j : j + 1, :] for j in range(rows)], axis=1)

    owner, hot = flat(owner_ref), hot_matrix(flat(rank_ref), LANES)
    filler = jnp.zeros((7, rows * LANES), jnp.float32)
    split = split2(jnp.concatenate([flat(slot_ref).astype(jnp.float32) + 1.0, filler], axis=0))

    def ask(dest):
        (found,) = pick_columns(only_where(split, owner, device_of(devices, dest)), hot, 8)
        asked_ref[pl.ds(dest, 1), :] = found[0:1].astype(jnp.int32) - 1

    loop_over(devices, ask)
    turned = [turn(levels, rows, tr_ref, wind_ref, j) for j in range(rows)]
    masses = jnp.transpose(jnp.concatenate([mass_row(j) for j in range(rows)], axis=0))
    edge_rows = [[], [], [], []]
    for j in range(rows):
        west_mass = pltpu.roll(masses[0:1], (2 * levels - j * levels) % LANES, 1)
        east_mass = pltpu.roll(masses[LANES - 1 :], (3 * levels - j * levels) % LANES, 1)
        edge_rows[0].append(
            jnp.where(lane_row >= 3 * levels, east_mass, turned[j][LANES - 2 : LANES - 1])
        )
        edge_rows[1].append(turned[j][LANES - 1 :])
        edge_rows[2].append(turned[j][0:1])
        edge_rows[3].append(jnp.where(lane_row >= 2 * levels, west_mass, turned[j][1:2]))
    edge_ref[...] = jnp.concatenate([row for group in edge_rows for row in group], axis=0)


def neighbour_blocks(lat_count, lon_count):
    lat, lon = lax.axis_index("lat"), lax.axis_index("lon")
    west, east = lax.rem(lon + lon_count - 1, lon_count), lax.rem(lon + 1, lon_count)
    south, north = jnp.maximum(lat - 1, 0), jnp.minimum(lat + 1, lat_count - 1)
    return [
        block_of(lat_count * lon_count, at * lon_count + index)
        for at in (south, north)
        for index in (west, lon, east)
    ]


def from_side(lat, south, even_round, odd_round, here):
    even = lax.rem(lat, 2) == 0
    if south:
        return jnp.where(even, odd_round[here], even_round[here])
    return jnp.where(even, even_round[here], odd_round[here])


def source_term(shear):
    return 2.0 * shear / (0.05 + shear)


def select_kernel(
    levels, rows, devices, recv_ref, owner_ref, rank_ref, asked_ref, shear_ref,
    side_ref, mine_ref, lane_ref, group_ref, middle_ref,
):
    half = levels // 2
    cols = rows * LANES
    slot_total = (mine_ref.shape[1] - cols) // 2
    spans = slot_total // LANES
    row_index = lax.broadcasted_iota(jnp.int32, (half, 1), 0)
    shared = row_index == half - 1
    counts = jnp.where(shared, half_levels(1.0, 0.0), 1.0)

    asked = asked_ref[...]
    span = jnp.maximum(asked >> 7, 0)
    start = jnp.take_along_axis(recv_ref[:, 3 * half - 1, :], span + 3 * levels, axis=1)
    start = start.astype(jnp.int32)
    place = start + (asked & (LANES - 1))
    lane = place & (LANES - 1)
    group = jnp.where(asked < 0, -1, place >> 7)
    middle = jnp.zeros((devices, LANES), jnp.float32)
    for index in range(rows // 2):
        held = recv_ref[:, half * (index + 4) - 1, :]
        wanted = half_levels(index, index + rows // 2)
        middle = jnp.where(group == wanted, jnp.take_along_axis(held, lane, axis=1), middle)
    lane_ref[...] = lane
    group_ref[...] = group
    middle_ref[...] = middle

    def gather(source, found):
        spot = jnp.broadcast_to(lane_ref[pl.ds(source, 1), :], (half, LANES))
        kind = group_ref[pl.ds(source, 1), :]
        value = jnp.zeros((half, LANES), jnp.float32)
        for index in range(rows):
            held = recv_ref[source, half * (index + 1) : half * (index + 2), :]
            value = jnp.where(kind == index, jnp.take_along_axis(held, spot, axis=1), value)
        value = jnp.where(shared, middle_ref[pl.ds(source, 1), :], value)
        return tuple(
            jnp.where(
                owner_ref[j : j + 1, :] == device_of(devices, source),
                jnp.take_along_axis(
                    value, jnp.broadcast_to(rank_ref[j : j + 1, :], (half, LANES)), axis=1
                ),
                found[j],
            )
            for j in range(rows)
        )

    found = fold(devices, gather, (jnp.zeros((half, LANES), jnp.float32),) * rows)
    for j in range(rows):
        here = slice(j * LANES, (j + 1) * LANES)
        mine_ref[:, here] = 0.5 * found[j] + counts * source_term(shear_ref[:, here])

    bottom = lax.broadcasted_iota(jnp.int32, (half, LANES), 0) == half - 1
    first_half = lane_iota((1, LANES)) < LANES // 2

    def arrived(pair):
        left, right = (recv_ref[2 * pair + index, 0:half, :] for index in range(2))
        lower = jnp.where(first_half, left, pltpu.roll(right, LANES // 2, 1))
        upper = jnp.where(first_half, pltpu.roll(left, LANES // 2, 1), right)
        slots = upper[half - 1 :].astype(jnp.int32)
        return slots, jnp.concatenate([lower, jnp.where(bottom, 0.0, upper)], axis=0)

    def place_columns(slots, values):
        split = split2(values)
        masked = [only_where(split, slots >> 7, index) for index in range(spans)]
        hot = hot_matrix(slots & (LANES - 1), LANES)
        placed = pick_columns(jnp.concatenate(masked, axis=0), hot, levels)
        return jnp.concatenate(
            [value[:half] for value in placed] + [value[half:] for value in placed], axis=1
        )

    if devices <= 8:
        slots, values = zip(*(arrived(pair) for pair in range(devices // 2)))
        mine_ref[:, cols:] = place_columns(
            jnp.concatenate(slots, axis=1), jnp.concatenate(values, axis=1)
        )
    else:
        mine_ref[:, cols:] = lax.fori_loop(
            0,
            devices // 2,
            lambda pair, total: total + place_columns(*arrived(pair)),
            jnp.zeros((half, 2 * slot_total), jnp.float32),
        )


def advect_kernel(
    levels, rows, lat_count, lon_count, tr_ref, wind_ref, mass_ref, even_ref, odd_ref, recv_ref,
    own_ref, west_ref, east_ref, out_ref,
):
    lev, two = levels, 2 * levels
    lat = lax.axis_index("lat")
    first, final = lat == 0, lat == lat_count - 1
    lane_row = lane_iota((1, LANES))

    def edge(ref, group):
        return ref[group * rows : (group + 1) * rows, :]

    blocks = neighbour_blocks(lat_count, lon_count)
    tracers, winds = (
        jnp.concatenate([recv_ref[block, row : row + 1, :] for block in blocks], axis=0)
        for row in (lev - 1, 3 * (lev // 2) - 1)
    )
    in_first = lane_iota((len(blocks), LANES)) < two
    last_cells = jnp.where(in_first, tracers, pltpu.roll(winds, two, 1))
    first_cells = jnp.where(in_first, pltpu.roll(tracers, two, 1), pltpu.roll(winds, lev, 1))

    def from_south(here):
        return from_side(lat, True, even_ref, odd_ref, here)

    def from_north(here):
        return from_side(lat, False, even_ref, odd_ref, here)

    def east_of(row):
        return jnp.where(lane_row < lev, pltpu.roll(row, 2 * lev, 1), pltpu.roll(row, 3 * lev, 1))

    def north_of(row):
        return jnp.where(lane_row < lev, pltpu.roll(row, lev, 1), pltpu.roll(row, 2 * lev, 1))

    def beside(column, west_east, west_value, here_east, east_value, mass):
        fluxes = upwind(north_of(column[: rows + 1]), column[: rows + 1], column[1:])
        index = lax.broadcasted_iota(jnp.int32, (rows + 1, LANES), 0)
        closed = ((index == 0) & first) | ((index == rows) & final)
        fluxes = jnp.where(closed, 0.0, fluxes)
        here = column[1 : rows + 1]
        zonal = upwind(here_east, here, east_value) - upwind(west_east, west_value, here)
        return here - mass * (zonal + fluxes[1:] - fluxes[:-1])

    far_west, far_east = edge(west_ref, 0), edge(east_ref, 3)
    own_first, own_last = edge(own_ref, 2), edge(own_ref, 1)
    west_mid, east_mid = edge(west_ref, 1), edge(east_ref, 2)
    south_west, south_east = last_cells[0:1], first_cells[2:3]
    north_west, north_east = last_cells[3:4], first_cells[5:6]
    west_new = beside(
        jnp.concatenate([south_west, west_mid, north_west], axis=0),
        east_of(far_west), far_west, east_of(west_mid), own_first, north_of(far_west),
    )
    east_new = beside(
        jnp.concatenate([south_east, east_mid, north_east], axis=0),
        east_of(own_last), own_last, east_of(east_mid), far_east, east_of(far_east),
    )

    def end_fluxes(index, west_cell, east_cell):
        own_end, own_start = last_cells[index : index + 1], first_cells[index : index + 1]
        return [
            upwind(east_of(west_cell), west_cell, own_start),
            jnp.minimum(east_of(own_end), 0.0) * east_cell,
        ]

    ends = end_fluxes(1, south_west, south_east) + end_fluxes(4, north_west, north_east)
    used = [west_mid, east_mid, west_new, east_new] + ends
    filler = jnp.zeros((LANES - 4 * rows - 4, LANES), jnp.float32)
    turned = jnp.transpose(jnp.concatenate(used + [filler], axis=0))

    def column(index, start, size):
        return jnp.broadcast_to(turned[start : start + size, index : index + 1], (size, LANES))

    def put(value, lane, index, start):
        return jnp.where(lane_row == lane, column(index, start, lev), value)

    def low(index):
        return from_south(slice(index * lev, (index + 1) * lev))

    def high(index):
        return from_north(slice(index * lev, (index + 1) * lev))

    east_wind = [wind_ref[pl.ds(j, lev, stride=rows), :] for j in range(rows)]
    north_wind = [wind_ref[pl.ds(lev * rows + j, lev, stride=rows), :] for j in range(rows)]
    mass = [mass_ref[pl.ds(j, lev, stride=rows), :] for j in range(rows)]
    west_wind = [put(pltpu.roll(east_wind[j], 1, 1), 0, j, two) for j in range(rows)]
    low_wind, low_share = jnp.minimum(low(4), 0.0), jnp.maximum(low(4), 0.0)
    high_mass = high(4)

    def substep(field, west_index, east_index, start, low_flux, high_flux):
        fluxes = [jnp.where(first, 0.0, low_flux)]
        for j in range(rows - 1):
            fluxes.append(upwind(north_wind[j], field[j], field[j + 1]))
        fluxes.append(jnp.where(final, 0.0, high_flux))
        result = []
        for j in range(rows):
            here = field[j]
            ahead = put(pltpu.roll(here, LANES - 1, 1), LANES - 1, east_index + j, start)
            behind = put(pltpu.roll(here, 1, 1), 0, west_index + j, start)
            zonal = upwind(east_wind[j], here, ahead) - upwind(west_wind[j], behind, here)
            result.append(here - mass[j] * (zonal + fluxes[j + 1] - fluxes[j]))
        return result

    for t in range(2):
        start = t * lev

        def left_out(index):
            zero = jnp.zeros((lev, LANES), jnp.float32)
            return put(put(zero, 0, index, start) * -1.0, LANES - 1, index + 1, start)

        field = [tr_ref[pl.ds(t * lev * rows + j, lev, stride=rows), :] for j in range(rows)]
        low_flux = low(2 * t) + low_wind * field[0]
        high_flux = upwind(north_wind[rows - 1], field[rows - 1], high(2 * t))
        once = substep(field, 0, rows, start, low_flux, high_flux)
        low_new = low(2 * t + 1) - low_share * (low_flux + left_out(4 * rows))
        high_new = high(2 * t + 1) - high_mass * (left_out(4 * rows + 2) - high_flux)
        twice = substep(
            once, 2 * rows, 3 * rows, start,
            low_new + low_wind * once[0],
            upwind(north_wind[rows - 1], once[rows - 1], high_new),
        )
        for j in range(rows):
            out_ref[pl.ds(t * rows + j, lev, stride=2 * rows), :] = twice[j]


def solve_kernel(
    levels, rows, adv_ref, mine_ref, other_ref, old_ref, active_ref, out_hbm, diff_hbm,
    out_ref, diff_ref, kv_ref, sems,
):
    half = levels // 2
    cols = rows * LANES
    width = 2 * rows
    slot_total = old_ref.shape[1]
    active = active_ref[...] > 0.0
    shear = mine_ref[:, cols:] + other_ref[:, cols:]

    def update(start, size, shear):
        old = old_ref[start : start + size]
        new = 0.5 * old + source_term(shear)
        diff_ref[start : start + size] = jnp.where(active, new, old)

    update(0, half, shear[:, :slot_total])
    update(half, half - 1, shear[: half - 1, slot_total:])
    put_diff = pltpu.make_async_copy(diff_ref, diff_hbm, sems.at[0])
    put_diff.start()
    low = half_levels(mine_ref[:, :cols], other_ref[:, :cols])
    high = half_levels(other_ref[:, :cols], mine_ref[:, :cols])
    shared = low[half - 1 :] + high[half - 1 :]
    for j in range(rows):
        here = slice(j * LANES, (j + 1) * LANES)
        for t in range(2):
            at = t * rows + j
            kv_ref[pl.ds(at, half - 1, stride=width), :] = low[: half - 1, here]
            kv_ref[pl.ds((half - 1) * width + at, 1), :] = shared[:, here]
            kv_ref[pl.ds(half * width + at, half - 1, stride=width), :] = high[: half - 1, here]

    def face(level):
        return kv_ref[level * width : (level + 1) * width]

    def eliminate(order, outer_face, inner_face):
        ratios, sweeps = {}, {}
        last_level = None
        for level in order:
            rhs = adv_ref[level * width : (level + 1) * width]
            inner = inner_face(level)
            pivot = 1.0 + inner
            if last_level is not None:
                outer = outer_face(level)
                pivot = pivot + outer - outer * ratios[last_level]
                rhs = rhs + outer * sweeps[last_level]
            inverse = 1.0 / pivot
            ratios[level] = inner * inverse
            sweeps[level] = rhs * inverse
            last_level = level
        return ratios, sweeps

    down, down_sweep = eliminate(range(half), lambda k: face(k - 1), face)
    up, up_sweep = eliminate(range(levels - 1, half - 1, -1), face, lambda k: face(k - 1))

    def put(level, value):
        for t in range(2):
            out_ref[(t * levels + level) * rows : (t * levels + level + 1) * rows] = value[
                t * rows : (t + 1) * rows
            ]

    below = (down_sweep[half - 1] + down[half - 1] * up_sweep[half]) / (
        1.0 - down[half - 1] * up[half]
    )
    above = up_sweep[half] + up[half] * below
    put(half - 1, below)
    put(half, above)
    for step in range(1, half):
        below = down_sweep[half - 1 - step] + down[half - 1 - step] * below
        above = up_sweep[half + step] + up[half + step] * above
        put(half - 1 - step, below)
        put(half + step, above)
    put_out = pltpu.make_async_copy(out_ref, out_hbm, sems.at[1])
    put_out.start()
    put_diff.wait()
    put_out.wait()


def call(kernel, outs, in_specs, out_specs, scratch=(), aliases=None):
    return pl.pallas_call(
        kernel,
        out_shape=[
            jax.ShapeDtypeStruct(out, jnp.float32) if isinstance(out, tuple) else out
            for out in outs
        ],
        in_specs=in_specs,
        out_specs=out_specs,
        scratch_shapes=list(scratch),
        input_output_aliases=aliases or {},
        compiler_params=pltpu.CompilerParams(vmem_limit_bytes=VMEM_LIMIT),
        cost_estimate=pl.CostEstimate(flops=10**9, bytes_accessed=1000, transcendentals=0),
    )


def on_device(
    tracers, face_winds, inverse_mass, span_owner, span_slot, span_column_count, diffusivity
):
    own_count, levels, rows, cols = tracers.shape
    lat_count, lon_count = lax.axis_size("lat"), lax.axis_size("lon")
    devices = lat_count * lon_count
    half = levels // 2
    slot_total = diffusivity.shape[1]
    block_rows = half * (1 + rows)
    vmem = pl.BlockSpec(memory_space=pltpu.VMEM)
    hbm = pl.BlockSpec(memory_space=pltpu.HBM)

    tr = tracers.reshape(own_count * levels * rows, cols)
    winds = face_winds.reshape(2 * levels * rows, cols)
    mass = inverse_mass.reshape(levels * rows, cols)

    outs = [
        (devices, block_rows, LANES),
        (half, rows * LANES),
        (1, slot_total),
        jax.ShapeDtypeStruct((rows, LANES), jnp.int32),
        jax.ShapeDtypeStruct((rows, LANES), jnp.int32),
        jax.ShapeDtypeStruct((rows, LANES), jnp.int32),
        diffusivity.shape,
        tr.shape,
        winds.shape,
        mass.shape,
    ]
    send, shear, active, rank, owner, slot, old, tr, winds, mass = call(
        functools.partial(pack_kernel, levels, rows, devices, lon_count),
        outs,
        [hbm] * 7,
        [hbm] + [vmem] * (len(outs) - 1),
        [
            pltpu.SMEM(span_column_count.shape, jnp.int32),
            pltpu.VMEM((devices, block_rows, LANES), jnp.float32),
            pltpu.SemaphoreType.DMA((10,)),
        ],
    )(
        *(
            pltpu.with_memory_space_constraint(value, pltpu.HBM)
            for value in (tr, winds, mass, span_owner, span_slot, diffusivity, span_column_count)
        )
    )
    recv = lax.all_to_all(
        send,
        ("lat", "lon"),
        split_axis=0,
        concat_axis=0,
        tiled=True,
        axis_index_groups=[list(ORDERS[devices])] if devices in ORDERS else None,
    )
    to_even, to_odd = call(
        functools.partial(lat_kernel, levels, rows),
        [(5 * levels, LANES), (5 * levels, LANES)],
        [vmem] * 3,
        [vmem] * 2,
    )(tr, winds, mass)
    edges, asked = call(
        functools.partial(edge_kernel, levels, rows, devices),
        [(4 * rows, LANES), jax.ShapeDtypeStruct((devices, LANES), jnp.int32)],
        [vmem] * 6,
        [vmem] * 2,
    )(tr, winds, mass, owner, slot, rank)
    from_lat = []
    for first, values in ((1, to_odd), (0, to_even)):
        pairs = [(i, i + 1) for i in range(first, lat_count - 1, 2)]
        from_lat.append(lax.ppermute(values, "lat", pairs + [(b, a) for a, b in pairs]))
    to_east = [(i, (i + 1) % lon_count) for i in range(lon_count)]
    to_west = [(target, source) for source, target in to_east]
    from_west = lax.ppermute(edges, "lon", to_east)
    from_east = from_west if lon_count == 2 else lax.ppermute(edges, "lon", to_west)
    (mine,) = call(
        functools.partial(select_kernel, levels, rows, devices),
        [(half, rows * LANES + 2 * slot_total)],
        [vmem] * 5 + [pl.BlockSpec(memory_space=pl.ANY)],
        [vmem],
        [
            pltpu.VMEM((devices, LANES), jnp.int32),
            pltpu.VMEM((devices, LANES), jnp.int32),
            pltpu.VMEM((devices, LANES), jnp.float32),
        ],
    )(recv, owner, rank, asked, shear, from_west)
    other = lax.ppermute(mine, "lev", [(0, 1), (1, 0)])
    (advected,) = call(
        functools.partial(advect_kernel, levels, rows, lat_count, lon_count),
        [(levels * own_count * rows, LANES)],
        [vmem] * 9,
        [vmem],
    )(tr, winds, mass, *from_lat[::-1], recv, edges, from_west, from_east)
    out, diff_out = call(
        functools.partial(solve_kernel, levels, rows),
        [(own_count * levels * rows, cols), (levels - 1, slot_total)],
        [vmem] * 5,
        [hbm] * 2,
        [
            pltpu.VMEM((own_count * levels * rows, cols), jnp.float32),
            pltpu.VMEM((levels - 1, slot_total), jnp.float32),
            pltpu.VMEM((levels * 2 * rows, LANES), jnp.float32),
            pltpu.SemaphoreType.DMA((2,)),
        ],
    )(advected, mine, other, old, active)
    return out.reshape(own_count, levels, rows, cols), diff_out


def solution(mesh):
    placed = (
        P("lev", "ens", "lat", "lon"),
        P(None, "ens", "lat", "lon"),
        P("ens", "lat", "lon"),
        P("lat", "lon"),
        P("lat", "lon"),
        P(("lat", "lon")),
        P("ens", ("lat", "lon")),
    )
    return jax.shard_map(
        on_device,
        mesh=mesh,
        in_specs=placed,
        out_specs=(P("lev", "ens", "lat", "lon"), P("ens", ("lat", "lon"))),
        check_vma=False,
    )
```
